256 devices in a mesh: sta: 16 (over z, y_lo), seg: 16 (over y_hi, x, core).
Axes of the slice: x: 4, y: 4 (y_hi: 2, y_lo: 2; y = y_hi * 2 + y_lo), z: 8, core: 2. Of those that a mesh axis runs over, the one named last changes fastest.
Arguments:
- spectra: bfloat16 [2, 32, 512, 4096], P(None, 'seg', None, 'sta'), may hold values from -6 to 6
- bin_index: int32 [512], replicated, may hold values from 0 to 4096
Outputs:
- correlation: float32 [2, 4096, 4096], P(None, ('sta', 'seg'))
The draws below stay inside these ranges and needn't reach their ends.
All inputs are finite; a program needn't handle non-finite values.
Results may differ from the reference program's by a relative error of at most 0.012.
Values may be sent and summed in bfloat16 or wider, within the bound.
No kernel may reach another device: no remote copies, remote signals or barrier semaphores. Data moves between devices by JAX's collectives and lax.ppermute only.
A program may use at most 64 MiB of HBM per device.

```python
import math
import jax
import jax.numpy as jnp
from jax import lax

S = 4096
NFFT = 8192
F = 512
SEG_DEV = 2
LAGS = 2
LAG_STEP = 37
HALF = 64
SEGMENTS = 32
N_SEG = 16


def with_ends(array, own_key, low, top_value):
    shape = array.shape
    index_at = [jax.random.randint(jax.random.fold_in(own_key, axis), (), 0, shape[axis]) for axis in range(len(shape))]
    array = array.at[tuple(index_at)].set(low)
    longest = shape.index(max(shape))
    index_at[longest] = (index_at[longest] + 1) % shape[longest]
    return array.at[tuple(index_at)].set(top_value)


def level_of(key, extent, pieces, least, high):
    def one(position, parts):
        draws = jax.random.uniform(jax.random.fold_in(jax.random.fold_in(key, 6), position), (parts,), jnp.float32, least / len(pieces), high / len(pieces))
        return jnp.repeat(jnp.exp(draws), extent[position] // parts).reshape((-1,) + (1,) * (len(extent) - position - 1))

    loudness = one(*pieces[0])
    for cut in pieces[1:]:
        loudness = loudness * one(*cut)
    return loudness


def gaussian(rng, dims, width, limit, pieces=(), kind=jnp.bfloat16):
    result = jax.random.normal(rng, dims, jnp.float32) * width
    if len(pieces) > 0:
        result = level_of(rng, dims, pieces, -0.22, 0.18) * result
    return jnp.clip(result, min=-limit, max=limit).astype(kind)


def setup_inputs(seed: int = 0) -> dict:
    keys = jax.random.split(jax.random.key(seed), 3)
    spectra = gaussian(keys[0], (2, SEGMENTS, F, S), 1.0, 6.0, ((1, 16), (3, 16)))
    bin_index = with_ends(jax.random.randint(keys[1], (F,), 0, NFFT // 2 + 1), jax.random.fold_in(keys[1], 1), 0, (NFFT // 2 + 1) - 1).astype(jnp.int32)
    return {"spectra": spectra, "bin_index": bin_index}


def whiten(spectra):
    values = spectra.astype(jnp.float32)
    energy = values[0] * values[0] + values[1] * values[1]
    freq_bins = values.shape[2]
    bin_pos = jnp.arange(freq_bins, dtype=jnp.int32)
    window = (jnp.abs(bin_pos[:, None] - bin_pos[None, :]) <= HALF).astype(jnp.float32)
    bin_count = lax.optimization_barrier(jnp.sum(window, axis=1))
    smoothed = jnp.einsum('gf,sfc->sgc', window, energy, precision=lax.Precision.HIGHEST) / bin_count[None, :, None]
    return (values / jnp.sqrt(smoothed + 1e-06)[None]).astype(jnp.bfloat16)

def phases(bin_index):
    lag_samples = (jnp.arange(LAGS, dtype=jnp.int32) + 1) * LAG_STEP
    phase_turn = lag_samples[:, None] * bin_index[None, :].astype(jnp.int32) % NFFT
    phase_angle = 2.0 * math.pi / NFFT * phase_turn.astype(jnp.float32)
    return (jnp.cos(phase_angle), jnp.sin(phase_angle))

def rotate(whitened, cosine, sine_part):
    real_part = whitened[0].astype(jnp.float32)[None]
    imag_part = whitened[1].astype(jnp.float32)[None]
    cos_part = cosine[:, None, :, None]
    sin_part = sine_part[:, None, :, None]
    rot_real = real_part * cos_part - imag_part * sin_part
    rot_imag = real_part * sin_part + imag_part * cos_part
    stacked = jnp.stack([rot_real, rot_imag], axis=1).astype(jnp.bfloat16)
    return stacked.reshape(cosine.shape[0], -1, whitened.shape[3])

def reference(spectra, bin_index):
    whitened = whiten(spectra)
    cosine, sine_part = phases(bin_index)
    norm_scale = 1.0 / math.sqrt(SEGMENTS * F)
    stations = whitened.shape[3]

    def add_group(group_idx, total):
        first_seg = (group_idx * SEG_DEV).astype(jnp.int32)
        group_spec = lax.dynamic_slice_in_dim(whitened, first_seg, SEG_DEV, 1)
        rotated = rotate(group_spec, cosine, sine_part).astype(jnp.float32)
        columns = group_spec.reshape(-1, stations).astype(jnp.float32)
        product = jnp.einsum('mki,kj->mij', rotated, columns, precision=lax.Precision.HIGHEST)
        stacked = lax.optimization_barrier((product * norm_scale).astype(jnp.bfloat16))
        return total + stacked.astype(jnp.float32)
    zero_total = jnp.zeros((LAGS, stations, stations), jnp.float32)
    return lax.fori_loop(0, N_SEG, add_group, zero_total)
```

```python
import math

import jax
import jax.numpy as jnp
import numpy as np
from jax import lax
from jax.experimental import pallas as pl
from jax.experimental.pallas import tpu as pltpu
from jax.sharding import Mesh
from jax.sharding import PartitionSpec as P

NFFT = 8192
LAGS = 2
LAG_STEP = 37
HALF = 64
BINS = 512
BLOCK = 256
DEPTH = 2048
AXES = ("z", "ylo", "yhi", "x", "c")
SIZES = (8, 2, 2, 4, 2)
F32 = jnp.float32
BF16 = jnp.bfloat16
MIB = 1 << 20


def dot_nt(a, b):
    return lax.dot_general(a, b, (((1,), (1,)), ((), ())), preferred_element_type=F32)


def params(mib, **kw):
    return pltpu.CompilerParams(vmem_limit_bytes=mib * MIB, **kw)


def cost(flops, bytes_accessed):
    return pl.CostEstimate(flops=flops, bytes_accessed=bytes_accessed, transcendentals=0)


def move(x, step):
    pairs = []
    for i, at in enumerate(np.ndindex(*SIZES)):
        to = tuple(int(v) % s for v, s in zip(step(*at), SIZES))
        pairs.append((i, int(np.ravel_multi_index(to, SIZES))))
    return lax.ppermute(x, AXES, pairs)


def sign(c):
    return 1 - 2 * c


def whiten_kernel(x_ref, o_ref):
    row = lax.broadcasted_iota(jnp.int32, (BINS, BINS), 0)
    col = lax.broadcasted_iota(jnp.int32, (BINS, BINS), 1)
    window = (jnp.abs(row - col) <= HALF).astype(F32).astype(BF16)
    pos = lax.broadcasted_iota(jnp.int32, (1, BINS), 1)
    count = jnp.minimum(pos + HALF, BINS - 1) - jnp.maximum(pos - HALF, 0) + 1
    inverse = 1.0 / count.astype(F32)
    for s in range(2):
        re = x_ref[0, s].astype(F32).T
        im = x_ref[1, s].astype(F32).T
        energy = re * re + im * im
        high = energy.astype(BF16)
        low = (energy - high.astype(F32)).astype(BF16)
        total = jnp.dot(high, window, preferred_element_type=F32)
        total += jnp.dot(low, window, preferred_element_type=F32)
        scale = lax.rsqrt(total * inverse + 1e-06)
        o_ref[:, s * BINS : (s + 1) * BINS] = (re * scale).astype(BF16)
        o_ref[:, (2 + s) * BINS : (3 + s) * BINS] = (im * scale).astype(BF16)


def whiten(spectra, half):
    return pl.pallas_call(
        whiten_kernel,
        grid=(1,),
        in_specs=[pl.BlockSpec((2, 2, BINS, 128), lambda i: (0, 0, 0, half))],
        out_specs=pl.BlockSpec((128, DEPTH), lambda i: (0, 0)),
        out_shape=jax.ShapeDtypeStruct((128, DEPTH), BF16),
        compiler_params=params(16),
        cost_estimate=cost(2 * 4 * 128 * 512 * 512, MIB),
        name="whiten",
    )(spectra)


def phases(bin_index):
    lag_samples = (jnp.arange(LAGS, dtype=jnp.int32) + 1) * LAG_STEP
    phase_turn = lag_samples[:, None] * bin_index[None, :] % NFFT
    phase_angle = 2.0 * math.pi / NFFT * phase_turn.astype(F32)
    cosine, sine = jnp.cos(phase_angle), jnp.sin(phase_angle)
    return jnp.concatenate([cosine, cosine], 1), jnp.concatenate([sine, sine], 1)


def rotate_kernel(a_ref, b_ref, cos_ref, sin_ref, plus_ref, minus_ref):
    half = DEPTH // 2
    for n, ref in enumerate((a_ref, b_ref)):

        @pl.loop(0, 8)
        def _(i):
            at = pl.ds(pl.multiple_of(i * 16, 16), 16)
            to = pl.ds(pl.multiple_of(n * 128 + i * 16, 16), 16)
            re = ref[at, :half].astype(F32)
            im = ref[at, half:].astype(F32)
            for m in range(LAGS):
                cosine, sine = cos_ref[m : m + 1, :], sin_ref[m : m + 1, :]
                rc, rs, ic, is_ = re * cosine, re * sine, im * cosine, im * sine
                plus_ref[m, to, :half] = (rc - is_).astype(BF16)
                plus_ref[m, to, half:] = (rs + ic).astype(BF16)
                minus_ref[m, to, :half] = (rc + is_).astype(BF16)
                minus_ref[m, to, half:] = (ic - rs).astype(BF16)


def rotations(chunks, cosine, sine):
    shape = jax.ShapeDtypeStruct((LAGS, BLOCK, DEPTH), BF16)
    return pl.pallas_call(
        rotate_kernel,
        out_shape=(shape, shape),
        compiler_params=params(16),
        cost_estimate=cost(2 * 8 * 256 * 2048, 6 * MIB),
        name="rotate",
    )(*chunks, cosine, sine)


def store_product(acc_ref, m, first, value, scale):
    n = value.shape[1]
    for h in range(2):
        for x in range(4):
            at = h * 128 + x * 32
            acc_ref[m, h, x, :, first : first + n] = (value[at : at + 32] * scale).astype(BF16)


def products(xi, parts, chunks, wide, scale, name):
    count = len(chunks)

    def kernel(xi_ref, *refs):
        ins, outs, acc_ref = refs[:count], refs[count : count + 4], refs[count + 4]
        for m in range(LAGS):
            for first, value in parts(m, ins):
                store_product(acc_ref, m, first, value, scale)
        for s in range(4):
            to = lax.rem(xi_ref[0] + s, 4)
            for m in range(LAGS):
                for h in range(2):
                    outs[s][h, m] = acc_ref[m, h, to]

    shape = jax.ShapeDtypeStruct((2, LAGS, 32, wide), BF16)
    whole = pl.BlockSpec(memory_space=pltpu.VMEM)
    return pl.pallas_call(
        kernel,
        in_specs=[pl.BlockSpec(memory_space=pltpu.SMEM)] + [whole] * count,
        out_specs=[whole] * 4,
        out_shape=(shape,) * 4,
        scratch_shapes=[pltpu.VMEM((LAGS, 2, 4, 32, wide), BF16)],
        compiler_params=params(28),
        cost_estimate=cost(2 * 2 * 256 * wide * DEPTH, 8 * MIB),
        name=name,
    )(xi, *chunks)


def both(a_ref, b_ref):
    return jnp.concatenate([a_ref[...], b_ref[...]], 0)


def sum_x(yi, groups):
    widths = [g[0].shape[3] for g in groups]
    total = sum(widths)
    flat = [a for g in groups for a in g]

    def kernel(yi_ref, *refs):
        keep_ref, send_ref = refs[-2:]
        mine, other = yi_ref[0], 1 - yi_ref[0]
        first = 0
        for k, n in enumerate(widths):
            four = refs[4 * k : 4 * k + 4]
            for m in range(LAGS):
                for r in range(0, 32, 16):
                    at = pl.ds(r, 16)
                    val = [f[mine, m, at, :].astype(F32) for f in four]
                    keep_ref[m, at, first : first + n] = (val[0] + val[1]) + (val[2] + val[3])
                    val = [f[other, m, at, :].astype(F32) for f in four]
                    send_ref[m, at, first : first + n] = ((val[0] + val[1]) + (val[2] + val[3])).astype(BF16)
            first += n

    whole = pl.BlockSpec(memory_space=pltpu.VMEM)
    return pl.pallas_call(
        kernel,
        in_specs=[pl.BlockSpec(memory_space=pltpu.SMEM)] + [whole] * len(flat),
        out_specs=[whole] * 2,
        out_shape=(jax.ShapeDtypeStruct((LAGS, 32, total), F32), jax.ShapeDtypeStruct((LAGS, 32, total), BF16)),
        compiler_params=params(16),
        cost_estimate=cost(1000, 2 * MIB),
        name="sum_x",
    )(yi, *flat)


def sum_y(ci, keep, recv, outputs):
    def kernel(ci_ref, keep_ref, recv_ref, *outs):
        for which in ("same", "other"):
            core = ci_ref[0] if which == "same" else 1 - ci_ref[0]
            at = pl.ds(pl.multiple_of(core * 16, 16), 16)
            for m in range(LAGS):
                for out, (pieces, kind) in zip(outs, outputs):
                    if kind != which:
                        continue
                    to = 0
                    for first, n in pieces:
                        cols = slice(first, first + n)
                        value = keep_ref[m, at, cols] + recv_ref[m, at, cols].astype(F32)
                        out[m, :, to : to + n] = value.astype(BF16)
                        to += n

    shapes = [jax.ShapeDtypeStruct((LAGS, 16, sum(n for _, n in p)), BF16) for p, _ in outputs]
    whole = pl.BlockSpec(memory_space=pltpu.VMEM)
    return pl.pallas_call(
        kernel,
        in_specs=[pl.BlockSpec(memory_space=pltpu.SMEM), whole, whole],
        out_specs=[whole] * len(shapes),
        out_shape=tuple(shapes),
        compiler_params=params(16),
        cost_estimate=cost(1000, MIB),
        name="sum_y",
    )(ci, keep, recv)


def finish(place, same, other):
    arrays = [a for a, _ in same] + [a for a, _ in other]
    lists = [(b, 0) for _, b in same] + [(b, 1) for _, b in other]

    def kernel(place_ref, *refs):
        out = refs[-1]
        z, y, c = place_ref[0], place_ref[1], place_ref[2]
        for ref, (blocks, kind) in zip(refs[:-1], lists):
            way = 1 - 2 * c if kind == 0 else 2 * c - 1
            for n, (dist, dy) in enumerate(blocks):
                zz = lax.rem(z - way * dist + 16, 8)
                yy = y if dy == 0 else 1 - y
                cols = pl.ds(pl.multiple_of((zz * 2 + yy) * BLOCK, BLOCK), BLOCK)
                for m in range(LAGS):
                    value = ref[m, :, n * BLOCK : (n + 1) * BLOCK].astype(F32)
                    if kind == 0:
                        out[m, :, cols] = value
                    else:
                        out[m, :, cols] += value

    whole = pl.BlockSpec(memory_space=pltpu.VMEM)
    return pl.pallas_call(
        kernel,
        in_specs=[pl.BlockSpec(memory_space=pltpu.SMEM)] + [whole] * len(arrays),
        out_specs=whole,
        out_shape=jax.ShapeDtypeStruct((LAGS, 16, 4096), F32),
        compiler_params=params(16),
        cost_estimate=cost(1000, MIB),
        name="finish",
    )(place, *arrays)


def chain_step(z, ylo, yhi, x, c):
    return z + sign(c), ylo, yhi, x, c


def y_step(z, ylo, yhi, x, c):
    return z, 1 - ylo, yhi, x, c


def y_cross(z, ylo, yhi, x, c):
    return z, 1 - ylo, yhi, x, 1 - c


def yhi_step(z, ylo, yhi, x, c):
    return z, ylo, 1 - yhi, x, c


def core_step(z, ylo, yhi, x, c):
    return z, ylo, yhi, x, 1 - c


def x_step(s):
    return lambda z, ylo, yhi, x, c: (z, ylo, yhi, x + s, c)


def back(d):
    return lambda z, ylo, yhi, x, c: (z - sign(c) * d, ylo, yhi, x, c)


def back_cross(d):
    return lambda z, ylo, yhi, x, c: (z - sign(c) * d, ylo, yhi, x, 1 - c)


def reduce_x(slots):
    return [slots[0]] + [move(slots[s], x_step(s)) for s in (1, 3, 2)]


def batch(yi, ci, groups, classes):
    keep, send = sum_x(yi, groups)
    recv = move(send, yhi_step)
    own, wy, ret = [], [], []
    first = 0
    for g, (n_own, n_wy, d) in zip(groups, classes):
        own.append((first, n_own))
        if n_wy:
            wy.append((first + n_own, n_wy))
        if d:
            ret.append((d, first + n_own + n_wy))
        first += g[0].shape[3]
    outputs = [(own, "same"), (own, "other"), (wy, "same"), (wy, "other")]
    for d, at in ret:
        outputs += [([(at, 2 * BLOCK)], "same"), ([(at, 2 * BLOCK)], "other")]
    got = sum_y(ci, keep, recv, outputs)
    same = [got[0], move(got[2], y_step)]
    other = [move(got[1], core_step), move(got[3], y_cross)]
    for k, (d, _) in enumerate(ret):
        same.append(move(got[4 + 2 * k], back(d)))
        other.append(move(got[5 + 2 * k], back_cross(d)))
    return same, other


def body(spectra, bin_index):
    scale = 1.0 / math.sqrt(32 * BINS)
    z, y = lax.axis_index("z"), lax.axis_index("ylo")
    yi, xi, ci = (lax.axis_index(a).astype(jnp.int32).reshape(1) for a in ("yhi", "x", "c"))
    place = jnp.stack([z, y, lax.axis_index("c")]).astype(jnp.int32)

    own = [whiten(spectra, 0), whiten(spectra, 1)]
    block = own
    arrived = []
    for _ in range(4):
        block = [move(b, chain_step) for b in block]
        arrived.append(block)
    near = [move(b, y_step) for b in own]

    cosine, sine = phases(bin_index)
    own_plus, own_minus = rotations(own, cosine, sine)
    near_plus, near_minus = rotations(near, cosine, sine)

    def all_pairs(m, ins, at=0):
        b = both(ins[at], ins[at + 1])
        op, om, np_, nm = ins[-4:]
        yield 0, dot_nt(op[m], b)
        yield BLOCK, dot_nt(np_[m], b)
        yield 2 * BLOCK, dot_nt(b, om[m])
        yield 3 * BLOCK, dot_nt(b, nm[m])

    def first_pairs(m, ins):
        op, om, np_, nm = ins[-4:]
        b = both(ins[0], ins[1])
        yield 0, dot_nt(op[m], both(ins[2], ins[3]))
        yield BLOCK, dot_nt(op[m], both(ins[4], ins[5]))
        yield 2 * BLOCK, dot_nt(op[m], b)
        yield 3 * BLOCK, dot_nt(np_[m], b)
        yield 4 * BLOCK, dot_nt(b, om[m])
        yield 5 * BLOCK, dot_nt(b, nm[m])

    def last_pairs(m, ins):
        b = both(ins[0], ins[1])
        yield 0, dot_nt(ins[2][m], b)
        yield BLOCK, dot_nt(ins[3][m], b)

    rotated = [own_plus, own_minus, near_plus, near_minus]
    g1 = reduce_x(products(xi, first_pairs, arrived[0] + own + near + rotated, 6 * BLOCK, scale, "pairs_0_1"))
    g2 = reduce_x(products(xi, all_pairs, arrived[1] + rotated, 4 * BLOCK, scale, "pairs_2"))
    g3 = reduce_x(products(xi, all_pairs, arrived[2] + rotated, 4 * BLOCK, scale, "pairs_3"))
    g4 = reduce_x(products(xi, last_pairs, arrived[3] + [own_plus, near_plus], 2 * BLOCK, scale, "pairs_4"))

    same1, other1 = batch(yi, ci, [g1, g2], [(3 * BLOCK, BLOCK, 1), (BLOCK, BLOCK, 2)])
    same2, other2 = batch(yi, ci, [g3, g4], [(BLOCK, BLOCK, 3), (BLOCK, BLOCK, 0)])
    blocks1 = [[(0, 0), (0, 1), (1, 0), (2, 0)], [(1, 1), (2, 1)], [(-1, 0), (-1, 1)], [(-2, 0), (-2, 1)]]
    blocks2 = [[(3, 0), (4, 0)], [(3, 1), (4, 1)], [(-3, 0), (-3, 1)]]
    ids = blocks1 + blocks2
    return finish(place, list(zip(same1 + same2, ids)), list(zip(other1 + other2, ids)))


def solution(mesh):
    torus = Mesh(mesh.devices.reshape(SIZES), AXES)
    placed = (P(None, ("yhi", "x", "c"), None, ("z", "ylo")), P())
    return jax.shard_map(
        body, mesh=torus, in_specs=placed, out_specs=P(None, AXES, None), check_vma=False
    )
```

```python
import math

import jax
import jax.numpy as jnp
import numpy as np
from jax import lax
from jax.experimental import pallas as pl
from jax.experimental.pallas import tpu as pltpu
from jax.sharding import Mesh
from jax.sharding import PartitionSpec as P

NFFT = 8192
LAGS = 2
LAG_STEP = 37
HALF = 64
BINS = 512
BLOCK = 256
DEPTH = 2048
AXES = ("z", "ylo", "yhi", "x", "c")
SIZES = (8, 2, 2, 4, 2)
F32 = jnp.float32
BF16 = jnp.bfloat16
MIB = 1 << 20


def dot_nt(a, b):
    return lax.dot_general(a, b, (((1,), (1,)), ((), ())), preferred_element_type=F32)


def params(mib, **kw):
    return pltpu.CompilerParams(vmem_limit_bytes=mib * MIB, **kw)


def cost(flops, bytes_accessed):
    return pl.CostEstimate(flops=flops, bytes_accessed=bytes_accessed, transcendentals=0)


def move(x, step):
    pairs = []
    for i, at in enumerate(np.ndindex(*SIZES)):
        to = tuple(int(v) % s for v, s in zip(step(*at), SIZES))
        pairs.append((i, int(np.ravel_multi_index(to, SIZES))))
    return lax.ppermute(x, AXES, pairs)


def sign(c):
    return 1 - 2 * c


def whiten_kernel(x_ref, o_ref):
    row = lax.broadcasted_iota(jnp.int32, (BINS, BINS), 0)
    col = lax.broadcasted_iota(jnp.int32, (BINS, BINS), 1)
    window = (jnp.abs(row - col) <= HALF).astype(F32).astype(BF16)
    pos = lax.broadcasted_iota(jnp.int32, (1, BINS), 1)
    count = jnp.minimum(pos + HALF, BINS - 1) - jnp.maximum(pos - HALF, 0) + 1
    inverse = 1.0 / count.astype(F32)
    for s in range(2):
        re = x_ref[0, s].astype(F32).T
        im = x_ref[1, s].astype(F32).T
        energy = re * re + im * im
        high = energy.astype(BF16)
        low = (energy - high.astype(F32)).astype(BF16)
        total = jnp.dot(high, window, preferred_element_type=F32)
        total += jnp.dot(low, window, preferred_element_type=F32)
        scale = lax.rsqrt(total * inverse + 1e-06)
        o_ref[:, s * BINS : (s + 1) * BINS] = (re * scale).astype(BF16)
        o_ref[:, (2 + s) * BINS : (3 + s) * BINS] = (im * scale).astype(BF16)


def whiten(spectra, half):
    return pl.pallas_call(
        whiten_kernel,
        grid=(1,),
        in_specs=[pl.BlockSpec((2, 2, BINS, 128), lambda i: (0, 0, 0, half))],
        out_specs=pl.BlockSpec((128, DEPTH), lambda i: (0, 0)),
        out_shape=jax.ShapeDtypeStruct((128, DEPTH), BF16),
        compiler_params=params(16),
        cost_estimate=cost(2 * 4 * 128 * 512 * 512, MIB),
        name="whiten",
    )(spectra)


def phases(bin_index):
    lag_samples = (jnp.arange(LAGS, dtype=jnp.int32) + 1) * LAG_STEP
    phase_turn = lag_samples[:, None] * bin_index[None, :] % NFFT
    phase_angle = 2.0 * math.pi / NFFT * phase_turn.astype(F32)
    cosine, sine = jnp.cos(phase_angle), jnp.sin(phase_angle)
    return jnp.concatenate([cosine, cosine], 1), jnp.concatenate([sine, sine], 1)


def rotate_kernel(a_ref, b_ref, cos_ref, sin_ref, plus_ref, minus_ref):
    half = DEPTH // 2
    for n, ref in enumerate((a_ref, b_ref)):

        @pl.loop(0, 8)
        def _(i):
            at = pl.ds(pl.multiple_of(i * 16, 16), 16)
            to = pl.ds(pl.multiple_of(n * 128 + i * 16, 16), 16)
            re = ref[at, :half].astype(F32)
            im = ref[at, half:].astype(F32)
            for m in range(LAGS):
                cosine, sine = cos_ref[m : m + 1, :], sin_ref[m : m + 1, :]
                rc, rs, ic, is_ = re * cosine, re * sine, im * cosine, im * sine
                plus_ref[m, to, :half] = (rc - is_).astype(BF16)
                plus_ref[m, to, half:] = (rs + ic).astype(BF16)
                minus_ref[m, to, :half] = (rc + is_).astype(BF16)
                minus_ref[m, to, half:] = (ic - rs).astype(BF16)


def rotations(chunks, cosine, sine):
    shape = jax.ShapeDtypeStruct((LAGS, BLOCK, DEPTH), BF16)
    return pl.pallas_call(
        rotate_kernel,
        out_shape=(shape, shape),
        compiler_params=params(16),
        cost_estimate=cost(2 * 8 * 256 * 2048, 6 * MIB),
        name="rotate",
    )(*chunks, cosine, sine)


def store_product(acc_ref, m, first, value, scale):
    n = value.shape[1]
    for h in range(2):
        for x in range(4):
            at = h * 128 + x * 32
            acc_ref[m, h, x, :, first : first + n] = (value[at : at + 32] * scale).astype(BF16)


def products(at, parts, chunks, wide, scale, name):
    count = len(chunks)

    def kernel(at_ref, *refs):
        ins, (keep_ref, send_ref), acc_ref = refs[:count], refs[count : count + 2], refs[count + 2]
        x, c = at_ref[0], at_ref[1]
        near, far = 1 + 2 * c, 3 - 2 * c
        for m in range(LAGS):
            for first, value in parts(m, ins):
                store_product(acc_ref, m, first, value, scale)
        slices = ((keep_ref, 0, x), (keep_ref, 1, x ^ far), (send_ref, 0, x ^ near), (send_ref, 1, x ^ 2))
        for out, k, which in slices:
            for m in range(LAGS):
                for h in range(2):
                    out[k, h, m] = acc_ref[m, h, which]

    shape = jax.ShapeDtypeStruct((2, 2, LAGS, 32, wide), BF16)
    whole = pl.BlockSpec(memory_space=pltpu.VMEM)
    return pl.pallas_call(
        kernel,
        in_specs=[pl.BlockSpec(memory_space=pltpu.SMEM)] + [whole] * count,
        out_specs=[whole] * 2,
        out_shape=(shape,) * 2,
        scratch_shapes=[pltpu.VMEM((LAGS, 2, 4, 32, wide), BF16)],
        compiler_params=params(24),
        cost_estimate=cost(2 * 2 * 256 * wide * DEPTH, 8 * MIB),
        name=name,
    )(at, *chunks)


def both(a_ref, b_ref):
    return jnp.concatenate([a_ref[...], b_ref[...]], 0)


def sum_1(keep, recv):
    n = keep.shape[4]

    def kernel(keep_ref, recv_ref, kept_ref, send_ref):
        for h in range(2):
            for m in range(LAGS):
                kept_ref[h, m] = keep_ref[0, h, m].astype(F32) + recv_ref[0, h, m].astype(F32)
                send_ref[h, m] = (keep_ref[1, h, m].astype(F32) + recv_ref[1, h, m].astype(F32)).astype(BF16)

    whole = pl.BlockSpec(memory_space=pltpu.VMEM)
    return pl.pallas_call(
        kernel,
        in_specs=[whole] * 2,
        out_specs=[whole] * 2,
        out_shape=tuple(jax.ShapeDtypeStruct((2, LAGS, 32, n), t) for t in (F32, BF16)),
        compiler_params=params(16),
        cost_estimate=cost(1000, MIB),
        name="sum_1",
    )(keep, recv)


def sum_2(yi, groups):
    widths = [g[0].shape[3] for g in groups]
    total = sum(widths)
    flat = [a for g in groups for a in g]

    def kernel(yi_ref, *refs):
        keep_ref, send_ref = refs[-2:]
        mine, other = yi_ref[0], 1 - yi_ref[0]
        first = 0
        for k, n in enumerate(widths):
            kept, recv = refs[2 * k], refs[2 * k + 1]
            for m in range(LAGS):
                keep_ref[m, :, first : first + n] = kept[mine, m] + recv[mine, m].astype(F32)
                send_ref[m, :, first : first + n] = (kept[other, m] + recv[other, m].astype(F32)).astype(BF16)
            first += n

    whole = pl.BlockSpec(memory_space=pltpu.VMEM)
    return pl.pallas_call(
        kernel,
        in_specs=[pl.BlockSpec(memory_space=pltpu.SMEM)] + [whole] * len(flat),
        out_specs=[whole] * 2,
        out_shape=(jax.ShapeDtypeStruct((LAGS, 32, total), F32), jax.ShapeDtypeStruct((LAGS, 32, total), BF16)),
        compiler_params=params(16),
        cost_estimate=cost(1000, MIB),
        name="sum_2",
    )(yi, *flat)


def sum_y(ci, keep, recv, outputs):
    def kernel(ci_ref, keep_ref, recv_ref, *outs):
        for which in ("same", "other"):
            core = ci_ref[0] if which == "same" else 1 - ci_ref[0]
            at = pl.ds(pl.multiple_of(core * 16, 16), 16)
            for m in range(LAGS):
                for out, (pieces, kind) in zip(outs, outputs):
                    if kind != which:
                        continue
                    to = 0
                    for first, n in pieces:
                        cols = slice(first, first + n)
                        value = keep_ref[m, at, cols] + recv_ref[m, at, cols].astype(F32)
                        out[m, :, to : to + n] = value.astype(BF16)
                        to += n

    shapes = [jax.ShapeDtypeStruct((LAGS, 16, sum(n for _, n in p)), BF16) for p, _ in outputs]
    whole = pl.BlockSpec(memory_space=pltpu.VMEM)
    return pl.pallas_call(
        kernel,
        in_specs=[pl.BlockSpec(memory_space=pltpu.SMEM), whole, whole],
        out_specs=[whole] * len(shapes),
        out_shape=tuple(shapes),
        compiler_params=params(16),
        cost_estimate=cost(1000, MIB),
        name="sum_y",
    )(ci, keep, recv)


def finish(place, same, other):
    arrays = [a for a, _ in same] + [a for a, _ in other]
    lists = [(b, 0) for _, b in same] + [(b, 1) for _, b in other]

    def kernel(place_ref, *refs):
        out = refs[-1]
        z, y, c = place_ref[0], place_ref[1], place_ref[2]
        for ref, (blocks, kind) in zip(refs[:-1], lists):
            way = 1 - 2 * c if kind == 0 else 2 * c - 1
            for n, (dist, dy) in enumerate(blocks):
                zz = lax.rem(z - way * dist + 16, 8)
                yy = y if dy == 0 else 1 - y
                cols = pl.ds(pl.multiple_of((zz * 2 + yy) * BLOCK, BLOCK), BLOCK)
                for m in range(LAGS):
                    value = ref[m, :, n * BLOCK : (n + 1) * BLOCK].astype(F32)
                    if kind == 0:
                        out[m, :, cols] = value
                    else:
                        out[m, :, cols] += value

    whole = pl.BlockSpec(memory_space=pltpu.VMEM)
    return pl.pallas_call(
        kernel,
        in_specs=[pl.BlockSpec(memory_space=pltpu.SMEM)] + [whole] * len(arrays),
        out_specs=whole,
        out_shape=jax.ShapeDtypeStruct((LAGS, 16, 4096), F32),
        compiler_params=params(16),
        cost_estimate=cost(1000, MIB),
        name="finish",
    )(place, *arrays)


def chain_step(z, ylo, yhi, x, c):
    return z + sign(c), ylo, yhi, x, c


def y_step(z, ylo, yhi, x, c):
    return z, 1 - ylo, yhi, x, c


def y_cross(z, ylo, yhi, x, c):
    return z, 1 - ylo, yhi, x, 1 - c


def yhi_step(z, ylo, yhi, x, c):
    return z, ylo, 1 - yhi, x, c


def core_step(z, ylo, yhi, x, c):
    return z, ylo, yhi, x, 1 - c


def x_near(z, ylo, yhi, x, c):
    return z, ylo, yhi, x ^ (1 + 2 * c), c


def x_far(z, ylo, yhi, x, c):
    return z, ylo, yhi, x ^ (3 - 2 * c), c


def back(d):
    return lambda z, ylo, yhi, x, c: (z - sign(c) * d, ylo, yhi, x, c)


def back_cross(d):
    return lambda z, ylo, yhi, x, c: (z - sign(c) * d, ylo, yhi, x, 1 - c)


def after(value, *others):
    return lax.optimization_barrier((value,) + others)[0]


def batch(yi, ci, groups, classes):
    keep, send = sum_2(yi, groups)
    recv = move(send, yhi_step)
    own, wy, ret = [], [], []
    first = 0
    for g, (n_own, n_wy, d) in zip(groups, classes):
        own.append((first, n_own))
        if n_wy:
            wy.append((first + n_own, n_wy))
        if d:
            ret.append((d, first + n_own + n_wy))
        first += g[0].shape[3]
    outputs = [(own, "same"), (own, "other"), (wy, "same"), (wy, "other")]
    for d, at in ret:
        outputs += [([(at, 2 * BLOCK)], "same"), ([(at, 2 * BLOCK)], "other")]
    got = sum_y(ci, keep, recv, outputs)
    same = [got[0], move(got[2], y_step)]
    other = [move(got[1], core_step), move(got[3], y_cross)]
    for k, (d, _) in enumerate(ret):
        same.append(move(got[4 + 2 * k], back(d)))
        other.append(move(got[5 + 2 * k], back_cross(d)))
    return same, other


def body(spectra, bin_index):
    scale = 1.0 / math.sqrt(32 * BINS)
    z, y = lax.axis_index("z"), lax.axis_index("ylo")
    yi, ci = (lax.axis_index(a).astype(jnp.int32).reshape(1) for a in ("yhi", "c"))
    at = jnp.stack([lax.axis_index("x"), lax.axis_index("c")]).astype(jnp.int32)
    place = jnp.stack([z, y, lax.axis_index("c")]).astype(jnp.int32)

    own = [whiten(spectra, 0), whiten(spectra, 1)]
    block = own
    arrived = []
    for _ in range(4):
        block = [move(b, chain_step) for b in block]
        arrived.append(block)
    near = [move(b, y_step) for b in own]

    cosine, sine = phases(bin_index)
    own_plus, own_minus = rotations(own, cosine, sine)
    near_plus, near_minus = rotations(near, cosine, sine)

    def all_pairs(m, ins, at=0):
        b = both(ins[at], ins[at + 1])
        op, om, np_, nm = ins[-4:]
        yield 0, dot_nt(op[m], b)
        yield BLOCK, dot_nt(np_[m], b)
        yield 2 * BLOCK, dot_nt(b, om[m])
        yield 3 * BLOCK, dot_nt(b, nm[m])

    def first_pairs(m, ins):
        op, om, np_, nm = ins[-4:]
        b = both(ins[0], ins[1])
        yield 0, dot_nt(op[m], both(ins[2], ins[3]))
        yield BLOCK, dot_nt(op[m], both(ins[4], ins[5]))
        yield 2 * BLOCK, dot_nt(op[m], b)
        yield 3 * BLOCK, dot_nt(np_[m], b)
        yield 4 * BLOCK, dot_nt(b, om[m])
        yield 5 * BLOCK, dot_nt(b, nm[m])

    def last_pairs(m, ins):
        b = both(ins[0], ins[1])
        yield 0, dot_nt(ins[2][m], b)
        yield BLOCK, dot_nt(ins[3][m], b)

    rotated = [own_plus, own_minus, near_plus, near_minus]
    at_a = after(at, arrived[1][0])
    keep_a, send_a = products(at_a, first_pairs, arrived[0] + own + near + rotated, 6 * BLOCK, scale, "pairs_0_1")
    recv_a = move(send_a, x_near)
    keep_b, send_b = products(after(at, keep_a), all_pairs, arrived[1] + rotated, 4 * BLOCK, scale, "pairs_2")
    recv_b = move(send_b, x_near)
    kept_a, send_a = sum_1(after(keep_a, arrived[2][1]), recv_a)
    recv_a = move(send_a, x_far)
    at_c = after(at, kept_a)
    keep_c, send_c = products(at_c, all_pairs, arrived[2] + rotated, 4 * BLOCK, scale, "pairs_3")
    recv_c = move(send_c, x_near)
    kept_b, send_b = sum_1(after(keep_b, keep_c), recv_b)
    recv_b = move(send_b, x_far)
    at_d = after(at, kept_b)
    keep_d, send_d = products(at_d, last_pairs, arrived[3] + [own_plus, near_plus], 2 * BLOCK, scale, "pairs_4")
    recv_d = move(send_d, x_near)
    kept_c, send_c = sum_1(after(keep_c, keep_d), recv_c)
    recv_c = move(send_c, x_far)
    kept_a = after(kept_a, kept_c)
    same1, other1 = batch(yi, ci, [(kept_a, recv_a), (kept_b, recv_b)], [(3 * BLOCK, BLOCK, 1), (BLOCK, BLOCK, 2)])
    kept_d, send_d = sum_1(keep_d, recv_d)
    recv_d = move(send_d, x_far)
    same2, other2 = batch(yi, ci, [(kept_c, recv_c), (kept_d, recv_d)], [(BLOCK, BLOCK, 3), (BLOCK, BLOCK, 0)])
    blocks1 = [[(0, 0), (0, 1), (1, 0), (2, 0)], [(1, 1), (2, 1)], [(-1, 0), (-1, 1)], [(-2, 0), (-2, 1)]]
    blocks2 = [[(3, 0), (4, 0)], [(3, 1), (4, 1)], [(-3, 0), (-3, 1)]]
    ids = blocks1 + blocks2
    return finish(place, list(zip(same1 + same2, ids)), list(zip(other1 + other2, ids)))


def solution(mesh):
    torus = Mesh(mesh.devices.reshape(SIZES), AXES)
    placed = (P(None, ("yhi", "x", "c"), None, ("z", "ylo")), P())
    return jax.shard_map(
        body, mesh=torus, in_specs=placed, out_specs=P(None, AXES, None), check_vma=False
    )
```

```python
import math

import jax
import jax.numpy as jnp
import numpy as np
from jax import lax
from jax.experimental import pallas as pl
from jax.experimental.pallas import tpu as pltpu
from jax.sharding import Mesh
from jax.sharding import PartitionSpec as P

NFFT = 8192
LAGS = 2
LAG_STEP = 37
HALF = 64
BINS = 512
BLOCK = 256
DEPTH = 2048
AXES = ("z", "ylo", "yhi", "x", "c")
SIZES = (8, 2, 2, 4, 2)
F32 = jnp.float32
BF16 = jnp.bfloat16
MIB = 1 << 20


def dot_nt(a, b):
    return lax.dot_general(a, b, (((1,), (1,)), ((), ())), preferred_element_type=F32)


def params(mib, **kw):
    return pltpu.CompilerParams(vmem_limit_bytes=mib * MIB, **kw)


def cost(flops, bytes_accessed):
    return pl.CostEstimate(flops=flops, bytes_accessed=bytes_accessed, transcendentals=0)


def move(x, step):
    pairs = []
    for i, at in enumerate(np.ndindex(*SIZES)):
        to = tuple(int(v) % s for v, s in zip(step(*at), SIZES))
        pairs.append((i, int(np.ravel_multi_index(to, SIZES))))
    return lax.ppermute(x, AXES, pairs)


def sign(c):
    return 1 - 2 * c


def whiten_kernel(place_ref, x_ref, o_ref):
    row = lax.broadcasted_iota(jnp.int32, (BINS, BINS), 0)
    col = lax.broadcasted_iota(jnp.int32, (BINS, BINS), 1)
    window = (jnp.abs(row - col) <= HALF).astype(F32).astype(BF16)
    pos = lax.broadcasted_iota(jnp.int32, (1, BINS), 1)
    count = jnp.minimum(pos + HALF, BINS - 1) - jnp.maximum(pos - HALF, 0) + 1
    inverse = 1.0 / count.astype(F32)
    for s in range(2):
        re = x_ref[0, s].astype(F32).T
        im = x_ref[1, s].astype(F32).T
        energy = re * re + im * im
        high = energy.astype(BF16)
        low = (energy - high.astype(F32)).astype(BF16)
        total = jnp.dot(high, window, preferred_element_type=F32)
        total += jnp.dot(low, window, preferred_element_type=F32)
        scale = lax.rsqrt(total * inverse + 1e-06)
        o_ref[:, s * BINS : (s + 1) * BINS] = (re * scale).astype(BF16)
        o_ref[:, (2 + s) * BINS : (3 + s) * BINS] = (im * scale).astype(BF16)


def whiten(place, spectra, half):
    return pl.pallas_call(
        whiten_kernel,
        grid=(1,),
        in_specs=[pl.BlockSpec(memory_space=pltpu.SMEM), pl.BlockSpec((2, 2, BINS, 128), lambda i: (0, 0, 0, half))],
        out_specs=pl.BlockSpec((128, DEPTH), lambda i: (0, 0)),
        out_shape=jax.ShapeDtypeStruct((128, DEPTH), BF16),
        compiler_params=params(12),
        cost_estimate=cost(2 * 4 * 128 * 512 * 512, MIB),
        name="whiten",
    )(place, spectra)


def phases(bin_index):
    lag_samples = (jnp.arange(LAGS, dtype=jnp.int32) + 1) * LAG_STEP
    phase_turn = lag_samples[:, None] * bin_index[None, :] % NFFT
    phase_angle = 2.0 * math.pi / NFFT * phase_turn.astype(F32)
    cosine, sine = jnp.cos(phase_angle), jnp.sin(phase_angle)
    return jnp.concatenate([cosine, cosine], 1), jnp.concatenate([sine, sine], 1)


def rotate_kernel(a_ref, b_ref, cos_ref, sin_ref, plus_ref, minus_ref):
    half = DEPTH // 2
    for n, ref in enumerate((a_ref, b_ref)):

        @pl.loop(0, 8)
        def _(i):
            at = pl.ds(pl.multiple_of(i * 16, 16), 16)
            to = pl.ds(pl.multiple_of(n * 128 + i * 16, 16), 16)
            re = ref[at, :half].astype(F32)
            im = ref[at, half:].astype(F32)
            for m in range(LAGS):
                cosine, sine = cos_ref[m : m + 1, :], sin_ref[m : m + 1, :]
                rc, rs, ic, is_ = re * cosine, re * sine, im * cosine, im * sine
                plus_ref[m, to, :half] = (rc - is_).astype(BF16)
                plus_ref[m, to, half:] = (rs + ic).astype(BF16)
                minus_ref[m, to, :half] = (rc + is_).astype(BF16)
                minus_ref[m, to, half:] = (ic - rs).astype(BF16)


def rotations(chunks, cosine, sine):
    shape = jax.ShapeDtypeStruct((LAGS, BLOCK, DEPTH), BF16)
    return pl.pallas_call(
        rotate_kernel,
        out_shape=(shape, shape),
        compiler_params=params(12),
        cost_estimate=cost(2 * 8 * 256 * 2048, 6 * MIB),
        name="rotate",
    )(*chunks, cosine, sine)


def store_product(acc_ref, m, first, value, scale):
    n = value.shape[1]
    for h in range(2):
        for x in range(4):
            at = h * 128 + x * 32
            acc_ref[m, h, x, :, first : first + n] = (value[at : at + 32] * scale).astype(BF16)


def products(at, parts, chunks, wide, scale, name):
    count = len(chunks)

    def kernel(at_ref, *refs):
        ins, (keep_ref, send_ref), acc_ref = refs[:count], refs[count : count + 2], refs[count + 2]
        x, c = at_ref[3], at_ref[4]
        near, far = 1 + 2 * c, 3 - 2 * c
        for m in range(LAGS):
            for first, value in parts(m, ins):
                store_product(acc_ref, m, first, value, scale)
        slices = ((keep_ref, 0, x), (keep_ref, 1, x ^ far), (send_ref, 0, x ^ near), (send_ref, 1, x ^ 2))
        for out, k, which in slices:
            for m in range(LAGS):
                for h in range(2):
                    out[k, h, m] = acc_ref[m, h, which]

    shape = jax.ShapeDtypeStruct((2, 2, LAGS, 32, wide), BF16)
    whole = pl.BlockSpec(memory_space=pltpu.VMEM)
    return pl.pallas_call(
        kernel,
        in_specs=[pl.BlockSpec(memory_space=pltpu.SMEM)] + [whole] * count,
        out_specs=[whole] * 2,
        out_shape=(shape,) * 2,
        scratch_shapes=[pltpu.VMEM((LAGS, 2, 4, 32, wide), BF16)],
        compiler_params=params(14),
        cost_estimate=cost(2 * 2 * 256 * wide * DEPTH, 8 * MIB),
        name=name,
    )(at, *chunks)


def both(a_ref, b_ref):
    return jnp.concatenate([a_ref[...], b_ref[...]], 0)


def call(kernel, scalars, arrays, shapes, name):
    whole = pl.BlockSpec(memory_space=pltpu.VMEM)
    lead = [] if scalars is None else [scalars]
    return pl.pallas_call(
        kernel,
        in_specs=[pl.BlockSpec(memory_space=pltpu.SMEM)] * len(lead) + [whole] * len(arrays),
        out_specs=[whole] * len(shapes),
        out_shape=tuple(jax.ShapeDtypeStruct(s, t) for s, t in shapes),
        compiler_params=params(12),
        cost_estimate=cost(1000, MIB),
        name=name,
    )(*lead, *arrays)


def sum_1(groups, picks):
    total = sum(n for _, _, n in picks)

    def kernel(*refs):
        kept_ref, send_ref = refs[-2:]
        for h in range(2):
            for m in range(LAGS):
                to = 0
                for g, first, n in picks:
                    cols, out = slice(first, first + n), slice(to, to + n)
                    keep, recv = refs[2 * g], refs[2 * g + 1]
                    kept_ref[h, m, :, out] = keep[0, h, m, :, cols].astype(F32) + recv[0, h, m, :, cols].astype(F32)
                    value = keep[1, h, m, :, cols].astype(F32) + recv[1, h, m, :, cols].astype(F32)
                    send_ref[h, m, :, out] = value.astype(BF16)
                    to += n

    shape = (2, LAGS, 32, total)
    return call(kernel, None, [r for g in groups for r in g], [(shape, F32), (shape, BF16)], "sum_1")


def sum_2(yi, kept, recv):
    n = kept.shape[3]

    def kernel(yi_ref, kept_ref, recv_ref, keep_ref, send_ref):
        mine, other = yi_ref[2], 1 - yi_ref[2]
        for m in range(LAGS):
            keep_ref[m] = kept_ref[mine, m] + recv_ref[mine, m].astype(F32)
            send_ref[m] = (kept_ref[other, m] + recv_ref[other, m].astype(F32)).astype(BF16)

    return call(kernel, yi, [kept, recv], [((LAGS, 32, n), F32), ((LAGS, 32, n), BF16)], "sum_2")


def sum_y(keep, recv, widths, extra=None):
    arrays = [keep, recv] + ([] if extra is None else [extra])
    more = 0 if extra is None else extra.shape[2]

    def kernel(*refs):
        keep_ref, recv_ref, outs = refs[0], refs[1], refs[len(arrays) :]
        for m in range(LAGS):
            first = 0
            for k, (out, n) in enumerate(zip(outs, widths)):
                to = 0
                if k == 1 and more:
                    out[m, :, :more] = refs[2][m]
                    to = more
                cols = slice(first, first + n)
                out[m, :, to : to + n] = (keep_ref[m, :, cols] + recv_ref[m, :, cols].astype(F32)).astype(BF16)
                first += n

    shapes = [((LAGS, 32, n + (more if k == 1 else 0)), BF16) for k, n in enumerate(widths)]
    return call(kernel, None, arrays, shapes, "sum_y")


def sum_last(yi, kept, recv):
    def kernel(yi_ref, kept_ref, recv_ref, keep, send, near_mine, near_other):
        mine, other = yi_ref[2], 1 - yi_ref[2]

        def total(h, m, cols):
            return kept_ref[h, m, :, cols] + recv_ref[h, m, :, cols].astype(F32)

        for m in range(LAGS):
            keep[m] = total(mine, m, slice(0, BLOCK))
            send[m] = total(other, m, slice(0, BLOCK)).astype(BF16)
            near_mine[m] = total(mine, m, slice(BLOCK, 2 * BLOCK)).astype(BF16)
            near_other[m] = total(other, m, slice(BLOCK, 2 * BLOCK)).astype(BF16)

    shape = (LAGS, 32, BLOCK)
    return call(kernel, yi, [kept, recv], [(shape, F32), (shape, BF16), (shape, BF16), (shape, BF16)], "sum_last")


def split_last(ci, keep, recv, near_a, near_b):
    def kernel(ci_ref, keep_ref, recv_ref, a_ref, b_ref, mine_ref, send_ref):
        for out, core in ((mine_ref, ci_ref[4]), (send_ref, 1 - ci_ref[4])):
            at = pl.ds(pl.multiple_of(core * 16, 16), 16)
            for m in range(LAGS):
                own = keep_ref[m, at, :] + recv_ref[m, at, :].astype(F32)
                near = a_ref[m, at, :].astype(F32) + b_ref[m, at, :].astype(F32)
                out[m, :, :BLOCK] = own.astype(out.dtype)
                out[m, :, BLOCK:] = near.astype(out.dtype)

    shape = (LAGS, 16, 2 * BLOCK)
    return call(kernel, ci, [keep, recv, near_a, near_b], [(shape, F32), (shape, BF16)], "split_last")


def split(ci, arrays):
    total = sum(a.shape[2] for a in arrays)

    def kernel(ci_ref, *refs):
        at = pl.ds(pl.multiple_of((1 - ci_ref[4]) * 16, 16), 16)
        first = 0
        for ref in refs[:-1]:
            n = ref.shape[2]
            for m in range(LAGS):
                refs[-1][m, :, first : first + n] = ref[m, at, :]
            first += n

    return call(kernel, ci, arrays, [((LAGS, 16, total), BF16)], "split")[0]


def finish(place, arrays, blocks, recv, last, last_recv, last_blocks):
    def kernel(place_ref, *refs):
        out = refs[-1]
        ins, recv_ref, last_ref, last_recv_ref = refs[:-4], refs[-4], refs[-3], refs[-2]
        z, y, c = place_ref[0], place_ref[1], place_ref[4]
        rows = pl.ds(pl.multiple_of(c * 16, 16), 16)

        def cols(block, way):
            dist, dy = block
            zz = lax.rem(z - way * dist + 16, 8)
            yy = y if dy == 0 else 1 - y
            return pl.ds(pl.multiple_of((zz * 2 + yy) * BLOCK, BLOCK), BLOCK)

        for m in range(LAGS):
            for ref, ids in zip(ins, blocks):
                for n, block in enumerate(ids):
                    out[m, :, cols(block, 1 - 2 * c)] = ref[m, rows, n * BLOCK : (n + 1) * BLOCK].astype(F32)
            for n, block in enumerate(last_blocks):
                out[m, :, cols(block, 1 - 2 * c)] = last_ref[m, :, n * BLOCK : (n + 1) * BLOCK]
            for ref, ids in ((recv_ref, sum(blocks, [])), (last_recv_ref, last_blocks)):
                for n, block in enumerate(ids):
                    out[m, :, cols(block, 2 * c - 1)] += ref[m, :, n * BLOCK : (n + 1) * BLOCK].astype(F32)

    given = list(arrays) + [recv, last, last_recv]
    return call(kernel, place, given, [((LAGS, 16, 4096), F32)], "finish")[0]


def chain_step(z, ylo, yhi, x, c):
    return z + sign(c), ylo, yhi, x, c


def y_step(z, ylo, yhi, x, c):
    return z, 1 - ylo, yhi, x, c


def y_both(z, ylo, yhi, x, c):
    return z, 1 - ylo, 1 - yhi, x, c


def yhi_step(z, ylo, yhi, x, c):
    return z, ylo, 1 - yhi, x, c


def core_step(z, ylo, yhi, x, c):
    return z, ylo, yhi, x, 1 - c


def x_near(z, ylo, yhi, x, c):
    return z, ylo, yhi, x ^ (1 + 2 * c), c


def x_far(z, ylo, yhi, x, c):
    return z, ylo, yhi, x ^ (3 - 2 * c), c


def back(d):
    return lambda z, ylo, yhi, x, c: (z - sign(c) * d, ylo, yhi, x, c)


def after(value, *others):
    return lax.optimization_barrier((value,) + others)[0]


def body(spectra, bin_index):
    scale = 1.0 / math.sqrt(32 * BINS)
    place = jnp.stack([lax.axis_index(a) for a in AXES]).astype(jnp.int32)
    at = yi = ci = place

    own = [whiten(place, spectra, 0), whiten(place, spectra, 1)]
    block = own
    arrived = []
    for _ in range(4):
        block = [move(b, chain_step) for b in block]
        arrived.append(block)
    near = [move(b, y_step) for b in own]

    cosine, sine = phases(bin_index)
    own_plus, own_minus = rotations(own, cosine, sine)
    near_plus, near_minus = rotations(near, cosine, sine)

    def all_pairs(m, ins, at=0):
        b = both(ins[at], ins[at + 1])
        op, om, np_, nm = ins[-4:]
        yield 0, dot_nt(op[m], b)
        yield BLOCK, dot_nt(np_[m], b)
        yield 2 * BLOCK, dot_nt(b, om[m])
        yield 3 * BLOCK, dot_nt(b, nm[m])

    def own_pairs(m, ins):
        op, om = ins[-2:]
        b = both(ins[0], ins[1])
        yield 0, dot_nt(op[m], both(ins[2], ins[3]))
        yield BLOCK, dot_nt(op[m], b)
        yield 2 * BLOCK, dot_nt(b, om[m])

    def near_pairs(m, ins):
        op, np_, nm = ins[-3:]
        b = both(ins[0], ins[1])
        yield 0, dot_nt(op[m], both(ins[2], ins[3]))
        yield BLOCK, dot_nt(np_[m], b)
        yield 2 * BLOCK, dot_nt(b, nm[m])

    def last_pairs(m, ins):
        b = both(ins[0], ins[1])
        yield 0, dot_nt(ins[2][m], b)
        yield BLOCK, dot_nt(ins[3][m], b)

    rotated = [own_plus, own_minus, near_plus, near_minus]
    straight = [(0, 0, 4 * BLOCK)]

    keep_o, send_o = products(at, own_pairs, arrived[0] + own + rotated[:2], 3 * BLOCK, scale, "pairs_own")
    recv_o = move(send_o, x_near)
    at_n = after(at, arrived[1][0], keep_o)
    near_rotated = [own_plus, near_plus, near_minus]
    keep_n, send_n = products(at_n, near_pairs, arrived[0] + near + near_rotated, 3 * BLOCK, scale, "pairs_near")
    recv_n = move(send_n, x_near)
    keep_b, send_b = products(after(at, keep_n), all_pairs, arrived[1] + rotated, 4 * BLOCK, scale, "pairs_2")
    recv_b = move(send_b, x_near)
    picks = [(0, 0, 2 * BLOCK), (1, 0, BLOCK), (1, BLOCK, BLOCK), (0, 2 * BLOCK, BLOCK), (1, 2 * BLOCK, BLOCK)]
    kept_a, send_a = sum_1([(after(keep_o, arrived[2][0], keep_b), recv_o), (keep_n, recv_n)], picks)
    recv_a = move(send_a, x_far)
    keep_c, send_c = products(after(at, kept_a), all_pairs, arrived[2] + rotated, 4 * BLOCK, scale, "pairs_3")
    recv_c = move(send_c, x_near)
    kept_b, send_b = sum_1([(after(keep_b, keep_c, arrived[3][0]), recv_b)], straight)
    recv_b = move(send_b, x_far)
    keep_a, send_a = sum_2(yi, after(kept_a, kept_b), recv_a)
    recv_a = move(send_a, yhi_step)
    kept_c, send_c = sum_1([(after(keep_c, keep_a, arrived[3][1]), recv_c)], straight)
    recv_c = move(send_c, x_far)
    at_d = after(at, kept_c)
    keep_d, send_d = products(at_d, last_pairs, arrived[3] + [own_plus, near_plus], 2 * BLOCK, scale, "pairs_4")
    recv_d = move(send_d, x_near)
    keep_b, send_b = sum_2(yi, after(kept_b, keep_d), recv_b)
    recv_b = move(send_b, yhi_step)
    keep_c, send_c = sum_2(yi, after(kept_c, keep_b), recv_c)
    recv_c = move(send_c, yhi_step)
    own_a, near_a, ret_1 = sum_y(after(keep_a, keep_c), recv_a, [3 * BLOCK, BLOCK, 2 * BLOCK])
    ret_1 = move(ret_1, back(1))
    kept_d, send_d = sum_1([(after(keep_d, own_a), recv_d)], [(0, 0, 2 * BLOCK)])
    recv_d = move(send_d, x_far)
    own_b, near_b, ret_2 = sum_y(after(keep_b, kept_d), recv_b, [BLOCK, BLOCK, 2 * BLOCK], near_a)
    ret_2 = move(ret_2, back(2))
    keep_d, *send_d = sum_last(yi, after(kept_d, own_b), recv_d)
    recv_d = [move(v, step) for v, step in zip(send_d, (yhi_step, y_step, y_both))]
    own_c, near_c, ret_3 = sum_y(after(keep_c, keep_d), recv_c, [BLOCK, BLOCK, 2 * BLOCK], near_b)
    ret_3 = move(ret_3, back(3))
    near_c = move(near_c, y_step)
    mine_d, other_d = split_last(ci, keep_d, *recv_d)
    other_d = move(other_d, core_step)
    arrays = [own_a, own_b, own_c, near_c, ret_1, ret_2, ret_3]
    blocks = [[(0, 0), (1, 0), (0, 1)], [(2, 0)], [(3, 0)], [(1, 1), (2, 1), (3, 1)]]
    blocks += [[(-d, 0), (-d, 1)] for d in (1, 2, 3)]
    others = move(split(ci, arrays), core_step)
    return finish(place, arrays, blocks, others, mine_d, other_d, [(4, 0), (4, 1)])


def solution(mesh):
    torus = Mesh(mesh.devices.reshape(SIZES), AXES)
    placed = (P(None, ("yhi", "x", "c"), None, ("z", "ylo")), P())
    return jax.shard_map(
        body, mesh=torus, in_specs=placed, out_specs=P(None, AXES, None), check_vma=False
    )
```

```python
import math

import jax
import jax.numpy as jnp
import numpy as np
from jax import lax
from jax.experimental import pallas as pl
from jax.experimental.pallas import tpu as pltpu
from jax.sharding import Mesh
from jax.sharding import PartitionSpec as P

NFFT = 8192
LAGS = 2
LAG_STEP = 37
HALF = 64
BINS = 512
BLOCK = 256
DEPTH = 2048
AXES = ("z", "ylo", "yhi", "x", "c")
SIZES = (8, 2, 2, 4, 2)
F32 = jnp.float32
BF16 = jnp.bfloat16
MIB = 1 << 20


def dot_nt(a, b):
    return lax.dot_general(a, b, (((1,), (1,)), ((), ())), preferred_element_type=F32)


def params(mib, **kw):
    return pltpu.CompilerParams(vmem_limit_bytes=mib * MIB, **kw)


def cost(flops, bytes_accessed):
    return pl.CostEstimate(flops=flops, bytes_accessed=bytes_accessed, transcendentals=0)


def move(x, step):
    pairs = []
    for i, at in enumerate(np.ndindex(*SIZES)):
        to = tuple(int(v) % s for v, s in zip(step(*at), SIZES))
        pairs.append((i, int(np.ravel_multi_index(to, SIZES))))
    return lax.ppermute(x, AXES, pairs)


def sign(c):
    return 1 - 2 * c


def whiten_kernel(x_ref, o_ref):
    row = lax.broadcasted_iota(jnp.int32, (BINS, BINS), 0)
    col = lax.broadcasted_iota(jnp.int32, (BINS, BINS), 1)
    window = (jnp.abs(row - col) <= HALF).astype(F32).astype(BF16)
    pos = lax.broadcasted_iota(jnp.int32, (1, BINS), 1)
    count = jnp.minimum(pos + HALF, BINS - 1) - jnp.maximum(pos - HALF, 0) + 1
    inverse = 1.0 / count.astype(F32)
    for s in range(2):
        re = x_ref[0, s].astype(F32).T
        im = x_ref[1, s].astype(F32).T
        energy = re * re + im * im
        high = energy.astype(BF16)
        low = (energy - high.astype(F32)).astype(BF16)
        total = jnp.dot(high, window, preferred_element_type=F32)
        total += jnp.dot(low, window, preferred_element_type=F32)
        scale = lax.rsqrt(total * inverse + 1e-06)
        o_ref[:, s * BINS : (s + 1) * BINS] = (re * scale).astype(BF16)
        o_ref[:, (2 + s) * BINS : (3 + s) * BINS] = (im * scale).astype(BF16)


def whiten(spectra, half):
    return pl.pallas_call(
        whiten_kernel,
        grid=(1,),
        in_specs=[pl.BlockSpec((2, 2, BINS, 128), lambda i: (0, 0, 0, half))],
        out_specs=pl.BlockSpec((128, DEPTH), lambda i: (0, 0)),
        out_shape=jax.ShapeDtypeStruct((128, DEPTH), BF16),
        compiler_params=params(12),
        cost_estimate=cost(2 * 4 * 128 * 512 * 512, MIB),
        name="whiten",
    )(spectra)


def phases(bin_index):
    lag_samples = (jnp.arange(LAGS, dtype=jnp.int32) + 1) * LAG_STEP
    phase_turn = lag_samples[:, None] * bin_index[None, :] % NFFT
    phase_angle = 2.0 * math.pi / NFFT * phase_turn.astype(F32)
    cosine, sine = jnp.cos(phase_angle), jnp.sin(phase_angle)
    return jnp.concatenate([cosine, cosine], 1), jnp.concatenate([sine, sine], 1)


def rotate_kernel(a_ref, b_ref, cos_ref, sin_ref, plus_ref, minus_ref):
    half = DEPTH // 2
    for n, ref in enumerate((a_ref, b_ref)):

        @pl.loop(0, 8)
        def _(i):
            at = pl.ds(pl.multiple_of(i * 16, 16), 16)
            to = pl.ds(pl.multiple_of(n * 128 + i * 16, 16), 16)
            re = ref[at, :half].astype(F32)
            im = ref[at, half:].astype(F32)
            for m in range(LAGS):
                cosine, sine = cos_ref[m : m + 1, :], sin_ref[m : m + 1, :]
                rc, rs, ic, is_ = re * cosine, re * sine, im * cosine, im * sine
                plus_ref[m, to, :half] = (rc - is_).astype(BF16)
                plus_ref[m, to, half:] = (rs + ic).astype(BF16)
                minus_ref[m, to, :half] = (rc + is_).astype(BF16)
                minus_ref[m, to, half:] = (ic - rs).astype(BF16)


def rotations(chunks, cosine, sine):
    shape = jax.ShapeDtypeStruct((LAGS, BLOCK, DEPTH), BF16)
    return pl.pallas_call(
        rotate_kernel,
        out_shape=(shape, shape),
        compiler_params=params(12),
        cost_estimate=cost(2 * 8 * 256 * 2048, 6 * MIB),
        name="rotate",
    )(*chunks, cosine, sine)


def store_product(acc_ref, m, first, value, scale):
    n = value.shape[1]
    for h in range(2):
        for x in range(4):
            at = h * 128 + x * 32
            acc_ref[m, h, x, :, first : first + n] = (value[at : at + 32] * scale).astype(BF16)


def products(at, parts, chunks, wide, scale, name):
    count = len(chunks)

    def kernel(at_ref, *refs):
        ins, (keep_ref, send_ref), acc_ref = refs[:count], refs[count : count + 2], refs[count + 2]
        x, c = at_ref[3], at_ref[4]
        near, far = 1 + 2 * c, 3 - 2 * c
        for m in range(LAGS):
            for first, value in parts(m, ins):
                store_product(acc_ref, m, first, value, scale)
        slices = ((keep_ref, 0, x), (keep_ref, 1, x ^ far), (send_ref, 0, x ^ near), (send_ref, 1, x ^ 2))
        for out, k, which in slices:
            for m in range(LAGS):
                for h in range(2):
                    out[k, h, m] = acc_ref[m, h, which]

    shape = jax.ShapeDtypeStruct((2, 2, LAGS, 32, wide), BF16)
    whole = pl.BlockSpec(memory_space=pltpu.VMEM)
    return pl.pallas_call(
        kernel,
        in_specs=[pl.BlockSpec(memory_space=pltpu.SMEM)] + [whole] * count,
        out_specs=[whole] * 2,
        out_shape=(shape,) * 2,
        scratch_shapes=[pltpu.VMEM((LAGS, 2, 4, 32, wide), BF16)],
        compiler_params=params(14),
        cost_estimate=cost(2 * 2 * 256 * wide * DEPTH, 8 * MIB),
        name=name,
    )(at, *chunks)


def both(a_ref, b_ref):
    return jnp.concatenate([a_ref[...], b_ref[...]], 0)


def call(kernel, scalars, arrays, shapes, name):
    whole = pl.BlockSpec(memory_space=pltpu.VMEM)
    lead = [] if scalars is None else [scalars]
    return pl.pallas_call(
        kernel,
        in_specs=[pl.BlockSpec(memory_space=pltpu.SMEM)] * len(lead) + [whole] * len(arrays),
        out_specs=[whole] * len(shapes),
        out_shape=tuple(jax.ShapeDtypeStruct(s, t) for s, t in shapes),
        compiler_params=params(12),
        cost_estimate=cost(1000, MIB),
        name=name,
    )(*lead, *arrays)


def sum_1(groups, picks):
    total = sum(n for _, _, n in picks)

    def kernel(*refs):
        kept_ref, send_ref = refs[-2:]
        for h in range(2):
            for m in range(LAGS):
                to = 0
                for g, first, n in picks:
                    cols, out = slice(first, first + n), slice(to, to + n)
                    keep, recv = refs[2 * g], refs[2 * g + 1]
                    kept_ref[h, m, :, out] = keep[0, h, m, :, cols].astype(F32) + recv[0, h, m, :, cols].astype(F32)
                    value = keep[1, h, m, :, cols].astype(F32) + recv[1, h, m, :, cols].astype(F32)
                    send_ref[h, m, :, out] = value.astype(BF16)
                    to += n

    shape = (2, LAGS, 32, total)
    return call(kernel, None, [r for g in groups for r in g], [(shape, F32), (shape, BF16)], "sum_1")


def sum_2(place, groups):
    widths = [g[0].shape[3] for g in groups]

    def kernel(place_ref, *refs):
        keep_ref, send_ref = refs[-2:]
        mine, other = place_ref[2], 1 - place_ref[2]
        first = 0
        for k, n in enumerate(widths):
            kept, recv, cols = refs[2 * k], refs[2 * k + 1], slice(first, first + n)
            for m in range(LAGS):
                keep_ref[m, :, cols] = kept[mine, m] + recv[mine, m].astype(F32)
                send_ref[m, :, cols] = (kept[other, m] + recv[other, m].astype(F32)).astype(BF16)
            first += n

    shape = (LAGS, 32, sum(widths))
    return call(kernel, place, [r for g in groups for r in g], [(shape, F32), (shape, BF16)], "sum_2")


def sum_y(keep, recv, outputs, extra=None):
    arrays = [keep, recv] + ([] if extra is None else [extra])
    more = 0 if extra is None else extra.shape[2]

    def kernel(*refs):
        keep_ref, recv_ref, outs = refs[0], refs[1], refs[len(arrays) :]
        for m in range(LAGS):
            for k, (out, picks) in enumerate(zip(outs, outputs)):
                to = 0
                if k == 1 and more:
                    out[m, :, :more] = refs[2][m]
                    to = more
                for first, n in picks:
                    cols = slice(first, first + n)
                    out[m, :, to : to + n] = (keep_ref[m, :, cols] + recv_ref[m, :, cols].astype(F32)).astype(BF16)
                    to += n

    shapes = [((LAGS, 32, sum(n for _, n in p) + (more if k == 1 else 0)), BF16) for k, p in enumerate(outputs)]
    return call(kernel, None, arrays, shapes, "sum_y")


def split(place, arrays):
    total = sum(a.shape[2] for a in arrays)

    def kernel(place_ref, *refs):
        at = pl.ds(pl.multiple_of((1 - place_ref[4]) * 16, 16), 16)
        first = 0
        for ref in refs[:-1]:
            n = ref.shape[2]
            for m in range(LAGS):
                refs[-1][m, :, first : first + n] = ref[m, at, :]
            first += n

    return call(kernel, place, arrays, [((LAGS, 16, total), BF16)], "split")[0]


def finish(place, arrays, blocks, recv):
    def kernel(place_ref, *refs):
        ins, recv_ref, out = refs[:-2], refs[-2], refs[-1]
        z, y, c = place_ref[0], place_ref[1], place_ref[4]
        rows = pl.ds(pl.multiple_of(c * 16, 16), 16)

        def cols(block, way):
            dist, dy = block
            zz = lax.rem(z - way * dist + 16, 8)
            yy = y if dy == 0 else 1 - y
            return pl.ds(pl.multiple_of((zz * 2 + yy) * BLOCK, BLOCK), BLOCK)

        for m in range(LAGS):
            for ref, ids in zip(ins, blocks):
                for n, block in enumerate(ids):
                    out[m, :, cols(block, 1 - 2 * c)] = ref[m, rows, n * BLOCK : (n + 1) * BLOCK].astype(F32)
            for n, block in enumerate(sum(blocks, [])):
                out[m, :, cols(block, 2 * c - 1)] += recv_ref[m, :, n * BLOCK : (n + 1) * BLOCK].astype(F32)

    return call(kernel, place, list(arrays) + [recv], [((LAGS, 16, 4096), F32)], "finish")[0]


def chain_step(z, ylo, yhi, x, c):
    return z + sign(c), ylo, yhi, x, c


def y_step(z, ylo, yhi, x, c):
    return z, 1 - ylo, yhi, x, c


def yhi_step(z, ylo, yhi, x, c):
    return z, ylo, 1 - yhi, x, c


def core_step(z, ylo, yhi, x, c):
    return z, ylo, yhi, x, 1 - c


def x_near(z, ylo, yhi, x, c):
    return z, ylo, yhi, x ^ (1 + 2 * c), c


def x_far(z, ylo, yhi, x, c):
    return z, ylo, yhi, x ^ (3 - 2 * c), c


def back(d):
    return lambda z, ylo, yhi, x, c: (z - sign(c) * d, ylo, yhi, x, c)


def after(value, *others):
    return lax.optimization_barrier((value,) + others)[0]


def body(spectra, bin_index):
    scale = 1.0 / math.sqrt(32 * BINS)
    place = jnp.stack([lax.axis_index(a) for a in AXES]).astype(jnp.int32)

    spectra = after(spectra, place)
    own = [whiten(spectra, 0), whiten(spectra, 1)]
    near = [move(b, y_step) for b in own]
    first = [move(b, chain_step) for b in own]
    first[0] = after(first[0], near[0])
    second = [move(b, chain_step) for b in first]

    cosine, sine = phases(bin_index)
    own_plus, own_minus = rotations(own, cosine, sine)
    near_plus, near_minus = rotations(near, cosine, sine)

    def all_pairs(m, ins, at=0):
        b = both(ins[at], ins[at + 1])
        op, om, np_, nm = ins[-4:]
        yield 0, dot_nt(op[m], b)
        yield BLOCK, dot_nt(np_[m], b)
        yield 2 * BLOCK, dot_nt(b, om[m])
        yield 3 * BLOCK, dot_nt(b, nm[m])

    def own_pairs(m, ins):
        op, om = ins[-2:]
        b = both(ins[0], ins[1])
        yield 0, dot_nt(op[m], both(ins[2], ins[3]))
        yield BLOCK, dot_nt(op[m], b)
        yield 2 * BLOCK, dot_nt(b, om[m])

    def near_pairs(m, ins):
        op, np_, nm = ins[-3:]
        b = both(ins[0], ins[1])
        yield 0, dot_nt(op[m], both(ins[2], ins[3]))
        yield BLOCK, dot_nt(np_[m], b)
        yield 2 * BLOCK, dot_nt(b, nm[m])

    def last_pairs(m, ins):
        b = both(ins[0], ins[1])
        yield 0, dot_nt(ins[2][m], b)
        yield BLOCK, dot_nt(ins[3][m], b)

    rotated = [own_plus, own_minus, near_plus, near_minus]
    straight = [(0, 0, 4 * BLOCK)]

    keep_o, send_o = products(place, own_pairs, first + own + rotated[:2], 3 * BLOCK, scale, "pairs_own")
    recv_o = move(send_o, x_near)
    third = [move(b, chain_step) for b in (after(second[0], near[1], keep_o), second[1])]
    fourth = [move(b, chain_step) for b in third]
    at = after(place, second[1], keep_o)
    near_rotated = [own_plus, near_plus, near_minus]
    keep_n, send_n = products(at, near_pairs, first + near + near_rotated, 3 * BLOCK, scale, "pairs_near")
    recv_n = move(send_n, x_near)
    at = after(place, keep_n, third[0])
    keep_b, send_b = products(at, all_pairs, second + rotated, 4 * BLOCK, scale, "pairs_2")
    recv_b = move(send_b, x_near)
    picks = [(0, 0, 2 * BLOCK), (1, 0, BLOCK), (1, BLOCK, BLOCK), (0, 2 * BLOCK, BLOCK), (1, 2 * BLOCK, BLOCK)]
    kept_a, send_a = sum_1([(after(keep_o, keep_b), recv_o), (keep_n, recv_n)], picks)
    recv_a = move(send_a, x_far)
    at = after(place, kept_a)
    keep_c, send_c = products(at, all_pairs, third + rotated, 4 * BLOCK, scale, "pairs_3")
    recv_c = move(send_c, x_near)
    kept_b, send_b = sum_1([(after(keep_b, keep_c, fourth[0]), recv_b)], straight)
    recv_b = move(send_b, x_far)
    at = after(place, kept_b)
    keep_d, send_d = products(at, last_pairs, fourth + [own_plus, near_plus], 2 * BLOCK, scale, "pairs_4")
    recv_d = move(send_d, x_near)
    kept_c, send_c = sum_1([(after(keep_c, keep_d), recv_c)], straight)
    recv_c = move(send_c, x_far)
    keep_ab, send_ab = sum_2(place, [(after(kept_a, kept_c), recv_a), (kept_b, recv_b)])
    recv_ab = move(send_ab, yhi_step)
    kept_d, send_d = sum_1([(after(keep_d, keep_ab), recv_d)], [(0, 0, 2 * BLOCK)])
    recv_d = move(send_d, x_far)
    keep_cd, send_cd = sum_2(place, [(kept_c, recv_c), (kept_d, recv_d)])
    recv_cd = move(send_cd, yhi_step)
    outputs = [[(0, 768), (1536, 256)], [(768, 256), (1792, 256)], [(1024, 512)], [(2048, 512)]]
    own_ab, near_ab, ret_1, ret_2 = sum_y(after(keep_ab, keep_cd), recv_ab, outputs)
    ret_1, ret_2 = move(ret_1, back(1)), move(ret_2, back(2))
    outputs = [[(0, 256), (1024, 256)], [(256, 256), (1280, 256)], [(512, 512)]]
    own_cd, near_all, ret_3 = sum_y(after(keep_cd, own_ab), recv_cd, outputs, near_ab)
    ret_3 = move(ret_3, back(3))
    near_all = move(near_all, y_step)
    arrays = [own_ab, own_cd, near_all, ret_1, ret_2, ret_3]
    blocks = [[(0, 0), (1, 0), (0, 1), (2, 0)], [(3, 0), (4, 0)], [(1, 1), (2, 1), (3, 1), (4, 1)]]
    blocks += [[(-d, 0), (-d, 1)] for d in (1, 2, 3)]
    others = move(split(place, arrays), core_step)
    return finish(place, arrays, blocks, others)


def solution(mesh):
    torus = Mesh(mesh.devices.reshape(SIZES), AXES)
    placed = (P(None, ("yhi", "x", "c"), None, ("z", "ylo")), P())
    return jax.shard_map(
        body, mesh=torus, in_specs=placed, out_specs=P(None, AXES, None), check_vma=False
    )
```

```python
import math

import jax
import jax.numpy as jnp
import numpy as np
from jax import lax
from jax.experimental import pallas as pl
from jax.experimental.pallas import tpu as pltpu
from jax.sharding import Mesh
from jax.sharding import PartitionSpec as P

NFFT = 8192
LAGS = 2
LAG_STEP = 37
HALF = 64
BINS = 512
BLOCK = 256
DEPTH = 2048
AXES = ("z", "ylo", "yhi", "x", "c")
SIZES = (8, 2, 2, 4, 2)
F32 = jnp.float32
BF16 = jnp.bfloat16
MIB = 1 << 20


def dot_nt(a, b):
    return lax.dot_general(a, b, (((1,), (1,)), ((), ())), preferred_element_type=F32)


def params(mib, **kw):
    return pltpu.CompilerParams(vmem_limit_bytes=mib * MIB, **kw)


def cost(flops, bytes_accessed):
    return pl.CostEstimate(flops=flops // 10, bytes_accessed=bytes_accessed // 10, transcendentals=0)


def move(x, step):
    pairs = []
    for i, at in enumerate(np.ndindex(*SIZES)):
        to = tuple(int(v) % s for v, s in zip(step(*at), SIZES))
        pairs.append((i, int(np.ravel_multi_index(to, SIZES))))
    return lax.ppermute(x, AXES, pairs)


def sign(c):
    return 1 - 2 * c


def whiten_kernel(x_ref, o_ref):
    row = lax.broadcasted_iota(jnp.int32, (BINS, BINS), 0)
    col = lax.broadcasted_iota(jnp.int32, (BINS, BINS), 1)
    window = (jnp.abs(row - col) <= HALF).astype(F32).astype(BF16)
    pos = lax.broadcasted_iota(jnp.int32, (1, BINS), 1)
    count = jnp.minimum(pos + HALF, BINS - 1) - jnp.maximum(pos - HALF, 0) + 1
    inverse = 1.0 / count.astype(F32)
    for s in range(2):
        re = x_ref[0, s].astype(F32).T
        im = x_ref[1, s].astype(F32).T
        energy = re * re + im * im
        high = energy.astype(BF16)
        low = (energy - high.astype(F32)).astype(BF16)
        total = jnp.dot(high, window, preferred_element_type=F32)
        total += jnp.dot(low, window, preferred_element_type=F32)
        scale = lax.rsqrt(total * inverse + 1e-06)
        o_ref[:, s * BINS : (s + 1) * BINS] = (re * scale).astype(BF16)
        o_ref[:, (2 + s) * BINS : (3 + s) * BINS] = (im * scale).astype(BF16)


def whiten(spectra, half):
    return pl.pallas_call(
        whiten_kernel,
        grid=(1,),
        in_specs=[pl.BlockSpec((2, 2, BINS, 128), lambda i: (0, 0, 0, half))],
        out_specs=pl.BlockSpec((128, DEPTH), lambda i: (0, 0)),
        out_shape=jax.ShapeDtypeStruct((128, DEPTH), BF16),
        compiler_params=params(12),
        cost_estimate=cost(2 * 4 * 128 * 512 * 512, MIB),
        name="whiten",
    )(spectra)


def phases(bin_index):
    lag_samples = (jnp.arange(LAGS, dtype=jnp.int32) + 1) * LAG_STEP
    phase_turn = lag_samples[:, None] * bin_index[None, :] % NFFT
    phase_angle = 2.0 * math.pi / NFFT * phase_turn.astype(F32)
    cosine, sine = jnp.cos(phase_angle), jnp.sin(phase_angle)
    return jnp.concatenate([cosine, cosine], 1), jnp.concatenate([sine, sine], 1)


def rotate_kernel(a_ref, b_ref, cos_ref, sin_ref, plus_ref, minus_ref):
    half = DEPTH // 2
    for n, ref in enumerate((a_ref, b_ref)):

        @pl.loop(0, 8)
        def _(i):
            at = pl.ds(pl.multiple_of(i * 16, 16), 16)
            to = pl.ds(pl.multiple_of(n * 128 + i * 16, 16), 16)
            re = ref[at, :half].astype(F32)
            im = ref[at, half:].astype(F32)
            for m in range(LAGS):
                cosine, sine = cos_ref[m : m + 1, :], sin_ref[m : m + 1, :]
                rc, rs, ic, is_ = re * cosine, re * sine, im * cosine, im * sine
                plus_ref[m, to, :half] = (rc - is_).astype(BF16)
                plus_ref[m, to, half:] = (rs + ic).astype(BF16)
                minus_ref[m, to, :half] = (rc + is_).astype(BF16)
                minus_ref[m, to, half:] = (ic - rs).astype(BF16)


def rotations(chunks, cosine, sine):
    shape = jax.ShapeDtypeStruct((LAGS, BLOCK, DEPTH), BF16)
    return pl.pallas_call(
        rotate_kernel,
        out_shape=(shape, shape),
        compiler_params=params(12),
        cost_estimate=cost(2 * 8 * 256 * 2048, 6 * MIB),
        name="rotate",
    )(*chunks, cosine, sine)


def store_product(acc_ref, m, first, value, scale):
    n = value.shape[1]
    for h in range(2):
        for x in range(4):
            at = h * 128 + x * 32
            acc_ref[m, h, x, :, first : first + n] = (value[at : at + 32] * scale).astype(BF16)


def products(at, parts, chunks, wide, scale, name):
    count = len(chunks)

    def kernel(at_ref, *refs):
        ins, (keep_ref, send_ref), acc_ref = refs[:count], refs[count : count + 2], refs[count + 2]
        x, c = at_ref[3], at_ref[4]
        near, far = 1 + 2 * c, 3 - 2 * c
        for m in range(LAGS):
            for first, value in parts(m, ins):
                store_product(acc_ref, m, first, value, scale)
        slices = ((keep_ref, 0, x), (keep_ref, 1, x ^ far), (send_ref, 0, x ^ near), (send_ref, 1, x ^ 2))
        for out, k, which in slices:
            for m in range(LAGS):
                for h in range(2):
                    out[k, h, m] = acc_ref[m, h, which]

    shape = jax.ShapeDtypeStruct((2, 2, LAGS, 32, wide), BF16)
    whole = pl.BlockSpec(memory_space=pltpu.VMEM)
    return pl.pallas_call(
        kernel,
        in_specs=[pl.BlockSpec(memory_space=pltpu.SMEM)] + [whole] * count,
        out_specs=[whole] * 2,
        out_shape=(shape,) * 2,
        scratch_shapes=[pltpu.VMEM((LAGS, 2, 4, 32, wide), BF16)],
        compiler_params=params(14),
        cost_estimate=cost(2 * 2 * 256 * wide * DEPTH, 8 * MIB),
        name=name,
    )(at, *chunks)


def both(a_ref, b_ref):
    return jnp.concatenate([a_ref[...], b_ref[...]], 0)


def call(kernel, scalars, arrays, shapes, name):
    whole = pl.BlockSpec(memory_space=pltpu.VMEM)
    lead = [] if scalars is None else [scalars]
    return pl.pallas_call(
        kernel,
        in_specs=[pl.BlockSpec(memory_space=pltpu.SMEM)] * len(lead) + [whole] * len(arrays),
        out_specs=[whole] * len(shapes),
        out_shape=tuple(jax.ShapeDtypeStruct(s, t) for s, t in shapes),
        compiler_params=params(12),
        cost_estimate=cost(1000, 80 * MIB),
        name=name,
    )(*lead, *arrays)


def sum_1(groups, picks):
    total = sum(n for _, _, n in picks)

    def kernel(*refs):
        kept_ref, send_ref = refs[-2:]
        for h in range(2):
            for m in range(LAGS):
                to = 0
                for g, first, n in picks:
                    cols, out = slice(first, first + n), slice(to, to + n)
                    keep, recv = refs[2 * g], refs[2 * g + 1]
                    kept_ref[h, m, :, out] = keep[0, h, m, :, cols].astype(F32) + recv[0, h, m, :, cols].astype(F32)
                    value = keep[1, h, m, :, cols].astype(F32) + recv[1, h, m, :, cols].astype(F32)
                    send_ref[h, m, :, out] = value.astype(BF16)
                    to += n

    shape = (2, LAGS, 32, total)
    return call(kernel, None, [r for g in groups for r in g], [(shape, F32), (shape, BF16)], "sum_1")


def sum_2(place, groups):
    widths = [g[0].shape[3] for g in groups]

    def kernel(place_ref, *refs):
        keep_ref, send_ref = refs[-2:]
        mine, other = place_ref[2], 1 - place_ref[2]
        first = 0
        for k, n in enumerate(widths):
            kept, recv, cols = refs[2 * k], refs[2 * k + 1], slice(first, first + n)
            for m in range(LAGS):
                keep_ref[m, :, cols] = kept[mine, m] + recv[mine, m].astype(F32)
                send_ref[m, :, cols] = (kept[other, m] + recv[other, m].astype(F32)).astype(BF16)
            first += n

    shape = (LAGS, 32, sum(widths))
    return call(kernel, place, [r for g in groups for r in g], [(shape, F32), (shape, BF16)], "sum_2")


def sum_y(keep, recv, outputs, extra=None):
    arrays = [keep, recv] + ([] if extra is None else [extra])
    more = 0 if extra is None else extra.shape[2]

    def kernel(*refs):
        keep_ref, recv_ref, outs = refs[0], refs[1], refs[len(arrays) :]
        for m in range(LAGS):
            for k, (out, picks) in enumerate(zip(outs, outputs)):
                to = 0
                if k == 1 and more:
                    out[m, :, :more] = refs[2][m]
                    to = more
                for first, n in picks:
                    cols = slice(first, first + n)
                    out[m, :, to : to + n] = (keep_ref[m, :, cols] + recv_ref[m, :, cols].astype(F32)).astype(BF16)
                    to += n

    shapes = [((LAGS, 32, sum(n for _, n in p) + (more if k == 1 else 0)), BF16) for k, p in enumerate(outputs)]
    return call(kernel, None, arrays, shapes, "sum_y")


def split(place, arrays):
    total = sum(a.shape[2] for a in arrays)

    def kernel(place_ref, *refs):
        at = pl.ds(pl.multiple_of((1 - place_ref[4]) * 16, 16), 16)
        first = 0
        for ref in refs[:-1]:
            n = ref.shape[2]
            for m in range(LAGS):
                refs[-1][m, :, first : first + n] = ref[m, at, :]
            first += n

    return call(kernel, place, arrays, [((LAGS, 16, total), BF16)], "split")[0]


def finish(place, arrays, blocks, recv):
    def kernel(place_ref, *refs):
        ins, recv_ref, out = refs[:-2], refs[-2], refs[-1]
        z, y, c = place_ref[0], place_ref[1], place_ref[4]
        rows = pl.ds(pl.multiple_of(c * 16, 16), 16)

        def cols(block, way):
            dist, dy = block
            zz = lax.rem(z - way * dist + 16, 8)
            yy = y if dy == 0 else 1 - y
            return pl.ds(pl.multiple_of((zz * 2 + yy) * BLOCK, BLOCK), BLOCK)

        for m in range(LAGS):
            for ref, ids in zip(ins, blocks):
                for n, block in enumerate(ids):
                    out[m, :, cols(block, 1 - 2 * c)] = ref[m, rows, n * BLOCK : (n + 1) * BLOCK].astype(F32)
            for n, block in enumerate(sum(blocks, [])):
                out[m, :, cols(block, 2 * c - 1)] += recv_ref[m, :, n * BLOCK : (n + 1) * BLOCK].astype(F32)

    return call(kernel, place, list(arrays) + [recv], [((LAGS, 16, 4096), F32)], "finish")[0]


def chain_step(z, ylo, yhi, x, c):
    return z + sign(c), ylo, yhi, x, c


def y_step(z, ylo, yhi, x, c):
    return z, 1 - ylo, yhi, x, c


def yhi_step(z, ylo, yhi, x, c):
    return z, ylo, 1 - yhi, x, c


def core_step(z, ylo, yhi, x, c):
    return z, ylo, yhi, x, 1 - c


def x_near(z, ylo, yhi, x, c):
    return z, ylo, yhi, x ^ (1 + 2 * c), c


def x_far(z, ylo, yhi, x, c):
    return z, ylo, yhi, x ^ (3 - 2 * c), c


def back(d):
    return lambda z, ylo, yhi, x, c: (z - sign(c) * d, ylo, yhi, x, c)


def after(value, *others):
    return lax.optimization_barrier((value,) + others)[0]


def body(spectra, bin_index):
    scale = 1.0 / math.sqrt(32 * BINS)
    place = jnp.stack([lax.axis_index(a) for a in AXES]).astype(jnp.int32)

    spectra = after(spectra, place)
    own = [whiten(spectra, 0), whiten(spectra, 1)]
    near = [move(b, y_step) for b in own]
    first = [move(b, chain_step) for b in own]
    first[0] = after(first[0], near[0])
    second = [move(b, chain_step) for b in first]

    cosine, sine = phases(bin_index)
    own_plus, own_minus = rotations(own, cosine, sine)
    near_plus, near_minus = rotations(near, cosine, sine)

    def all_pairs(m, ins, at=0):
        b = both(ins[at], ins[at + 1])
        op, om, np_, nm = ins[-4:]
        yield 0, dot_nt(op[m], b)
        yield BLOCK, dot_nt(np_[m], b)
        yield 2 * BLOCK, dot_nt(b, om[m])
        yield 3 * BLOCK, dot_nt(b, nm[m])

    def own_pairs(m, ins):
        op, om = ins[-2:]
        b = both(ins[0], ins[1])
        yield 0, dot_nt(op[m], both(ins[2], ins[3]))
        yield BLOCK, dot_nt(op[m], b)
        yield 2 * BLOCK, dot_nt(b, om[m])

    def near_pairs(m, ins):
        op, np_, nm = ins[-3:]
        b = both(ins[0], ins[1])
        yield 0, dot_nt(op[m], both(ins[2], ins[3]))
        yield BLOCK, dot_nt(np_[m], b)
        yield 2 * BLOCK, dot_nt(b, nm[m])

    def last_pairs(m, ins):
        b = both(ins[0], ins[1])
        yield 0, dot_nt(ins[2][m], b)
        yield BLOCK, dot_nt(ins[3][m], b)

    rotated = [own_plus, own_minus, near_plus, near_minus]
    straight = [(0, 0, 4 * BLOCK)]

    keep_o, send_o = products(place, own_pairs, first + own + rotated[:2], 3 * BLOCK, scale, "pairs_own")
    recv_o = move(send_o, x_near)
    third = [move(b, chain_step) for b in (after(second[0], near[1], keep_o), second[1])]
    fourth = [move(b, chain_step) for b in third]
    at = after(place, recv_o)
    near_rotated = [own_plus, near_plus, near_minus]
    keep_n, send_n = products(at, near_pairs, first + near + near_rotated, 3 * BLOCK, scale, "pairs_near")
    recv_n = move(send_n, x_near)
    at = after(place, recv_n)
    keep_b, send_b = products(at, all_pairs, second + rotated, 4 * BLOCK, scale, "pairs_2")
    recv_b = move(send_b, x_near)
    picks = [(0, 0, 2 * BLOCK), (1, 0, BLOCK), (1, BLOCK, BLOCK), (0, 2 * BLOCK, BLOCK), (1, 2 * BLOCK, BLOCK)]
    kept_a, send_a = sum_1([(after(keep_o, keep_b, third[0]), recv_o), (keep_n, recv_n)], picks)
    recv_a = move(send_a, x_far)
    kept_b, send_b = sum_1([(after(keep_b, kept_a, third[1]), recv_b)], straight)
    recv_b = move(send_b, x_far)
    at = after(place, kept_b)
    keep_c, send_c = products(at, all_pairs, third + rotated, 4 * BLOCK, scale, "pairs_3")
    recv_c = move(send_c, x_near)
    keep_ab, send_ab = sum_2(place, [(after(kept_a, keep_c), recv_a), (kept_b, recv_b)])
    recv_ab = move(send_ab, yhi_step)
    kept_c, send_c = sum_1([(after(keep_c, keep_ab, fourth[1]), recv_c)], straight)
    recv_c = move(send_c, x_far)
    at = after(place, kept_c)
    keep_d, send_d = products(at, last_pairs, fourth + [own_plus, near_plus], 2 * BLOCK, scale, "pairs_4")
    recv_d = move(send_d, x_near)
    outputs = [[(0, 768), (1536, 256)], [(768, 256), (1792, 256)], [(1024, 512)], [(2048, 512)]]
    own_ab, near_ab, ret_1, ret_2 = sum_y(after(keep_ab, keep_d), recv_ab, outputs)
    ret_1, ret_2 = move(ret_1, back(1)), move(ret_2, back(2))
    kept_d, send_d = sum_1([(after(keep_d, own_ab), recv_d)], [(0, 0, 2 * BLOCK)])
    recv_d = move(send_d, x_far)
    keep_cd, send_cd = sum_2(place, [(after(kept_c, kept_d), recv_c), (kept_d, recv_d)])
    recv_cd = move(send_cd, yhi_step)
    outputs = [[(0, 256), (1024, 256)], [(256, 256), (1280, 256)], [(512, 512)]]
    own_cd, near_all, ret_3 = sum_y(after(keep_cd, ret_1, ret_2), recv_cd, outputs, near_ab)
    ret_3 = move(ret_3, back(3))
    near_all = move(near_all, y_step)
    arrays = [own_ab, own_cd, near_all, ret_1, ret_2, ret_3]
    blocks = [[(0, 0), (1, 0), (0, 1), (2, 0)], [(3, 0), (4, 0)], [(1, 1), (2, 1), (3, 1), (4, 1)]]
    blocks += [[(-d, 0), (-d, 1)] for d in (1, 2, 3)]
    others = move(split(place, arrays), core_step)
    return finish(place, arrays, blocks, others)


def solution(mesh):
    torus = Mesh(mesh.devices.reshape(SIZES), AXES)
    placed = (P(None, ("yhi", "x", "c"), None, ("z", "ylo")), P())
    return jax.shard_map(
        body, mesh=torus, in_specs=placed, out_specs=P(None, AXES, None), check_vma=False
    )
```

```python
import math

import jax
import jax.numpy as jnp
import numpy as np
from jax import lax
from jax.experimental import pallas as pl
from jax.experimental.pallas import tpu as pltpu
from jax.sharding import Mesh
from jax.sharding import PartitionSpec as P

NFFT = 8192
LAGS = 2
LAG_STEP = 37
HALF = 64
BINS = 512
BLOCK = 256
DEPTH = 2048
AXES = ("z", "ylo", "yhi", "x", "c")
SIZES = (8, 2, 2, 4, 2)
F32 = jnp.float32
BF16 = jnp.bfloat16
MIB = 1 << 20


def dot_nt(a, b):
    return lax.dot_general(a, b, (((1,), (1,)), ((), ())), preferred_element_type=F32)


def params(mib, **kw):
    return pltpu.CompilerParams(vmem_limit_bytes=mib * MIB, **kw)


def cost(flops, bytes_accessed):
    return pl.CostEstimate(flops=flops, bytes_accessed=bytes_accessed, transcendentals=0)


def move(x, step):
    pairs = []
    for i, at in enumerate(np.ndindex(*SIZES)):
        to = tuple(int(v) % s for v, s in zip(step(*at), SIZES))
        pairs.append((i, int(np.ravel_multi_index(to, SIZES))))
    return lax.ppermute(x, AXES, pairs)


def sign(c):
    return 1 - 2 * c


def whiten_kernel(x_ref, o_ref):
    row = lax.broadcasted_iota(jnp.int32, (BINS, BINS), 0)
    col = lax.broadcasted_iota(jnp.int32, (BINS, BINS), 1)
    window = (jnp.abs(row - col) <= HALF).astype(F32).astype(BF16)
    pos = lax.broadcasted_iota(jnp.int32, (1, BINS), 1)
    count = jnp.minimum(pos + HALF, BINS - 1) - jnp.maximum(pos - HALF, 0) + 1
    inverse = 1.0 / count.astype(F32)
    for s in range(2):
        re = x_ref[0, s].astype(F32).T
        im = x_ref[1, s].astype(F32).T
        energy = re * re + im * im
        high = energy.astype(BF16)
        low = (energy - high.astype(F32)).astype(BF16)
        total = jnp.dot(high, window, preferred_element_type=F32)
        total += jnp.dot(low, window, preferred_element_type=F32)
        scale = lax.rsqrt(total * inverse + 1e-06)
        o_ref[:, s * BINS : (s + 1) * BINS] = (re * scale).astype(BF16)
        o_ref[:, (2 + s) * BINS : (3 + s) * BINS] = (im * scale).astype(BF16)


def whiten(spectra, half):
    return pl.pallas_call(
        whiten_kernel,
        grid=(1,),
        in_specs=[pl.BlockSpec((2, 2, BINS, 128), lambda i: (0, 0, 0, half))],
        out_specs=pl.BlockSpec((128, DEPTH), lambda i: (0, 0)),
        out_shape=jax.ShapeDtypeStruct((128, DEPTH), BF16),
        compiler_params=params(12),
        cost_estimate=cost(2 * 4 * 128 * 512 * 512, MIB),
        name="whiten",
    )(spectra)


def phases(bin_index):
    lag_samples = (jnp.arange(LAGS, dtype=jnp.int32) + 1) * LAG_STEP
    phase_turn = lag_samples[:, None] * bin_index[None, :] % NFFT
    phase_angle = 2.0 * math.pi / NFFT * phase_turn.astype(F32)
    cosine, sine = jnp.cos(phase_angle), jnp.sin(phase_angle)
    return jnp.concatenate([cosine, cosine], 1), jnp.concatenate([sine, sine], 1)


def rotate_kernel(a_ref, b_ref, cos_ref, sin_ref, plus_ref, minus_ref):
    half = DEPTH // 2
    for n, ref in enumerate((a_ref, b_ref)):

        @pl.loop(0, 8)
        def _(i):
            at = pl.ds(pl.multiple_of(i * 16, 16), 16)
            to = pl.ds(pl.multiple_of(n * 128 + i * 16, 16), 16)
            re = ref[at, :half].astype(F32)
            im = ref[at, half:].astype(F32)
            for m in range(LAGS):
                cosine, sine = cos_ref[m : m + 1, :], sin_ref[m : m + 1, :]
                rc, rs, ic, is_ = re * cosine, re * sine, im * cosine, im * sine
                plus_ref[m, to, :half] = (rc - is_).astype(BF16)
                plus_ref[m, to, half:] = (rs + ic).astype(BF16)
                minus_ref[m, to, :half] = (rc + is_).astype(BF16)
                minus_ref[m, to, half:] = (ic - rs).astype(BF16)


def rotations(chunks, cosine, sine):
    shape = jax.ShapeDtypeStruct((LAGS, BLOCK, DEPTH), BF16)
    return pl.pallas_call(
        rotate_kernel,
        out_shape=(shape, shape),
        compiler_params=params(12),
        cost_estimate=cost(2 * 8 * 256 * 2048, 6 * MIB),
        name="rotate",
    )(*chunks, cosine, sine)


def store_product(acc_ref, m, first, value, scale):
    n = value.shape[1]
    for h in range(2):
        for x in range(4):
            at = h * 128 + x * 32
            acc_ref[m, h, x, :, first : first + n] = (value[at : at + 32] * scale).astype(BF16)


def products(at, parts, chunks, wide, scale, name):
    count = len(chunks)

    def kernel(at_ref, *refs):
        ins, (keep_ref, send_ref), acc_ref = refs[:count], refs[count : count + 2], refs[count + 2]
        x, c = at_ref[3], at_ref[4]
        near, far = 1 + 2 * c, 3 - 2 * c
        for m in range(LAGS):
            for first, value in parts(m, ins):
                store_product(acc_ref, m, first, value, scale)
        slices = ((keep_ref, 0, x), (keep_ref, 1, x ^ far), (send_ref, 0, x ^ near), (send_ref, 1, x ^ 2))
        for out, k, which in slices:
            for m in range(LAGS):
                for h in range(2):
                    out[k, h, m] = acc_ref[m, h, which]

    shape = jax.ShapeDtypeStruct((2, 2, LAGS, 32, wide), BF16)
    whole = pl.BlockSpec(memory_space=pltpu.VMEM)
    return pl.pallas_call(
        kernel,
        in_specs=[pl.BlockSpec(memory_space=pltpu.SMEM)] + [whole] * count,
        out_specs=[whole] * 2,
        out_shape=(shape,) * 2,
        scratch_shapes=[pltpu.VMEM((LAGS, 2, 4, 32, wide), BF16)],
        compiler_params=params(14),
        cost_estimate=cost(2 * 2 * 256 * wide * DEPTH, 8 * MIB),
        name=name,
    )(at, *chunks)


def both(a_ref, b_ref):
    return jnp.concatenate([a_ref[...], b_ref[...]], 0)


def call(kernel, scalars, arrays, shapes, name):
    whole = pl.BlockSpec(memory_space=pltpu.VMEM)
    lead = [] if scalars is None else [scalars]
    return pl.pallas_call(
        kernel,
        in_specs=[pl.BlockSpec(memory_space=pltpu.SMEM)] * len(lead) + [whole] * len(arrays),
        out_specs=[whole] * len(shapes),
        out_shape=tuple(jax.ShapeDtypeStruct(s, t) for s, t in shapes),
        compiler_params=params(12),
        cost_estimate=cost(1000, 10 * MIB),
        name=name,
    )(*lead, *arrays)


def sum_1(groups, picks):
    total = sum(n for _, _, n in picks)

    def kernel(*refs):
        kept_ref, send_ref = refs[-2:]
        for h in range(2):
            for m in range(LAGS):
                to = 0
                for g, first, n in picks:
                    cols, out = slice(first, first + n), slice(to, to + n)
                    keep, recv = refs[2 * g], refs[2 * g + 1]
                    kept_ref[h, m, :, out] = keep[0, h, m, :, cols].astype(F32) + recv[0, h, m, :, cols].astype(F32)
                    value = keep[1, h, m, :, cols].astype(F32) + recv[1, h, m, :, cols].astype(F32)
                    send_ref[h, m, :, out] = value.astype(BF16)
                    to += n

    shape = (2, LAGS, 32, total)
    return call(kernel, None, [r for g in groups for r in g], [(shape, F32), (shape, BF16)], "sum_1")


def sum_2(place, groups):
    widths = [g[0].shape[3] for g in groups]

    def kernel(place_ref, *refs):
        keep_ref, send_ref = refs[-2:]
        mine, other = place_ref[2], 1 - place_ref[2]
        first = 0
        for k, n in enumerate(widths):
            kept, recv, cols = refs[2 * k], refs[2 * k + 1], slice(first, first + n)
            for m in range(LAGS):
                keep_ref[m, :, cols] = kept[mine, m] + recv[mine, m].astype(F32)
                send_ref[m, :, cols] = (kept[other, m] + recv[other, m].astype(F32)).astype(BF16)
            first += n

    shape = (LAGS, 32, sum(widths))
    return call(kernel, place, [r for g in groups for r in g], [(shape, F32), (shape, BF16)], "sum_2")


def sum_y(keep, recv, outputs, extra=None):
    arrays = [keep, recv] + ([] if extra is None else [extra])
    more = 0 if extra is None else extra.shape[2]

    def kernel(*refs):
        keep_ref, recv_ref, outs = refs[0], refs[1], refs[len(arrays) :]
        for m in range(LAGS):
            for k, (out, picks) in enumerate(zip(outs, outputs)):
                to = 0
                if k == 1 and more:
                    out[m, :, :more] = refs[2][m]
                    to = more
                for first, n in picks:
                    cols = slice(first, first + n)
                    out[m, :, to : to + n] = (keep_ref[m, :, cols] + recv_ref[m, :, cols].astype(F32)).astype(BF16)
                    to += n

    shapes = [((LAGS, 32, sum(n for _, n in p) + (more if k == 1 else 0)), BF16) for k, p in enumerate(outputs)]
    return call(kernel, None, arrays, shapes, "sum_y")


def split(place, arrays):
    total = sum(a.shape[2] for a in arrays)

    def kernel(place_ref, *refs):
        at = pl.ds(pl.multiple_of((1 - place_ref[4]) * 16, 16), 16)
        first = 0
        for ref in refs[:-1]:
            n = ref.shape[2]
            for m in range(LAGS):
                refs[-1][m, :, first : first + n] = ref[m, at, :]
            first += n

    return call(kernel, place, arrays, [((LAGS, 16, total), BF16)], "split")[0]


def finish(place, arrays, blocks, recv):
    def kernel(place_ref, *refs):
        ins, recv_ref, out = refs[:-2], refs[-2], refs[-1]
        z, y, c = place_ref[0], place_ref[1], place_ref[4]
        rows = pl.ds(pl.multiple_of(c * 16, 16), 16)

        def cols(block, way):
            dist, dy = block
            zz = lax.rem(z - way * dist + 16, 8)
            yy = y if dy == 0 else 1 - y
            return pl.ds(pl.multiple_of((zz * 2 + yy) * BLOCK, BLOCK), BLOCK)

        for m in range(LAGS):
            for ref, ids in zip(ins, blocks):
                for n, block in enumerate(ids):
                    out[m, :, cols(block, 1 - 2 * c)] = ref[m, rows, n * BLOCK : (n + 1) * BLOCK].astype(F32)
            for n, block in enumerate(sum(blocks, [])):
                out[m, :, cols(block, 2 * c - 1)] += recv_ref[m, :, n * BLOCK : (n + 1) * BLOCK].astype(F32)

    return call(kernel, place, list(arrays) + [recv], [((LAGS, 16, 4096), F32)], "finish")[0]


def chain_step(z, ylo, yhi, x, c):
    return z + sign(c), ylo, yhi, x, c


def y_step(z, ylo, yhi, x, c):
    return z, 1 - ylo, yhi, x, c


def yhi_step(z, ylo, yhi, x, c):
    return z, ylo, 1 - yhi, x, c


def core_step(z, ylo, yhi, x, c):
    return z, ylo, yhi, x, 1 - c


def x_near(z, ylo, yhi, x, c):
    return z, ylo, yhi, x ^ (1 + 2 * c), c


def x_far(z, ylo, yhi, x, c):
    return z, ylo, yhi, x ^ (3 - 2 * c), c


def back(d):
    return lambda z, ylo, yhi, x, c: (z - sign(c) * d, ylo, yhi, x, c)


def after(value, *others):
    return lax.optimization_barrier((value,) + others)[0]


def body(spectra, bin_index):
    scale = 1.0 / math.sqrt(32 * BINS)
    place = jnp.stack([lax.axis_index(a) for a in AXES]).astype(jnp.int32)

    spectra = after(spectra, place)
    own = [whiten(spectra, 0), whiten(spectra, 1)]
    near = [move(b, y_step) for b in own]
    first = [move(b, chain_step) for b in own]
    first[0] = after(first[0], near[0])
    second = [move(b, chain_step) for b in first]

    cosine, sine = phases(bin_index)
    own_plus, own_minus = rotations(own, cosine, sine)
    near_plus, near_minus = rotations(near, cosine, sine)

    def all_pairs(m, ins, at=0):
        b = both(ins[at], ins[at + 1])
        op, om, np_, nm = ins[-4:]
        yield 0, dot_nt(op[m], b)
        yield BLOCK, dot_nt(np_[m], b)
        yield 2 * BLOCK, dot_nt(b, om[m])
        yield 3 * BLOCK, dot_nt(b, nm[m])

    def own_pairs(m, ins):
        op, om = ins[-2:]
        b = both(ins[0], ins[1])
        yield 0, dot_nt(op[m], both(ins[2], ins[3]))
        yield BLOCK, dot_nt(op[m], b)
        yield 2 * BLOCK, dot_nt(b, om[m])

    def near_pairs(m, ins):
        op, np_, nm = ins[-3:]
        b = both(ins[0], ins[1])
        yield 0, dot_nt(op[m], both(ins[2], ins[3]))
        yield BLOCK, dot_nt(np_[m], b)
        yield 2 * BLOCK, dot_nt(b, nm[m])

    def last_pairs(m, ins):
        b = both(ins[0], ins[1])
        yield 0, dot_nt(ins[2][m], b)
        yield BLOCK, dot_nt(ins[3][m], b)

    rotated = [own_plus, own_minus, near_plus, near_minus]
    straight = [(0, 0, 4 * BLOCK)]

    keep_o, send_o = products(place, own_pairs, first + own + rotated[:2], 3 * BLOCK, scale, "pairs_own")
    recv_o = move(send_o, x_near)
    third = [move(b, chain_step) for b in (after(second[0], near[1], keep_o), second[1])]
    fourth = [move(b, chain_step) for b in third]
    at = after(place, recv_o)
    near_rotated = [own_plus, near_plus, near_minus]
    keep_n, send_n = products(at, near_pairs, first + near + near_rotated, 3 * BLOCK, scale, "pairs_near")
    recv_n = move(send_n, x_near)
    at = after(place, keep_n)
    keep_b, send_b = products(at, all_pairs, second + rotated, 4 * BLOCK, scale, "pairs_2")
    recv_b = move(send_b, x_near)
    picks = [(0, 0, 2 * BLOCK), (1, 0, BLOCK), (1, BLOCK, BLOCK), (0, 2 * BLOCK, BLOCK), (1, 2 * BLOCK, BLOCK)]
    kept_a, send_a = sum_1([(after(keep_o, keep_b, third[0]), recv_o), (keep_n, recv_n)], picks)
    recv_a = move(send_a, x_far)
    at = after(place, kept_a)
    keep_c, send_c = products(at, all_pairs, third + rotated, 4 * BLOCK, scale, "pairs_3")
    recv_c = move(send_c, x_near)
    kept_b, send_b = sum_1([(after(keep_b, keep_c, fourth[0]), recv_b)], straight)
    recv_b = move(send_b, x_far)
    at = after(place, kept_b)
    keep_d, send_d = products(at, last_pairs, fourth + [own_plus, near_plus], 2 * BLOCK, scale, "pairs_4")
    recv_d = move(send_d, x_near)
    kept_c, send_c = sum_1([(after(keep_c, keep_d), recv_c)], straight)
    recv_c = move(send_c, x_far)
    keep_ab, send_ab = sum_2(place, [(after(kept_a, kept_c), recv_a), (kept_b, recv_b)])
    recv_ab = move(send_ab, yhi_step)
    kept_d, send_d = sum_1([(after(keep_d, keep_ab), recv_d)], [(0, 0, 2 * BLOCK)])
    recv_d = move(send_d, x_far)
    keep_cd, send_cd = sum_2(place, [(kept_c, recv_c), (kept_d, recv_d)])
    recv_cd = move(send_cd, yhi_step)
    outputs = [[(0, 768), (1536, 256)], [(768, 256), (1792, 256)], [(1024, 512)], [(2048, 512)]]
    own_ab, near_ab, ret_1, ret_2 = sum_y(after(keep_ab, keep_cd), recv_ab, outputs)
    ret_1, ret_2 = move(ret_1, back(1)), move(ret_2, back(2))
    outputs = [[(0, 256), (1024, 256)], [(256, 256), (1280, 256)], [(512, 512)]]
    own_cd, near_all, ret_3 = sum_y(after(keep_cd, ret_1, ret_2), recv_cd, outputs, near_ab)
    ret_3 = move(ret_3, back(3))
    near_all = move(near_all, y_step)
    arrays = [own_ab, own_cd, near_all, ret_1, ret_2, ret_3]
    blocks = [[(0, 0), (1, 0), (0, 1), (2, 0)], [(3, 0), (4, 0)], [(1, 1), (2, 1), (3, 1), (4, 1)]]
    blocks += [[(-d, 0), (-d, 1)] for d in (1, 2, 3)]
    others = move(split(place, arrays), core_step)
    return finish(place, arrays, blocks, others)


def solution(mesh):
    torus = Mesh(mesh.devices.reshape(SIZES), AXES)
    placed = (P(None, ("yhi", "x", "c"), None, ("z", "ylo")), P())
    return jax.shard_map(
        body, mesh=torus, in_specs=placed, out_specs=P(None, AXES, None), check_vma=False
    )
```

```python
import math

import jax
import jax.numpy as jnp
import numpy as np
from jax import lax
from jax.experimental import pallas as pl
from jax.experimental.pallas import tpu as pltpu
from jax.sharding import Mesh
from jax.sharding import PartitionSpec as P

NFFT = 8192
LAGS = 2
LAG_STEP = 37
HALF = 64
BINS = 512
BLOCK = 256
DEPTH = 2048
AXES = ("z", "ylo", "yhi", "x", "c")
SIZES = (8, 2, 2, 4, 2)
F32 = jnp.float32
BF16 = jnp.bfloat16
MIB = 1 << 20


def dot_nt(a, b):
    return lax.dot_general(a, b, (((1,), (1,)), ((), ())), preferred_element_type=F32)


def params(mib, **kw):
    return pltpu.CompilerParams(vmem_limit_bytes=mib * MIB, **kw)


def cost(flops, bytes_accessed):
    return pl.CostEstimate(flops=flops, bytes_accessed=bytes_accessed, transcendentals=0)


def move(x, step):
    pairs = []
    for i, at in enumerate(np.ndindex(*SIZES)):
        to = tuple(int(v) % s for v, s in zip(step(*at), SIZES))
        pairs.append((i, int(np.ravel_multi_index(to, SIZES))))
    return lax.ppermute(x, AXES, pairs)


def sign(c):
    return 1 - 2 * c


def whiten_kernel(x_ref, o_ref):
    row = lax.broadcasted_iota(jnp.int32, (BINS, BINS), 0)
    col = lax.broadcasted_iota(jnp.int32, (BINS, BINS), 1)
    window = (jnp.abs(row - col) <= HALF).astype(F32).astype(BF16)
    pos = lax.broadcasted_iota(jnp.int32, (1, BINS), 1)
    count = jnp.minimum(pos + HALF, BINS - 1) - jnp.maximum(pos - HALF, 0) + 1
    inverse = 1.0 / count.astype(F32)
    for s in range(2):
        re = x_ref[0, s].astype(F32).T
        im = x_ref[1, s].astype(F32).T
        energy = re * re + im * im
        high = energy.astype(BF16)
        low = (energy - high.astype(F32)).astype(BF16)
        total = jnp.dot(high, window, preferred_element_type=F32)
        total += jnp.dot(low, window, preferred_element_type=F32)
        scale = lax.rsqrt(total * inverse + 1e-06)
        o_ref[:, s * BINS : (s + 1) * BINS] = (re * scale).astype(BF16)
        o_ref[:, (2 + s) * BINS : (3 + s) * BINS] = (im * scale).astype(BF16)


def whiten(spectra, half):
    return pl.pallas_call(
        whiten_kernel,
        grid=(1,),
        in_specs=[pl.BlockSpec((2, 2, BINS, 128), lambda i: (0, 0, 0, half))],
        out_specs=pl.BlockSpec((128, DEPTH), lambda i: (0, 0)),
        out_shape=jax.ShapeDtypeStruct((128, DEPTH), BF16),
        compiler_params=params(12),
        cost_estimate=cost(2 * 4 * 128 * 512 * 512, MIB),
        name="whiten",
    )(spectra)


def phases(bin_index):
    lag_samples = (jnp.arange(LAGS, dtype=jnp.int32) + 1) * LAG_STEP
    phase_turn = lag_samples[:, None] * bin_index[None, :] % NFFT
    phase_angle = 2.0 * math.pi / NFFT * phase_turn.astype(F32)
    cosine, sine = jnp.cos(phase_angle), jnp.sin(phase_angle)
    return jnp.concatenate([cosine, cosine], 1), jnp.concatenate([sine, sine], 1)


def rotate_kernel(a_ref, b_ref, cos_ref, sin_ref, plus_ref, minus_ref):
    half = DEPTH // 2
    for n, ref in enumerate((a_ref, b_ref)):

        @pl.loop(0, 8)
        def _(i):
            at = pl.ds(pl.multiple_of(i * 16, 16), 16)
            to = pl.ds(pl.multiple_of(n * 128 + i * 16, 16), 16)
            re = ref[at, :half].astype(F32)
            im = ref[at, half:].astype(F32)
            for m in range(LAGS):
                cosine, sine = cos_ref[m : m + 1, :], sin_ref[m : m + 1, :]
                rc, rs, ic, is_ = re * cosine, re * sine, im * cosine, im * sine
                plus_ref[m, to, :half] = (rc - is_).astype(BF16)
                plus_ref[m, to, half:] = (rs + ic).astype(BF16)
                minus_ref[m, to, :half] = (rc + is_).astype(BF16)
                minus_ref[m, to, half:] = (ic - rs).astype(BF16)


def rotations(chunks, cosine, sine):
    shape = jax.ShapeDtypeStruct((LAGS, BLOCK, DEPTH), BF16)
    return pl.pallas_call(
        rotate_kernel,
        out_shape=(shape, shape),
        compiler_params=params(12),
        cost_estimate=cost(2 * 8 * 256 * 2048, 6 * MIB),
        name="rotate",
    )(*chunks, cosine, sine)


def store_product(acc_ref, m, first, value, scale):
    n = value.shape[1]
    for h in range(2):
        for x in range(4):
            at = h * 128 + x * 32
            acc_ref[m, h, x, :, first : first + n] = (value[at : at + 32] * scale).astype(BF16)


def products(at, parts, chunks, wide, scale, name):
    count = len(chunks)

    def kernel(at_ref, *refs):
        ins, (keep_ref, send_ref), acc_ref = refs[:count], refs[count : count + 2], refs[count + 2]
        x, c = at_ref[3], at_ref[4]
        near, far = 1 + 2 * c, 3 - 2 * c
        for m in range(LAGS):
            for first, value in parts(m, ins):
                store_product(acc_ref, m, first, value, scale)
        slices = ((keep_ref, 0, x), (keep_ref, 1, x ^ far), (send_ref, 0, x ^ near), (send_ref, 1, x ^ 2))
        for out, k, which in slices:
            for m in range(LAGS):
                for h in range(2):
                    out[k, h, m] = acc_ref[m, h, which]

    shape = jax.ShapeDtypeStruct((2, 2, LAGS, 32, wide), BF16)
    whole = pl.BlockSpec(memory_space=pltpu.VMEM)
    return pl.pallas_call(
        kernel,
        in_specs=[pl.BlockSpec(memory_space=pltpu.SMEM)] + [whole] * count,
        out_specs=[whole] * 2,
        out_shape=(shape,) * 2,
        scratch_shapes=[pltpu.VMEM((LAGS, 2, 4, 32, wide), BF16)],
        compiler_params=params(14),
        cost_estimate=cost(2 * 2 * 256 * wide * DEPTH, 8 * MIB),
        name=name,
    )(at, *chunks)


def both(a_ref, b_ref):
    return jnp.concatenate([a_ref[...], b_ref[...]], 0)


def call(kernel, scalars, arrays, shapes, name):
    whole = pl.BlockSpec(memory_space=pltpu.VMEM)
    lead = [] if scalars is None else [scalars]
    return pl.pallas_call(
        kernel,
        in_specs=[pl.BlockSpec(memory_space=pltpu.SMEM)] * len(lead) + [whole] * len(arrays),
        out_specs=[whole] * len(shapes),
        out_shape=tuple(jax.ShapeDtypeStruct(s, t) for s, t in shapes),
        compiler_params=params(12),
        cost_estimate=cost(1000, 10 * MIB),
        name=name,
    )(*lead, *arrays)


def sum_1(groups, picks):
    total = sum(n for _, _, n in picks)

    def kernel(*refs):
        kept_ref, send_ref = refs[-2:]
        for h in range(2):
            for m in range(LAGS):
                to = 0
                for g, first, n in picks:
                    cols, out = slice(first, first + n), slice(to, to + n)
                    keep, recv = refs[2 * g], refs[2 * g + 1]
                    kept_ref[h, m, :, out] = keep[0, h, m, :, cols].astype(F32) + recv[0, h, m, :, cols].astype(F32)
                    value = keep[1, h, m, :, cols].astype(F32) + recv[1, h, m, :, cols].astype(F32)
                    send_ref[h, m, :, out] = value.astype(BF16)
                    to += n

    shape = (2, LAGS, 32, total)
    return call(kernel, None, [r for g in groups for r in g], [(shape, F32), (shape, BF16)], "sum_1")


def sum_2(place, groups):
    widths = [g[0].shape[3] for g in groups]

    def kernel(place_ref, *refs):
        keep_ref, send_ref = refs[-2:]
        mine, other = place_ref[2], 1 - place_ref[2]
        first = 0
        for k, n in enumerate(widths):
            kept, recv, cols = refs[2 * k], refs[2 * k + 1], slice(first, first + n)
            for m in range(LAGS):
                keep_ref[m, :, cols] = kept[mine, m] + recv[mine, m].astype(F32)
                send_ref[m, :, cols] = (kept[other, m] + recv[other, m].astype(F32)).astype(BF16)
            first += n

    shape = (LAGS, 32, sum(widths))
    return call(kernel, place, [r for g in groups for r in g], [(shape, F32), (shape, BF16)], "sum_2")


def sum_y(keep, recv, outputs, extra=None):
    arrays = [keep, recv] + ([] if extra is None else [extra])
    more = 0 if extra is None else extra.shape[2]

    def kernel(*refs):
        keep_ref, recv_ref, outs = refs[0], refs[1], refs[len(arrays) :]
        for m in range(LAGS):
            for k, (out, picks) in enumerate(zip(outs, outputs)):
                to = 0
                if k == 1 and more:
                    out[m, :, :more] = refs[2][m]
                    to = more
                for first, n in picks:
                    cols = slice(first, first + n)
                    out[m, :, to : to + n] = (keep_ref[m, :, cols] + recv_ref[m, :, cols].astype(F32)).astype(BF16)
                    to += n

    shapes = [((LAGS, 32, sum(n for _, n in p) + (more if k == 1 else 0)), BF16) for k, p in enumerate(outputs)]
    return call(kernel, None, arrays, shapes, "sum_y")


def split(place, arrays):
    total = sum(a.shape[2] for a in arrays)

    def kernel(place_ref, *refs):
        at = pl.ds(pl.multiple_of((1 - place_ref[4]) * 16, 16), 16)
        first = 0
        for ref in refs[:-1]:
            n = ref.shape[2]
            for m in range(LAGS):
                refs[-1][m, :, first : first + n] = ref[m, at, :]
            first += n

    return call(kernel, place, arrays, [((LAGS, 16, total), BF16)], "split")[0]


def finish(place, arrays, blocks, recv):
    def kernel(place_ref, *refs):
        ins, recv_ref, out = refs[:-2], refs[-2], refs[-1]
        z, y, c = place_ref[0], place_ref[1], place_ref[4]
        rows = pl.ds(pl.multiple_of(c * 16, 16), 16)

        def cols(block, way):
            dist, dy = block
            zz = lax.rem(z - way * dist + 16, 8)
            yy = y if dy == 0 else 1 - y
            return pl.ds(pl.multiple_of((zz * 2 + yy) * BLOCK, BLOCK), BLOCK)

        for m in range(LAGS):
            for ref, ids in zip(ins, blocks):
                for n, block in enumerate(ids):
                    out[m, :, cols(block, 1 - 2 * c)] = ref[m, rows, n * BLOCK : (n + 1) * BLOCK].astype(F32)
            for n, block in enumerate(sum(blocks, [])):
                out[m, :, cols(block, 2 * c - 1)] += recv_ref[m, :, n * BLOCK : (n + 1) * BLOCK].astype(F32)

    return call(kernel, place, list(arrays) + [recv], [((LAGS, 16, 4096), F32)], "finish")[0]


def chain_step(z, ylo, yhi, x, c):
    return z + sign(c), ylo, yhi, x, c


def y_step(z, ylo, yhi, x, c):
    return z, 1 - ylo, yhi, x, c


def yhi_step(z, ylo, yhi, x, c):
    return z, ylo, 1 - yhi, x, c


def core_step(z, ylo, yhi, x, c):
    return z, ylo, yhi, x, 1 - c


def x_near(z, ylo, yhi, x, c):
    return z, ylo, yhi, x ^ (1 + 2 * c), c


def x_far(z, ylo, yhi, x, c):
    return z, ylo, yhi, x ^ (3 - 2 * c), c


def back(d):
    return lambda z, ylo, yhi, x, c: (z - sign(c) * d, ylo, yhi, x, c)


def after(value, *others):
    return lax.optimization_barrier((value,) + others)[0]


def body(spectra, bin_index):
    scale = 1.0 / math.sqrt(32 * BINS)
    place = jnp.stack([lax.axis_index(a) for a in AXES]).astype(jnp.int32)

    spectra = after(spectra, place)
    own = [whiten(spectra, 0), whiten(spectra, 1)]
    near = [move(b, y_step) for b in own]
    first = [move(b, chain_step) for b in own]
    first[0] = after(first[0], near[0])
    second = [move(b, chain_step) for b in first]

    cosine, sine = phases(bin_index)
    own_plus, own_minus = rotations(own, cosine, sine)
    near_plus, near_minus = rotations(near, cosine, sine)

    def all_pairs(m, ins, at=0):
        b = both(ins[at], ins[at + 1])
        op, om, np_, nm = ins[-4:]
        yield 0, dot_nt(op[m], b)
        yield BLOCK, dot_nt(np_[m], b)
        yield 2 * BLOCK, dot_nt(b, om[m])
        yield 3 * BLOCK, dot_nt(b, nm[m])

    def own_pairs(m, ins):
        op, om = ins[-2:]
        b = both(ins[0], ins[1])
        yield 0, dot_nt(op[m], both(ins[2], ins[3]))
        yield BLOCK, dot_nt(op[m], b)
        yield 2 * BLOCK, dot_nt(b, om[m])

    def near_pairs(m, ins):
        op, np_, nm = ins[-3:]
        b = both(ins[0], ins[1])
        yield 0, dot_nt(op[m], both(ins[2], ins[3]))
        yield BLOCK, dot_nt(np_[m], b)
        yield 2 * BLOCK, dot_nt(b, nm[m])

    def last_pairs(m, ins):
        b = both(ins[0], ins[1])
        yield 0, dot_nt(ins[2][m], b)
        yield BLOCK, dot_nt(ins[3][m], b)

    rotated = [own_plus, own_minus, near_plus, near_minus]
    straight = [(0, 0, 4 * BLOCK)]

    keep_o, send_o = products(place, own_pairs, first + own + rotated[:2], 3 * BLOCK, scale, "pairs_own")
    recv_o = move(send_o, x_near)
    third = [move(after(second[0], near[1], keep_o), chain_step)]
    at = after(place, recv_o)
    near_rotated = [own_plus, near_plus, near_minus]
    keep_n, send_n = products(at, near_pairs, first + near + near_rotated, 3 * BLOCK, scale, "pairs_near")
    recv_n = move(send_n, x_near)
    third.append(move(after(second[1], keep_n), chain_step))
    at = after(place, keep_n)
    keep_b, send_b = products(at, all_pairs, second + rotated, 4 * BLOCK, scale, "pairs_2")
    recv_b = move(send_b, x_near)
    fourth = [move(b, chain_step) for b in (after(third[0], keep_b), third[1])]
    at = after(place, keep_b, recv_n)
    keep_c, send_c = products(at, all_pairs, third + rotated, 4 * BLOCK, scale, "pairs_3")
    recv_c = move(send_c, x_near)
    picks = [(0, 0, 2 * BLOCK), (1, 0, BLOCK), (1, BLOCK, BLOCK), (0, 2 * BLOCK, BLOCK), (1, 2 * BLOCK, BLOCK)]
    keep_o = after(keep_o, keep_c, fourth[0])
    kept_ab, send_ab = sum_1([(keep_o, recv_o), (keep_n, recv_n), (keep_b, recv_b)], picks + [(2, 0, 4 * BLOCK)])
    recv_ab = move(send_ab, x_far)
    kept_c, send_c = sum_1([(after(keep_c, kept_ab), recv_c)], straight)
    recv_c = move(send_c, x_far)
    at = after(place, kept_c)
    keep_d, send_d = products(at, last_pairs, fourth + [own_plus, near_plus], 2 * BLOCK, scale, "pairs_4")
    recv_d = move(send_d, x_near)
    keep_ab, send_ab = sum_2(place, [(after(kept_ab, keep_d), recv_ab)])
    recv_ab = move(send_ab, yhi_step)
    kept_d, send_d = sum_1([(after(keep_d, keep_ab), recv_d)], [(0, 0, 2 * BLOCK)])
    recv_d = move(send_d, x_far)
    keep_cd, send_cd = sum_2(place, [(kept_c, recv_c), (kept_d, recv_d)])
    recv_cd = move(send_cd, yhi_step)
    outputs = [[(0, 768), (1536, 256)], [(768, 256), (1792, 256)], [(1024, 512)], [(2048, 512)]]
    own_ab, near_ab, ret_1, ret_2 = sum_y(after(keep_ab, keep_cd), recv_ab, outputs)
    ret_1, ret_2 = move(ret_1, back(1)), move(ret_2, back(2))
    outputs = [[(0, 256), (1024, 256)], [(256, 256), (1280, 256)], [(512, 512)]]
    own_cd, near_all, ret_3 = sum_y(after(keep_cd, ret_1, ret_2), recv_cd, outputs, near_ab)
    ret_3 = move(ret_3, back(3))
    near_all = move(near_all, y_step)
    arrays = [own_ab, own_cd, near_all, ret_1, ret_2, ret_3]
    blocks = [[(0, 0), (1, 0), (0, 1), (2, 0)], [(3, 0), (4, 0)], [(1, 1), (2, 1), (3, 1), (4, 1)]]
    blocks += [[(-d, 0), (-d, 1)] for d in (1, 2, 3)]
    others = move(split(place, arrays), core_step)
    return finish(place, arrays, blocks, others)


def solution(mesh):
    torus = Mesh(mesh.devices.reshape(SIZES), AXES)
    placed = (P(None, ("yhi", "x", "c"), None, ("z", "ylo")), P())
    return jax.shard_map(
        body, mesh=torus, in_specs=placed, out_specs=P(None, AXES, None), check_vma=False
    )
```

```python
import math

import jax
import jax.numpy as jnp
import numpy as np
from jax import lax
from jax.experimental import pallas as pl
from jax.experimental.pallas import tpu as pltpu
from jax.sharding import Mesh
from jax.sharding import PartitionSpec as P

NFFT = 8192
LAGS = 2
LAG_STEP = 37
HALF = 64
BINS = 512
BLOCK = 256
DEPTH = 2048
AXES = ("z", "ylo", "yhi", "x", "c")
SIZES = (8, 2, 2, 4, 2)
F32 = jnp.float32
BF16 = jnp.bfloat16
MIB = 1 << 20


def dot_nt(a, b):
    return lax.dot_general(a, b, (((1,), (1,)), ((), ())), preferred_element_type=F32)


def params(mib, **kw):
    return pltpu.CompilerParams(vmem_limit_bytes=mib * MIB, **kw)


def cost(flops, bytes_accessed):
    return pl.CostEstimate(flops=flops, bytes_accessed=bytes_accessed, transcendentals=0)


def move(x, step):
    pairs = []
    for i, at in enumerate(np.ndindex(*SIZES)):
        to = tuple(int(v) % s for v, s in zip(step(*at), SIZES))
        pairs.append((i, int(np.ravel_multi_index(to, SIZES))))
    return lax.ppermute(x, AXES, pairs)


def sign(c):
    return 1 - 2 * c


def whiten_kernel(x_ref, o_ref):
    row = lax.broadcasted_iota(jnp.int32, (BINS, BINS), 0)
    col = lax.broadcasted_iota(jnp.int32, (BINS, BINS), 1)
    window = (jnp.abs(row - col) <= HALF).astype(F32).astype(BF16)
    pos = lax.broadcasted_iota(jnp.int32, (1, BINS), 1)
    count = jnp.minimum(pos + HALF, BINS - 1) - jnp.maximum(pos - HALF, 0) + 1
    inverse = 1.0 / count.astype(F32)
    for s in range(2):
        re = x_ref[0, s].astype(F32).T
        im = x_ref[1, s].astype(F32).T
        energy = re * re + im * im
        high = energy.astype(BF16)
        low = (energy - high.astype(F32)).astype(BF16)
        total = jnp.dot(high, window, preferred_element_type=F32)
        total += jnp.dot(low, window, preferred_element_type=F32)
        scale = lax.rsqrt(total * inverse + 1e-06)
        o_ref[:, s * BINS : (s + 1) * BINS] = (re * scale).astype(BF16)
        o_ref[:, (2 + s) * BINS : (3 + s) * BINS] = (im * scale).astype(BF16)


def whiten(spectra, half):
    return pl.pallas_call(
        whiten_kernel,
        grid=(1,),
        in_specs=[pl.BlockSpec((2, 2, BINS, 128), lambda i: (0, 0, 0, half))],
        out_specs=pl.BlockSpec((128, DEPTH), lambda i: (0, 0)),
        out_shape=jax.ShapeDtypeStruct((128, DEPTH), BF16),
        compiler_params=params(12),
        cost_estimate=cost(2 * 4 * 128 * 512 * 512, MIB),
        name="whiten",
    )(spectra)


def phases(bin_index):
    lag_samples = (jnp.arange(LAGS, dtype=jnp.int32) + 1) * LAG_STEP
    phase_turn = lag_samples[:, None] * bin_index[None, :] % NFFT
    phase_angle = 2.0 * math.pi / NFFT * phase_turn.astype(F32)
    cosine, sine = jnp.cos(phase_angle), jnp.sin(phase_angle)
    return jnp.concatenate([cosine, cosine], 1), jnp.concatenate([sine, sine], 1)


def rotate_kernel(a_ref, b_ref, cos_ref, sin_ref, plus_ref, minus_ref):
    half = DEPTH // 2
    for n, ref in enumerate((a_ref, b_ref)):

        @pl.loop(0, 8)
        def _(i):
            at = pl.ds(pl.multiple_of(i * 16, 16), 16)
            to = pl.ds(pl.multiple_of(n * 128 + i * 16, 16), 16)
            re = ref[at, :half].astype(F32)
            im = ref[at, half:].astype(F32)
            for m in range(LAGS):
                cosine, sine = cos_ref[m : m + 1, :], sin_ref[m : m + 1, :]
                rc, rs, ic, is_ = re * cosine, re * sine, im * cosine, im * sine
                plus_ref[m, to, :half] = (rc - is_).astype(BF16)
                plus_ref[m, to, half:] = (rs + ic).astype(BF16)
                minus_ref[m, to, :half] = (rc + is_).astype(BF16)
                minus_ref[m, to, half:] = (ic - rs).astype(BF16)


def rotations(chunks, cosine, sine):
    shape = jax.ShapeDtypeStruct((LAGS, BLOCK, DEPTH), BF16)
    return pl.pallas_call(
        rotate_kernel,
        out_shape=(shape, shape),
        compiler_params=params(12),
        cost_estimate=cost(2 * 8 * 256 * 2048, 6 * MIB),
        name="rotate",
    )(*chunks, cosine, sine)


def store_product(acc_ref, m, first, value, scale):
    n = value.shape[1]
    for h in range(2):
        for x in range(4):
            at = h * 128 + x * 32
            acc_ref[m, h, x, :, first : first + n] = (value[at : at + 32] * scale).astype(BF16)


def products(at, parts, chunks, wide, scale, name, yhi_first=False):
    count = len(chunks)

    def kernel(at_ref, *refs):
        ins, (keep_ref, send_ref), acc_ref = refs[:count], refs[count : count + 2], refs[count + 2]
        x, c = at_ref[3], at_ref[4]
        near, far = 1 + 2 * c, 3 - 2 * c
        for m in range(LAGS):
            for first, value in parts(m, ins):
                store_product(acc_ref, m, first, value, scale)
        if yhi_first:
            for out, h in ((keep_ref, at_ref[2]), (send_ref, 1 - at_ref[2])):
                for k, which in enumerate((x, x ^ far, x ^ near, x ^ 2)):
                    for m in range(LAGS):
                        out[k, m] = acc_ref[m, h, which]
            return
        slices = ((keep_ref, 0, x), (keep_ref, 1, x ^ far), (send_ref, 0, x ^ near), (send_ref, 1, x ^ 2))
        for out, k, which in slices:
            for m in range(LAGS):
                for h in range(2):
                    out[k, h, m] = acc_ref[m, h, which]

    shape = jax.ShapeDtypeStruct((4, LAGS, 32, wide) if yhi_first else (2, 2, LAGS, 32, wide), BF16)
    whole = pl.BlockSpec(memory_space=pltpu.VMEM)
    return pl.pallas_call(
        kernel,
        in_specs=[pl.BlockSpec(memory_space=pltpu.SMEM)] + [whole] * count,
        out_specs=[whole] * 2,
        out_shape=(shape,) * 2,
        scratch_shapes=[pltpu.VMEM((LAGS, 2, 4, 32, wide), BF16)],
        compiler_params=params(14),
        cost_estimate=cost(2 * 2 * 256 * wide * DEPTH, 8 * MIB),
        name=name,
    )(at, *chunks)


def both(a_ref, b_ref):
    return jnp.concatenate([a_ref[...], b_ref[...]], 0)


def call(kernel, scalars, arrays, shapes, name):
    whole = pl.BlockSpec(memory_space=pltpu.VMEM)
    lead = [] if scalars is None else [scalars]
    return pl.pallas_call(
        kernel,
        in_specs=[pl.BlockSpec(memory_space=pltpu.SMEM)] * len(lead) + [whole] * len(arrays),
        out_specs=[whole] * len(shapes),
        out_shape=tuple(jax.ShapeDtypeStruct(s, t) for s, t in shapes),
        compiler_params=params(12),
        cost_estimate=cost(1000, 10 * MIB),
        name=name,
    )(*lead, *arrays)


def sum_1(groups, picks):
    total = sum(n for _, _, n in picks)

    def kernel(*refs):
        kept_ref, send_ref = refs[-2:]
        for h in range(2):
            for m in range(LAGS):
                to = 0
                for g, first, n in picks:
                    cols, out = slice(first, first + n), slice(to, to + n)
                    keep, recv = refs[2 * g], refs[2 * g + 1]
                    kept_ref[h, m, :, out] = keep[0, h, m, :, cols].astype(F32) + recv[0, h, m, :, cols].astype(F32)
                    value = keep[1, h, m, :, cols].astype(F32) + recv[1, h, m, :, cols].astype(F32)
                    send_ref[h, m, :, out] = value.astype(BF16)
                    to += n

    shape = (2, LAGS, 32, total)
    return call(kernel, None, [r for g in groups for r in g], [(shape, F32), (shape, BF16)], "sum_1")


def sum_h(groups):
    widths = [g[0].shape[3] for g in groups]

    def kernel(*refs):
        keep_ref, send_ref = refs[-2:]
        for k in range(2):
            for m in range(LAGS):
                first = 0
                for g, n in enumerate(widths):
                    keep, recv, cols = refs[2 * g], refs[2 * g + 1], slice(first, first + n)
                    keep_ref[k, m, :, cols] = keep[k, m].astype(F32) + recv[k, m].astype(F32)
                    send_ref[k, m, :, cols] = (keep[2 + k, m].astype(F32) + recv[2 + k, m].astype(F32)).astype(BF16)
                    first += n

    shape = (2, LAGS, 32, sum(widths))
    return call(kernel, None, [r for g in groups for r in g], [(shape, F32), (shape, BF16)], "sum_h")


def sum_n(kept, recv):
    def kernel(kept_ref, recv_ref, keep_ref, send_ref):
        for m in range(LAGS):
            keep_ref[m] = kept_ref[0, m] + recv_ref[0, m].astype(F32)
            send_ref[m] = (kept_ref[1, m] + recv_ref[1, m].astype(F32)).astype(BF16)

    shape = kept.shape[1:]
    return call(kernel, None, [kept, recv], [(shape, F32), (shape, BF16)], "sum_n")


def sum_2(place, groups):
    widths = [g[0].shape[3] for g in groups]

    def kernel(place_ref, *refs):
        keep_ref, send_ref = refs[-2:]
        mine, other = place_ref[2], 1 - place_ref[2]
        first = 0
        for k, n in enumerate(widths):
            kept, recv, cols = refs[2 * k], refs[2 * k + 1], slice(first, first + n)
            for m in range(LAGS):
                keep_ref[m, :, cols] = kept[mine, m] + recv[mine, m].astype(F32)
                send_ref[m, :, cols] = (kept[other, m] + recv[other, m].astype(F32)).astype(BF16)
            first += n

    shape = (LAGS, 32, sum(widths))
    return call(kernel, place, [r for g in groups for r in g], [(shape, F32), (shape, BF16)], "sum_2")


def sum_y(keep, recv, outputs, extra=None):
    arrays = [keep, recv] + ([] if extra is None else [extra])
    more = 0 if extra is None else extra.shape[2]

    def kernel(*refs):
        keep_ref, recv_ref, outs = refs[0], refs[1], refs[len(arrays) :]
        for m in range(LAGS):
            for k, (out, picks) in enumerate(zip(outs, outputs)):
                to = 0
                if k == 1 and more:
                    out[m, :, :more] = refs[2][m]
                    to = more
                for first, n in picks:
                    cols = slice(first, first + n)
                    out[m, :, to : to + n] = (keep_ref[m, :, cols] + recv_ref[m, :, cols].astype(F32)).astype(BF16)
                    to += n

    shapes = [((LAGS, 32, sum(n for _, n in p) + (more if k == 1 else 0)), BF16) for k, p in enumerate(outputs)]
    return call(kernel, None, arrays, shapes, "sum_y")


def split(place, arrays):
    total = sum(a.shape[2] for a in arrays)

    def kernel(place_ref, *refs):
        at = pl.ds(pl.multiple_of((1 - place_ref[4]) * 16, 16), 16)
        first = 0
        for ref in refs[:-1]:
            n = ref.shape[2]
            for m in range(LAGS):
                refs[-1][m, :, first : first + n] = ref[m, at, :]
            first += n

    return call(kernel, place, arrays, [((LAGS, 16, total), BF16)], "split")[0]


def finish(place, arrays, blocks, recv):
    def kernel(place_ref, *refs):
        ins, recv_ref, out = refs[:-2], refs[-2], refs[-1]
        z, y, c = place_ref[0], place_ref[1], place_ref[4]
        rows = pl.ds(pl.multiple_of(c * 16, 16), 16)

        def cols(block, way):
            dist, dy = block
            zz = lax.rem(z - way * dist + 16, 8)
            yy = y if dy == 0 else 1 - y
            return pl.ds(pl.multiple_of((zz * 2 + yy) * BLOCK, BLOCK), BLOCK)

        for m in range(LAGS):
            for ref, ids in zip(ins, blocks):
                for n, block in enumerate(ids):
                    out[m, :, cols(block, 1 - 2 * c)] = ref[m, rows, n * BLOCK : (n + 1) * BLOCK].astype(F32)
            for n, block in enumerate(sum(blocks, [])):
                out[m, :, cols(block, 2 * c - 1)] += recv_ref[m, :, n * BLOCK : (n + 1) * BLOCK].astype(F32)

    return call(kernel, place, list(arrays) + [recv], [((LAGS, 16, 4096), F32)], "finish")[0]


def chain_step(z, ylo, yhi, x, c):
    return z + sign(c), ylo, yhi, x, c


def y_step(z, ylo, yhi, x, c):
    return z, 1 - ylo, yhi, x, c


def yhi_step(z, ylo, yhi, x, c):
    return z, ylo, 1 - yhi, x, c


def core_step(z, ylo, yhi, x, c):
    return z, ylo, yhi, x, 1 - c


def x_near(z, ylo, yhi, x, c):
    return z, ylo, yhi, x ^ (1 + 2 * c), c


def x_far(z, ylo, yhi, x, c):
    return z, ylo, yhi, x ^ (3 - 2 * c), c


def back(d):
    return lambda z, ylo, yhi, x, c: (z - sign(c) * d, ylo, yhi, x, c)


def after(value, *others):
    return lax.optimization_barrier((value,) + others)[0]


def body(spectra, bin_index):
    scale = 1.0 / math.sqrt(32 * BINS)
    place = jnp.stack([lax.axis_index(a) for a in AXES]).astype(jnp.int32)

    spectra = after(spectra, place)
    own = [whiten(spectra, 0), whiten(spectra, 1)]
    near = [move(b, y_step) for b in own]
    first = [move(b, chain_step) for b in own]
    first[0] = after(first[0], near[0])
    second = [move(b, chain_step) for b in first]

    cosine, sine = phases(bin_index)
    own_plus, own_minus = rotations(own, cosine, sine)
    near_plus, near_minus = rotations(near, cosine, sine)

    def all_pairs(m, ins, at=0):
        b = both(ins[at], ins[at + 1])
        op, om, np_, nm = ins[-4:]
        yield 0, dot_nt(op[m], b)
        yield BLOCK, dot_nt(np_[m], b)
        yield 2 * BLOCK, dot_nt(b, om[m])
        yield 3 * BLOCK, dot_nt(b, nm[m])

    def own_pairs(m, ins):
        op, om = ins[-2:]
        b = both(ins[0], ins[1])
        yield 0, dot_nt(op[m], both(ins[2], ins[3]))
        yield BLOCK, dot_nt(op[m], b)
        yield 2 * BLOCK, dot_nt(b, om[m])

    def near_pairs(m, ins):
        op, np_, nm = ins[-3:]
        b = both(ins[0], ins[1])
        yield 0, dot_nt(op[m], both(ins[2], ins[3]))
        yield BLOCK, dot_nt(np_[m], b)
        yield 2 * BLOCK, dot_nt(b, nm[m])

    def last_pairs(m, ins):
        b = both(ins[0], ins[1])
        yield 0, dot_nt(ins[2][m], b)
        yield BLOCK, dot_nt(ins[3][m], b)

    rotated = [own_plus, own_minus, near_plus, near_minus]
    straight = [(0, 0, 4 * BLOCK)]

    keep_o, send_o = products(place, own_pairs, first + own + rotated[:2], 3 * BLOCK, scale, "pairs_own")
    recv_o = move(send_o, x_near)
    third = [move(after(second[0], near[1], keep_o), chain_step)]
    at = after(place, recv_o)
    near_rotated = [own_plus, near_plus, near_minus]
    keep_n, send_n = products(at, near_pairs, first + near + near_rotated, 3 * BLOCK, scale, "pairs_near")
    recv_n = move(send_n, x_near)
    third.append(move(after(second[1], keep_n), chain_step))
    at = after(place, keep_n)
    keep_b, send_b = products(at, all_pairs, second + rotated, 4 * BLOCK, scale, "pairs_2")
    recv_b = move(send_b, x_near)
    fourth = [move(b, chain_step) for b in (after(third[0], keep_b), third[1])]
    at = after(place, keep_b, recv_n)
    keep_c, send_c = products(at, all_pairs, third + rotated, 4 * BLOCK, scale, "pairs_3", True)
    recv_c = move(send_c, yhi_step)
    picks = [(0, 0, 2 * BLOCK), (1, 0, BLOCK), (1, BLOCK, BLOCK), (0, 2 * BLOCK, BLOCK), (1, 2 * BLOCK, BLOCK)]
    keep_o = after(keep_o, keep_c, fourth[0])
    kept_ab, send_ab = sum_1([(keep_o, recv_o), (keep_n, recv_n), (keep_b, recv_b)], picks + [(2, 0, 4 * BLOCK)])
    recv_ab = move(send_ab, x_far)
    at = after(place, kept_ab)
    keep_d, send_d = products(at, last_pairs, fourth + [own_plus, near_plus], 2 * BLOCK, scale, "pairs_4", True)
    recv_d = move(send_d, yhi_step)
    keep_ab, send_ab = sum_2(place, [(after(kept_ab, keep_d), recv_ab)])
    recv_ab = move(send_ab, yhi_step)
    kept_cd, send_cd = sum_h([(after(keep_c, keep_ab), recv_c), (keep_d, recv_d)])
    recv_cd = move(send_cd, x_near)
    keep_cd, send_cd = sum_n(kept_cd, recv_cd)
    recv_cd = move(send_cd, x_far)
    outputs = [[(0, 768), (1536, 256)], [(768, 256), (1792, 256)], [(1024, 512)], [(2048, 512)]]
    own_ab, near_ab, ret_1, ret_2 = sum_y(after(keep_ab, keep_cd), recv_ab, outputs)
    ret_1, ret_2 = move(ret_1, back(1)), move(ret_2, back(2))
    outputs = [[(0, 256), (1024, 256)], [(256, 256), (1280, 256)], [(512, 512)]]
    own_cd, near_all, ret_3 = sum_y(after(keep_cd, ret_1), recv_cd, outputs, near_ab)
    ret_3 = move(ret_3, back(3))
    near_all = move(near_all, y_step)
    arrays = [own_ab, own_cd, near_all, ret_1, ret_2, ret_3]
    blocks = [[(0, 0), (1, 0), (0, 1), (2, 0)], [(3, 0), (4, 0)], [(1, 1), (2, 1), (3, 1), (4, 1)]]
    blocks += [[(-d, 0), (-d, 1)] for d in (1, 2, 3)]
    others = move(split(place, arrays), core_step)
    return finish(place, arrays, blocks, others)


def solution(mesh):
    torus = Mesh(mesh.devices.reshape(SIZES), AXES)
    placed = (P(None, ("yhi", "x", "c"), None, ("z", "ylo")), P())
    return jax.shard_map(
        body, mesh=torus, in_specs=placed, out_specs=P(None, AXES, None), check_vma=False
    )
```

```python
import math

import jax
import jax.numpy as jnp
import numpy as np
from jax import lax
from jax.experimental import pallas as pl
from jax.experimental.pallas import tpu as pltpu
from jax.sharding import Mesh
from jax.sharding import PartitionSpec as P

NFFT = 8192
LAGS = 2
LAG_STEP = 37
HALF = 64
BINS = 512
BLOCK = 256
DEPTH = 2048
AXES = ("z", "ylo", "yhi", "x", "c")
SIZES = (8, 2, 2, 4, 2)
F32 = jnp.float32
BF16 = jnp.bfloat16
MIB = 1 << 20


def dot_nt(a, b):
    return lax.dot_general(a, b, (((1,), (1,)), ((), ())), preferred_element_type=F32)


def params(mib, **kw):
    return pltpu.CompilerParams(vmem_limit_bytes=mib * MIB, **kw)


def cost(flops, bytes_accessed):
    return pl.CostEstimate(flops=flops, bytes_accessed=bytes_accessed, transcendentals=0)


def move(x, step):
    pairs = []
    for i, at in enumerate(np.ndindex(*SIZES)):
        to = tuple(int(v) % s for v, s in zip(step(*at), SIZES))
        pairs.append((i, int(np.ravel_multi_index(to, SIZES))))
    return lax.ppermute(x, AXES, pairs)


def sign(c):
    return 1 - 2 * c


def whiten_kernel(x_ref, o_ref):
    row = lax.broadcasted_iota(jnp.int32, (BINS, BINS), 0)
    col = lax.broadcasted_iota(jnp.int32, (BINS, BINS), 1)
    window = (jnp.abs(row - col) <= HALF).astype(F32).astype(BF16)
    pos = lax.broadcasted_iota(jnp.int32, (1, BINS), 1)
    count = jnp.minimum(pos + HALF, BINS - 1) - jnp.maximum(pos - HALF, 0) + 1
    inverse = 1.0 / count.astype(F32)
    for s in range(2):
        re = x_ref[0, s].astype(F32).T
        im = x_ref[1, s].astype(F32).T
        energy = re * re + im * im
        high = energy.astype(BF16)
        low = (energy - high.astype(F32)).astype(BF16)
        total = jnp.dot(high, window, preferred_element_type=F32)
        total += jnp.dot(low, window, preferred_element_type=F32)
        scale = lax.rsqrt(total * inverse + 1e-06)
        o_ref[:, s * BINS : (s + 1) * BINS] = (re * scale).astype(BF16)
        o_ref[:, (2 + s) * BINS : (3 + s) * BINS] = (im * scale).astype(BF16)


def whiten(spectra, half):
    return pl.pallas_call(
        whiten_kernel,
        grid=(1,),
        in_specs=[pl.BlockSpec((2, 2, BINS, 128), lambda i: (0, 0, 0, half))],
        out_specs=pl.BlockSpec((128, DEPTH), lambda i: (0, 0)),
        out_shape=jax.ShapeDtypeStruct((128, DEPTH), BF16),
        compiler_params=params(12),
        cost_estimate=cost(2 * 4 * 128 * 512 * 512, MIB),
        name="whiten",
    )(spectra)


def phases(bin_index):
    lag_samples = (jnp.arange(LAGS, dtype=jnp.int32) + 1) * LAG_STEP
    phase_turn = lag_samples[:, None] * bin_index[None, :] % NFFT
    phase_angle = 2.0 * math.pi / NFFT * phase_turn.astype(F32)
    cosine, sine = jnp.cos(phase_angle), jnp.sin(phase_angle)
    return jnp.concatenate([cosine, cosine], 1), jnp.concatenate([sine, sine], 1)


def rotate_kernel(a_ref, b_ref, cos_ref, sin_ref, plus_ref, minus_ref):
    half = DEPTH // 2
    for n, ref in enumerate((a_ref, b_ref)):

        @pl.loop(0, 8)
        def _(i):
            at = pl.ds(pl.multiple_of(i * 16, 16), 16)
            to = pl.ds(pl.multiple_of(n * 128 + i * 16, 16), 16)
            re = ref[at, :half].astype(F32)
            im = ref[at, half:].astype(F32)
            for m in range(LAGS):
                cosine, sine = cos_ref[m : m + 1, :], sin_ref[m : m + 1, :]
                rc, rs, ic, is_ = re * cosine, re * sine, im * cosine, im * sine
                plus_ref[m, to, :half] = (rc - is_).astype(BF16)
                plus_ref[m, to, half:] = (rs + ic).astype(BF16)
                minus_ref[m, to, :half] = (rc + is_).astype(BF16)
                minus_ref[m, to, half:] = (ic - rs).astype(BF16)


def rotations(chunks, cosine, sine):
    shape = jax.ShapeDtypeStruct((LAGS, BLOCK, DEPTH), BF16)
    return pl.pallas_call(
        rotate_kernel,
        out_shape=(shape, shape),
        compiler_params=params(12),
        cost_estimate=cost(2 * 8 * 256 * 2048, 6 * MIB),
        name="rotate",
    )(*chunks, cosine, sine)


def store_product(acc_ref, m, first, value, scale):
    n = value.shape[1]
    for h in range(2):
        for x in range(4):
            at = h * 128 + x * 32
            acc_ref[m, h, x, :, first : first + n] = (value[at : at + 32] * scale).astype(BF16)


def products(at, parts, chunks, wide, scale, name, stage="near"):
    count = len(chunks)

    def kernel(at_ref, *refs):
        ins, (keep_ref, send_ref), acc_ref = refs[:count], refs[count : count + 2], refs[count + 2]
        x, c = at_ref[3], at_ref[4]
        near, far = 1 + 2 * c, 3 - 2 * c
        for m in range(LAGS):
            for first, value in parts(m, ins):
                store_product(acc_ref, m, first, value, scale)
        if stage == "yhi":
            for out, h in ((keep_ref, at_ref[2]), (send_ref, 1 - at_ref[2])):
                for k, which in enumerate((x, x ^ far, x ^ near, x ^ 2)):
                    for m in range(LAGS):
                        out[k, m] = acc_ref[m, h, which]
            return
        if stage == "far":
            near, far = far, near
        slices = ((keep_ref, 0, x), (keep_ref, 1, x ^ far), (send_ref, 0, x ^ near), (send_ref, 1, x ^ 2))
        for out, k, which in slices:
            for m in range(LAGS):
                for h in range(2):
                    out[k, h, m] = acc_ref[m, h, which]

    shape = jax.ShapeDtypeStruct((4, LAGS, 32, wide) if stage == "yhi" else (2, 2, LAGS, 32, wide), BF16)
    whole = pl.BlockSpec(memory_space=pltpu.VMEM)
    return pl.pallas_call(
        kernel,
        in_specs=[pl.BlockSpec(memory_space=pltpu.SMEM)] + [whole] * count,
        out_specs=[whole] * 2,
        out_shape=(shape,) * 2,
        scratch_shapes=[pltpu.VMEM((LAGS, 2, 4, 32, wide), BF16)],
        compiler_params=params(14),
        cost_estimate=cost(2 * 2 * 256 * wide * DEPTH, 8 * MIB),
        name=name,
    )(at, *chunks)


def both(a_ref, b_ref):
    return jnp.concatenate([a_ref[...], b_ref[...]], 0)


def call(kernel, scalars, arrays, shapes, name):
    whole = pl.BlockSpec(memory_space=pltpu.VMEM)
    lead = [] if scalars is None else [scalars]
    return pl.pallas_call(
        kernel,
        in_specs=[pl.BlockSpec(memory_space=pltpu.SMEM)] * len(lead) + [whole] * len(arrays),
        out_specs=[whole] * len(shapes),
        out_shape=tuple(jax.ShapeDtypeStruct(s, t) for s, t in shapes),
        compiler_params=params(12),
        cost_estimate=cost(1000, 10 * MIB),
        name=name,
    )(*lead, *arrays)


def sum_1(groups, picks):
    total = sum(n for _, _, n in picks)

    def kernel(*refs):
        kept_ref, send_ref = refs[-2:]
        for h in range(2):
            for m in range(LAGS):
                to = 0
                for g, first, n in picks:
                    cols, out = slice(first, first + n), slice(to, to + n)
                    keep, recv = refs[2 * g], refs[2 * g + 1]
                    kept_ref[h, m, :, out] = keep[0, h, m, :, cols].astype(F32) + recv[0, h, m, :, cols].astype(F32)
                    value = keep[1, h, m, :, cols].astype(F32) + recv[1, h, m, :, cols].astype(F32)
                    send_ref[h, m, :, out] = value.astype(BF16)
                    to += n

    shape = (2, LAGS, 32, total)
    return call(kernel, None, [r for g in groups for r in g], [(shape, F32), (shape, BF16)], "sum_1")


def sum_h(keep_c, recv_c, keep_d, recv_d):
    nc, nd = keep_c.shape[3], keep_d.shape[4]

    def kernel(c_ref, rc_ref, d_ref, rd_ref, keep_ref, send_ref):
        for k in range(2):
            for m in range(LAGS):
                keep_ref[k, m, :, :nc] = c_ref[k, m].astype(F32) + rc_ref[k, m].astype(F32)
                send_ref[k, m, :, :nc] = (c_ref[2 + k, m].astype(F32) + rc_ref[2 + k, m].astype(F32)).astype(BF16)
                keep_ref[k, m, :, nc:] = d_ref[0, k, m].astype(F32) + rd_ref[0, k, m].astype(F32)
                send_ref[k, m, :, nc:] = (d_ref[1, k, m].astype(F32) + rd_ref[1, k, m].astype(F32)).astype(BF16)

    shape = (2, LAGS, 32, nc + nd)
    return call(kernel, None, [keep_c, recv_c, keep_d, recv_d], [(shape, F32), (shape, BF16)], "sum_h")


def sum_n(place, kept, recv, nc):
    n = kept.shape[3]

    def kernel(place_ref, kept_ref, recv_ref, keep_ref, send_c_ref, send_d_ref):
        mine, other = place_ref[2], 1 - place_ref[2]
        c, d = slice(0, nc), slice(nc, n)
        for m in range(LAGS):
            keep_ref[m, :, c] = kept_ref[0, m, :, c] + recv_ref[0, m, :, c].astype(F32)
            send_c_ref[m] = (kept_ref[1, m, :, c] + recv_ref[1, m, :, c].astype(F32)).astype(BF16)
            keep_ref[m, :, d] = kept_ref[mine, m, :, d] + recv_ref[mine, m, :, d].astype(F32)
            send_d_ref[m] = (kept_ref[other, m, :, d] + recv_ref[other, m, :, d].astype(F32)).astype(BF16)

    shapes = [((LAGS, 32, n), F32), ((LAGS, 32, nc), BF16), ((LAGS, 32, n - nc), BF16)]
    return call(kernel, place, [kept, recv], shapes, "sum_n")


def sum_2(place, groups):
    widths = [g[0].shape[3] for g in groups]

    def kernel(place_ref, *refs):
        keep_ref, send_ref = refs[-2:]
        mine, other = place_ref[2], 1 - place_ref[2]
        first = 0
        for k, n in enumerate(widths):
            kept, recv, cols = refs[2 * k], refs[2 * k + 1], slice(first, first + n)
            for m in range(LAGS):
                keep_ref[m, :, cols] = kept[mine, m] + recv[mine, m].astype(F32)
                send_ref[m, :, cols] = (kept[other, m] + recv[other, m].astype(F32)).astype(BF16)
            first += n

    shape = (LAGS, 32, sum(widths))
    return call(kernel, place, [r for g in groups for r in g], [(shape, F32), (shape, BF16)], "sum_2")


def sum_y(keep, recvs, outputs, extra=None):
    arrays = [keep] + list(recvs) + ([] if extra is None else [extra])
    more = 0 if extra is None else extra.shape[2]
    split_at = recvs[0].shape[2]

    def kernel(*refs):
        keep_ref, outs = refs[0], refs[len(arrays) :]
        for m in range(LAGS):
            for k, (out, picks) in enumerate(zip(outs, outputs)):
                to = 0
                if k == 1 and more:
                    out[m, :, :more] = refs[len(arrays) - 1][m]
                    to = more
                for first, n in picks:
                    recv_ref, at = (refs[1], first) if first < split_at else (refs[2], first - split_at)
                    value = keep_ref[m, :, first : first + n] + recv_ref[m, :, at : at + n].astype(F32)
                    out[m, :, to : to + n] = value.astype(BF16)
                    to += n

    shapes = [((LAGS, 32, sum(n for _, n in p) + (more if k == 1 else 0)), BF16) for k, p in enumerate(outputs)]
    return call(kernel, None, arrays, shapes, "sum_y")


def split(place, arrays):
    total = sum(a.shape[2] for a in arrays)

    def kernel(place_ref, *refs):
        at = pl.ds(pl.multiple_of((1 - place_ref[4]) * 16, 16), 16)
        first = 0
        for ref in refs[:-1]:
            n = ref.shape[2]
            for m in range(LAGS):
                refs[-1][m, :, first : first + n] = ref[m, at, :]
            first += n

    return call(kernel, place, arrays, [((LAGS, 16, total), BF16)], "split")[0]


def finish(place, arrays, blocks, recv):
    def kernel(place_ref, *refs):
        ins, recv_ref, out = refs[:-2], refs[-2], refs[-1]
        z, y, c = place_ref[0], place_ref[1], place_ref[4]
        rows = pl.ds(pl.multiple_of(c * 16, 16), 16)

        def cols(block, way):
            dist, dy = block
            zz = lax.rem(z - way * dist + 16, 8)
            yy = y if dy == 0 else 1 - y
            return pl.ds(pl.multiple_of((zz * 2 + yy) * BLOCK, BLOCK), BLOCK)

        for m in range(LAGS):
            for ref, ids in zip(ins, blocks):
                for n, block in enumerate(ids):
                    out[m, :, cols(block, 1 - 2 * c)] = ref[m, rows, n * BLOCK : (n + 1) * BLOCK].astype(F32)
            for n, block in enumerate(sum(blocks, [])):
                out[m, :, cols(block, 2 * c - 1)] += recv_ref[m, :, n * BLOCK : (n + 1) * BLOCK].astype(F32)

    return call(kernel, place, list(arrays) + [recv], [((LAGS, 16, 4096), F32)], "finish")[0]


def chain_step(z, ylo, yhi, x, c):
    return z + sign(c), ylo, yhi, x, c


def y_step(z, ylo, yhi, x, c):
    return z, 1 - ylo, yhi, x, c


def yhi_step(z, ylo, yhi, x, c):
    return z, ylo, 1 - yhi, x, c


def core_step(z, ylo, yhi, x, c):
    return z, ylo, yhi, x, 1 - c


def x_near(z, ylo, yhi, x, c):
    return z, ylo, yhi, x ^ (1 + 2 * c), c


def x_far(z, ylo, yhi, x, c):
    return z, ylo, yhi, x ^ (3 - 2 * c), c


def back(d):
    return lambda z, ylo, yhi, x, c: (z - sign(c) * d, ylo, yhi, x, c)


def after(value, *others):
    return lax.optimization_barrier((value,) + others)[0]


def body(spectra, bin_index):
    scale = 1.0 / math.sqrt(32 * BINS)
    place = jnp.stack([lax.axis_index(a) for a in AXES]).astype(jnp.int32)

    spectra = after(spectra, place)
    own = [whiten(spectra, 0), whiten(spectra, 1)]
    near = [move(b, y_step) for b in own]
    first = [move(b, chain_step) for b in own]
    first[0] = after(first[0], near[0])
    second = [move(b, chain_step) for b in first]

    cosine, sine = phases(bin_index)
    own_plus, own_minus = rotations(own, cosine, sine)
    near_plus, near_minus = rotations(near, cosine, sine)

    def all_pairs(m, ins, at=0):
        b = both(ins[at], ins[at + 1])
        op, om, np_, nm = ins[-4:]
        yield 0, dot_nt(op[m], b)
        yield BLOCK, dot_nt(np_[m], b)
        yield 2 * BLOCK, dot_nt(b, om[m])
        yield 3 * BLOCK, dot_nt(b, nm[m])

    def own_pairs(m, ins):
        op, om = ins[-2:]
        b = both(ins[0], ins[1])
        yield 0, dot_nt(op[m], both(ins[2], ins[3]))
        yield BLOCK, dot_nt(op[m], b)
        yield 2 * BLOCK, dot_nt(b, om[m])

    def near_pairs(m, ins):
        op, np_, nm = ins[-3:]
        b = both(ins[0], ins[1])
        yield 0, dot_nt(op[m], both(ins[2], ins[3]))
        yield BLOCK, dot_nt(np_[m], b)
        yield 2 * BLOCK, dot_nt(b, nm[m])

    def last_pairs(m, ins):
        b = both(ins[0], ins[1])
        yield 0, dot_nt(ins[2][m], b)
        yield BLOCK, dot_nt(ins[3][m], b)

    rotated = [own_plus, own_minus, near_plus, near_minus]
    straight = [(0, 0, 4 * BLOCK)]

    keep_o, send_o = products(place, own_pairs, first + own + rotated[:2], 3 * BLOCK, scale, "pairs_own")
    recv_o = move(send_o, x_near)
    third = [move(after(second[0], near[1], keep_o), chain_step)]
    at = after(place, recv_o)
    near_rotated = [own_plus, near_plus, near_minus]
    keep_n, send_n = products(at, near_pairs, first + near + near_rotated, 3 * BLOCK, scale, "pairs_near")
    recv_n = move(send_n, x_near)
    third.append(move(after(second[1], keep_n), chain_step))
    at = after(place, keep_n)
    keep_b, send_b = products(at, all_pairs, second + rotated, 4 * BLOCK, scale, "pairs_2")
    recv_b = move(send_b, x_near)
    fourth = [move(b, chain_step) for b in (after(third[0], keep_b), third[1])]
    at = after(place, keep_b, recv_n)
    keep_c, send_c = products(at, all_pairs, third + rotated, 4 * BLOCK, scale, "pairs_3", "yhi")
    recv_c = move(send_c, yhi_step)
    picks = [(0, 0, 2 * BLOCK), (1, 0, BLOCK), (1, BLOCK, BLOCK), (0, 2 * BLOCK, BLOCK), (1, 2 * BLOCK, BLOCK)]
    keep_o = after(keep_o, keep_c, fourth[0])
    kept_ab, send_ab = sum_1([(keep_o, recv_o), (keep_n, recv_n), (keep_b, recv_b)], picks + [(2, 0, 4 * BLOCK)])
    recv_ab = move(send_ab, x_far)
    at = after(place, kept_ab)
    keep_d, send_d = products(at, last_pairs, fourth + [own_plus, near_plus], 2 * BLOCK, scale, "pairs_4", "far")
    recv_d = move(send_d, x_far)
    keep_ab, send_ab = sum_2(place, [(after(kept_ab, keep_d), recv_ab)])
    recv_ab = move(send_ab, yhi_step)
    kept_cd, send_cd = sum_h(after(keep_c, keep_ab), recv_c, keep_d, recv_d)
    recv_cd = move(send_cd, x_near)
    keep_cd, send_c, send_d = sum_n(place, kept_cd, recv_cd, 4 * BLOCK)
    recv_cd = [move(send_c, x_far), move(send_d, yhi_step)]
    outputs = [[(0, 768), (1536, 256)], [(768, 256), (1792, 256)], [(1024, 512)], [(2048, 512)]]
    own_ab, near_ab, ret_1, ret_2 = sum_y(after(keep_ab, keep_cd), [recv_ab], outputs)
    ret_1, ret_2 = move(ret_1, back(1)), move(ret_2, back(2))
    outputs = [[(0, 256), (1024, 256)], [(256, 256), (1280, 256)], [(512, 512)]]
    own_cd, near_all, ret_3 = sum_y(after(keep_cd, ret_1, ret_2), recv_cd, outputs, near_ab)
    ret_3 = move(ret_3, back(3))
    near_all = move(near_all, y_step)
    arrays = [own_ab, own_cd, near_all, ret_1, ret_2, ret_3]
    blocks = [[(0, 0), (1, 0), (0, 1), (2, 0)], [(3, 0), (4, 0)], [(1, 1), (2, 1), (3, 1), (4, 1)]]
    blocks += [[(-d, 0), (-d, 1)] for d in (1, 2, 3)]
    others = move(split(place, arrays), core_step)
    return finish(place, arrays, blocks, others)


def solution(mesh):
    torus = Mesh(mesh.devices.reshape(SIZES), AXES)
    placed = (P(None, ("yhi", "x", "c"), None, ("z", "ylo")), P())
    return jax.shard_map(
        body, mesh=torus, in_specs=placed, out_specs=P(None, AXES, None), check_vma=False
    )
```

```python
import math

import jax
import jax.numpy as jnp
import numpy as np
from jax import lax
from jax.experimental import pallas as pl
from jax.experimental.pallas import tpu as pltpu
from jax.sharding import Mesh
from jax.sharding import PartitionSpec as P

NFFT = 8192
LAGS = 2
LAG_STEP = 37
HALF = 64
BINS = 512
BLOCK = 256
DEPTH = 2048
AXES = ("z", "ylo", "yhi", "x", "c")
SIZES = (8, 2, 2, 4, 2)
F32 = jnp.float32
BF16 = jnp.bfloat16
MIB = 1 << 20


def dot_nt(a, b):
    return lax.dot_general(a, b, (((1,), (1,)), ((), ())), preferred_element_type=F32)


def params(mib, **kw):
    return pltpu.CompilerParams(vmem_limit_bytes=mib * MIB, **kw)


def cost(flops, bytes_accessed):
    return pl.CostEstimate(flops=flops, bytes_accessed=bytes_accessed, transcendentals=0)


def move(x, step):
    pairs = []
    for i, at in enumerate(np.ndindex(*SIZES)):
        to = tuple(int(v) % s for v, s in zip(step(*at), SIZES))
        pairs.append((i, int(np.ravel_multi_index(to, SIZES))))
    return lax.ppermute(x, AXES, pairs)


def sign(c):
    return 1 - 2 * c


def whiten_kernel(x_ref, o_ref):
    row = lax.broadcasted_iota(jnp.int32, (BINS, BINS), 0)
    col = lax.broadcasted_iota(jnp.int32, (BINS, BINS), 1)
    window = (jnp.abs(row - col) <= HALF).astype(F32).astype(BF16)
    pos = lax.broadcasted_iota(jnp.int32, (1, BINS), 1)
    count = jnp.minimum(pos + HALF, BINS - 1) - jnp.maximum(pos - HALF, 0) + 1
    inverse = 1.0 / count.astype(F32)
    for s in range(2):
        re = x_ref[0, s].astype(F32).T
        im = x_ref[1, s].astype(F32).T
        energy = re * re + im * im
        high = energy.astype(BF16)
        low = (energy - high.astype(F32)).astype(BF16)
        total = jnp.dot(high, window, preferred_element_type=F32)
        total += jnp.dot(low, window, preferred_element_type=F32)
        scale = lax.rsqrt(total * inverse + 1e-06)
        o_ref[:, s * BINS : (s + 1) * BINS] = (re * scale).astype(BF16)
        o_ref[:, (2 + s) * BINS : (3 + s) * BINS] = (im * scale).astype(BF16)


def whiten(spectra, half):
    return pl.pallas_call(
        whiten_kernel,
        grid=(1,),
        in_specs=[pl.BlockSpec((2, 2, BINS, 128), lambda i: (0, 0, 0, half))],
        out_specs=pl.BlockSpec((128, DEPTH), lambda i: (0, 0)),
        out_shape=jax.ShapeDtypeStruct((128, DEPTH), BF16),
        compiler_params=params(12),
        cost_estimate=cost(2 * 4 * 128 * 512 * 512, MIB),
        name="whiten",
    )(spectra)


def phases(bin_index):
    lag_samples = (jnp.arange(LAGS, dtype=jnp.int32) + 1) * LAG_STEP
    phase_turn = lag_samples[:, None] * bin_index[None, :] % NFFT
    phase_angle = 2.0 * math.pi / NFFT * phase_turn.astype(F32)
    cosine, sine = jnp.cos(phase_angle), jnp.sin(phase_angle)
    return jnp.concatenate([cosine, cosine], 1), jnp.concatenate([sine, sine], 1)


def rotate_kernel(a_ref, b_ref, cos_ref, sin_ref, plus_ref, minus_ref):
    half = DEPTH // 2
    for n, ref in enumerate((a_ref, b_ref)):

        @pl.loop(0, 8)
        def _(i):
            at = pl.ds(pl.multiple_of(i * 16, 16), 16)
            to = pl.ds(pl.multiple_of(n * 128 + i * 16, 16), 16)
            re = ref[at, :half].astype(F32)
            im = ref[at, half:].astype(F32)
            for m in range(LAGS):
                cosine, sine = cos_ref[m : m + 1, :], sin_ref[m : m + 1, :]
                rc, rs, ic, is_ = re * cosine, re * sine, im * cosine, im * sine
                plus_ref[m, to, :half] = (rc - is_).astype(BF16)
                plus_ref[m, to, half:] = (rs + ic).astype(BF16)
                minus_ref[m, to, :half] = (rc + is_).astype(BF16)
                minus_ref[m, to, half:] = (ic - rs).astype(BF16)


def rotations(chunks, cosine, sine):
    shape = jax.ShapeDtypeStruct((LAGS, BLOCK, DEPTH), BF16)
    return pl.pallas_call(
        rotate_kernel,
        out_shape=(shape, shape),
        compiler_params=params(12),
        cost_estimate=cost(2 * 8 * 256 * 2048, 6 * MIB),
        name="rotate",
    )(*chunks, cosine, sine)


def store_product(acc_ref, m, first, value, scale):
    n = value.shape[1]
    for h in range(2):
        for x in range(4):
            at = h * 128 + x * 32
            acc_ref[m, h, x, :, first : first + n] = (value[at : at + 32] * scale).astype(BF16)


def products(at, parts, chunks, wide, scale, name, stage="near"):
    count = len(chunks)

    def kernel(at_ref, *refs):
        ins, (keep_ref, send_ref), acc_ref = refs[:count], refs[count : count + 2], refs[count + 2]
        x, c = at_ref[3], at_ref[4]
        near, far = 1 + 2 * c, 3 - 2 * c
        for m in range(LAGS):
            for first, value in parts(m, ins):
                store_product(acc_ref, m, first, value, scale)
        if stage == "yhi":
            for out, h in ((keep_ref, at_ref[2]), (send_ref, 1 - at_ref[2])):
                for k, which in enumerate((x, x ^ far, x ^ near, x ^ 2)):
                    for m in range(LAGS):
                        out[k, m] = acc_ref[m, h, which]
            return
        if stage == "far":
            near, far = far, near
        slices = ((keep_ref, 0, x), (keep_ref, 1, x ^ far), (send_ref, 0, x ^ near), (send_ref, 1, x ^ 2))
        for out, k, which in slices:
            for m in range(LAGS):
                for h in range(2):
                    out[k, h, m] = acc_ref[m, h, which]

    shape = jax.ShapeDtypeStruct((4, LAGS, 32, wide) if stage == "yhi" else (2, 2, LAGS, 32, wide), BF16)
    whole = pl.BlockSpec(memory_space=pltpu.VMEM)
    return pl.pallas_call(
        kernel,
        in_specs=[pl.BlockSpec(memory_space=pltpu.SMEM)] + [whole] * count,
        out_specs=[whole] * 2,
        out_shape=(shape,) * 2,
        scratch_shapes=[pltpu.VMEM((LAGS, 2, 4, 32, wide), BF16)],
        compiler_params=params(14),
        cost_estimate=cost(2 * 2 * 256 * wide * DEPTH, 8 * MIB),
        name=name,
    )(at, *chunks)


def both(a_ref, b_ref):
    return jnp.concatenate([a_ref[...], b_ref[...]], 0)


def call(kernel, scalars, arrays, shapes, name):
    whole = pl.BlockSpec(memory_space=pltpu.VMEM)
    lead = [] if scalars is None else [scalars]
    return pl.pallas_call(
        kernel,
        in_specs=[pl.BlockSpec(memory_space=pltpu.SMEM)] * len(lead) + [whole] * len(arrays),
        out_specs=[whole] * len(shapes),
        out_shape=tuple(jax.ShapeDtypeStruct(s, t) for s, t in shapes),
        compiler_params=params(12),
        cost_estimate=cost(1000, 10 * MIB),
        name=name,
    )(*lead, *arrays)


def sum_1(groups, picks):
    total = sum(n for _, _, n in picks)

    def kernel(*refs):
        kept_ref, send_ref = refs[-2:]
        for h in range(2):
            for m in range(LAGS):
                to = 0
                for g, first, n in picks:
                    cols, out = slice(first, first + n), slice(to, to + n)
                    keep, recv = refs[2 * g], refs[2 * g + 1]
                    kept_ref[h, m, :, out] = keep[0, h, m, :, cols].astype(F32) + recv[0, h, m, :, cols].astype(F32)
                    value = keep[1, h, m, :, cols].astype(F32) + recv[1, h, m, :, cols].astype(F32)
                    send_ref[h, m, :, out] = value.astype(BF16)
                    to += n

    shape = (2, LAGS, 32, total)
    return call(kernel, None, [r for g in groups for r in g], [(shape, F32), (shape, BF16)], "sum_1")


def sum_h(keep_c, recv_c, keep_d, recv_d):
    nc, nd = keep_c.shape[3], keep_d.shape[4]

    def kernel(c_ref, rc_ref, d_ref, rd_ref, keep_ref, send_ref):
        for k in range(2):
            for m in range(LAGS):
                keep_ref[k, m, :, :nc] = c_ref[k, m].astype(F32) + rc_ref[k, m].astype(F32)
                send_ref[k, m, :, :nc] = (c_ref[2 + k, m].astype(F32) + rc_ref[2 + k, m].astype(F32)).astype(BF16)
                keep_ref[k, m, :, nc:] = d_ref[0, k, m].astype(F32) + rd_ref[0, k, m].astype(F32)
                send_ref[k, m, :, nc:] = (d_ref[1, k, m].astype(F32) + rd_ref[1, k, m].astype(F32)).astype(BF16)

    shape = (2, LAGS, 32, nc + nd)
    return call(kernel, None, [keep_c, recv_c, keep_d, recv_d], [(shape, F32), (shape, BF16)], "sum_h")


def sum_n(place, kept, recv, nc):
    n = kept.shape[3]

    def kernel(place_ref, kept_ref, recv_ref, keep_ref, send_c_ref, send_d_ref):
        mine, other = place_ref[2], 1 - place_ref[2]
        c, d = slice(0, nc), slice(nc, n)
        for m in range(LAGS):
            keep_ref[m, :, c] = kept_ref[0, m, :, c] + recv_ref[0, m, :, c].astype(F32)
            send_c_ref[m] = (kept_ref[1, m, :, c] + recv_ref[1, m, :, c].astype(F32)).astype(BF16)
            keep_ref[m, :, d] = kept_ref[mine, m, :, d] + recv_ref[mine, m, :, d].astype(F32)
            send_d_ref[m] = (kept_ref[other, m, :, d] + recv_ref[other, m, :, d].astype(F32)).astype(BF16)

    shapes = [((LAGS, 32, n), F32), ((LAGS, 32, nc), BF16), ((LAGS, 32, n - nc), BF16)]
    return call(kernel, place, [kept, recv], shapes, "sum_n")


def sum_2(place, groups):
    widths = [g[0].shape[3] for g in groups]

    def kernel(place_ref, *refs):
        keep_ref, send_ref = refs[-2:]
        mine, other = place_ref[2], 1 - place_ref[2]
        first = 0
        for k, n in enumerate(widths):
            kept, recv, cols = refs[2 * k], refs[2 * k + 1], slice(first, first + n)
            for m in range(LAGS):
                keep_ref[m, :, cols] = kept[mine, m] + recv[mine, m].astype(F32)
                send_ref[m, :, cols] = (kept[other, m] + recv[other, m].astype(F32)).astype(BF16)
            first += n

    shape = (LAGS, 32, sum(widths))
    return call(kernel, place, [r for g in groups for r in g], [(shape, F32), (shape, BF16)], "sum_2")


def sum_y(keep, recvs, outputs, extra=None):
    arrays = [keep] + list(recvs) + ([] if extra is None else [extra])
    more = 0 if extra is None else extra.shape[2]
    split_at = recvs[0].shape[2]

    def kernel(*refs):
        keep_ref, outs = refs[0], refs[len(arrays) :]
        for m in range(LAGS):
            for k, (out, picks) in enumerate(zip(outs, outputs)):
                to = 0
                if k == 1 and more:
                    out[m, :, :more] = refs[len(arrays) - 1][m]
                    to = more
                for first, n in picks:
                    recv_ref, at = (refs[1], first) if first < split_at else (refs[2], first - split_at)
                    value = keep_ref[m, :, first : first + n] + recv_ref[m, :, at : at + n].astype(F32)
                    out[m, :, to : to + n] = value.astype(BF16)
                    to += n

    shapes = [((LAGS, 32, sum(n for _, n in p) + (more if k == 1 else 0)), BF16) for k, p in enumerate(outputs)]
    return call(kernel, None, arrays, shapes, "sum_y")


def split(place, arrays):
    total = sum(a.shape[2] for a in arrays)

    def kernel(place_ref, *refs):
        at = pl.ds(pl.multiple_of((1 - place_ref[4]) * 16, 16), 16)
        first = 0
        for ref in refs[:-1]:
            n = ref.shape[2]
            for m in range(LAGS):
                refs[-1][m, :, first : first + n] = ref[m, at, :]
            first += n

    return call(kernel, place, arrays, [((LAGS, 16, total), BF16)], "split")[0]


def finish(place, arrays, blocks, recv):
    def kernel(place_ref, *refs):
        ins, recv_ref, out = refs[:-2], refs[-2], refs[-1]
        z, y, c = place_ref[0], place_ref[1], place_ref[4]
        rows = pl.ds(pl.multiple_of(c * 16, 16), 16)

        def cols(block, way):
            dist, dy = block
            zz = lax.rem(z - way * dist + 16, 8)
            yy = y if dy == 0 else 1 - y
            return pl.ds(pl.multiple_of((zz * 2 + yy) * BLOCK, BLOCK), BLOCK)

        for m in range(LAGS):
            for ref, ids in zip(ins, blocks):
                for n, block in enumerate(ids):
                    out[m, :, cols(block, 1 - 2 * c)] = ref[m, rows, n * BLOCK : (n + 1) * BLOCK].astype(F32)
            for n, block in enumerate(sum(blocks, [])):
                out[m, :, cols(block, 2 * c - 1)] += recv_ref[m, :, n * BLOCK : (n + 1) * BLOCK].astype(F32)

    return call(kernel, place, list(arrays) + [recv], [((LAGS, 16, 4096), F32)], "finish")[0]


def chain_step(z, ylo, yhi, x, c):
    return z + sign(c), ylo, yhi, x, c


def y_step(z, ylo, yhi, x, c):
    return z, 1 - ylo, yhi, x, c


def yhi_step(z, ylo, yhi, x, c):
    return z, ylo, 1 - yhi, x, c


def core_step(z, ylo, yhi, x, c):
    return z, ylo, yhi, x, 1 - c


def x_near(z, ylo, yhi, x, c):
    return z, ylo, yhi, x ^ (1 + 2 * c), c


def x_far(z, ylo, yhi, x, c):
    return z, ylo, yhi, x ^ (3 - 2 * c), c


def back(d):
    return lambda z, ylo, yhi, x, c: (z - sign(c) * d, ylo, yhi, x, c)


def after(value, *others):
    return lax.optimization_barrier((value,) + others)[0]


def body(spectra, bin_index):
    scale = 1.0 / math.sqrt(32 * BINS)
    place = jnp.stack([lax.axis_index(a) for a in AXES]).astype(jnp.int32)

    spectra = after(spectra, place)
    own = [whiten(spectra, 0), whiten(spectra, 1)]
    near = [move(b, y_step) for b in own]
    first = [move(b, chain_step) for b in own]
    second = [move(b, chain_step) for b in (first[0], first[1])]

    cosine, sine = phases(bin_index)
    own_plus, own_minus = rotations(own, cosine, sine)
    near_plus, near_minus = rotations(near, cosine, sine)

    def all_pairs(m, ins, at=0):
        b = both(ins[at], ins[at + 1])
        op, om, np_, nm = ins[-4:]
        yield 0, dot_nt(op[m], b)
        yield BLOCK, dot_nt(np_[m], b)
        yield 2 * BLOCK, dot_nt(b, om[m])
        yield 3 * BLOCK, dot_nt(b, nm[m])

    def own_pairs(m, ins):
        op, om = ins[-2:]
        b = both(ins[0], ins[1])
        yield 0, dot_nt(op[m], both(ins[2], ins[3]))
        yield BLOCK, dot_nt(op[m], b)
        yield 2 * BLOCK, dot_nt(b, om[m])

    def near_pairs(m, ins):
        op, np_, nm = ins[-3:]
        b = both(ins[0], ins[1])
        yield 0, dot_nt(op[m], both(ins[2], ins[3]))
        yield BLOCK, dot_nt(np_[m], b)
        yield 2 * BLOCK, dot_nt(b, nm[m])

    def last_pairs(m, ins):
        b = both(ins[0], ins[1])
        yield 0, dot_nt(ins[2][m], b)
        yield BLOCK, dot_nt(ins[3][m], b)

    rotated = [own_plus, own_minus, near_plus, near_minus]
    straight = [(0, 0, 4 * BLOCK)]

    keep_o, send_o = products(place, own_pairs, first + own + rotated[:2], 3 * BLOCK, scale, "pairs_own")
    recv_o = move(send_o, x_near)
    third = [move(after(second[0], near[0], near[1], keep_o), chain_step)]
    at = after(place, recv_o)
    near_rotated = [own_plus, near_plus, near_minus]
    keep_n, send_n = products(at, near_pairs, first + near + near_rotated, 3 * BLOCK, scale, "pairs_near")
    recv_n = move(send_n, x_near)
    third.append(move(after(second[1], keep_n), chain_step))
    at = after(place, keep_n)
    keep_b, send_b = products(at, all_pairs, second + rotated, 4 * BLOCK, scale, "pairs_2")
    recv_b = move(send_b, x_near)
    fourth = [move(b, chain_step) for b in (after(third[0], keep_b), third[1])]
    at = after(place, keep_b, recv_n)
    keep_c, send_c = products(at, all_pairs, third + rotated, 4 * BLOCK, scale, "pairs_3", "yhi")
    recv_c = move(send_c, yhi_step)
    picks = [(0, 0, 2 * BLOCK), (1, 0, BLOCK), (1, BLOCK, BLOCK), (0, 2 * BLOCK, BLOCK), (1, 2 * BLOCK, BLOCK)]
    keep_o = after(keep_o, keep_c, fourth[0])
    kept_ab, send_ab = sum_1([(keep_o, recv_o), (keep_n, recv_n), (keep_b, recv_b)], picks + [(2, 0, 4 * BLOCK)])
    recv_ab = move(send_ab, x_far)
    at = after(place, kept_ab)
    keep_d, send_d = products(at, last_pairs, fourth + [own_plus, near_plus], 2 * BLOCK, scale, "pairs_4", "far")
    recv_d = move(send_d, x_far)
    keep_ab, send_ab = sum_2(place, [(after(kept_ab, keep_d), recv_ab)])
    recv_ab = move(send_ab, yhi_step)
    kept_cd, send_cd = sum_h(after(keep_c, keep_ab), recv_c, keep_d, recv_d)
    recv_cd = move(send_cd, x_near)
    keep_cd, send_c, send_d = sum_n(place, kept_cd, recv_cd, 4 * BLOCK)
    recv_cd = [move(send_c, x_far), move(send_d, yhi_step)]
    outputs = [[(0, 768), (1536, 256)], [(768, 256), (1792, 256)], [(1024, 512)], [(2048, 512)]]
    own_ab, near_ab, ret_1, ret_2 = sum_y(after(keep_ab, keep_cd), [recv_ab], outputs)
    ret_1, ret_2 = move(ret_1, back(1)), move(ret_2, back(2))
    outputs = [[(0, 256), (1024, 256)], [(256, 256), (1280, 256)], [(512, 512)]]
    own_cd, near_all, ret_3 = sum_y(after(keep_cd, ret_1, ret_2), recv_cd, outputs, near_ab)
    ret_3 = move(ret_3, back(3))
    near_all = move(near_all, y_step)
    arrays = [own_ab, own_cd, near_all, ret_1, ret_2, ret_3]
    blocks = [[(0, 0), (1, 0), (0, 1), (2, 0)], [(3, 0), (4, 0)], [(1, 1), (2, 1), (3, 1), (4, 1)]]
    blocks += [[(-d, 0), (-d, 1)] for d in (1, 2, 3)]
    others = move(split(place, arrays), core_step)
    return finish(place, arrays, blocks, others)


def solution(mesh):
    torus = Mesh(mesh.devices.reshape(SIZES), AXES)
    placed = (P(None, ("yhi", "x", "c"), None, ("z", "ylo")), P())
    return jax.shard_map(
        body, mesh=torus, in_specs=placed, out_specs=P(None, AXES, None), check_vma=False
    )
```

```python
import math

import jax
import jax.numpy as jnp
import numpy as np
from jax import lax
from jax.experimental import pallas as pl
from jax.experimental.pallas import tpu as pltpu
from jax.sharding import Mesh
from jax.sharding import PartitionSpec as P

NFFT = 8192
LAGS = 2
LAG_STEP = 37
HALF = 64
BINS = 512
BLOCK = 256
DEPTH = 2048
AXES = ("z", "ylo", "yhi", "x", "c")
SIZES = (8, 2, 2, 4, 2)
F32 = jnp.float32
BF16 = jnp.bfloat16
MIB = 1 << 20


def dot_nt(a, b):
    return lax.dot_general(a, b, (((1,), (1,)), ((), ())), preferred_element_type=F32)


def params(mib, **kw):
    return pltpu.CompilerParams(vmem_limit_bytes=mib * MIB, **kw)


def cost(flops, bytes_accessed):
    return pl.CostEstimate(flops=flops, bytes_accessed=bytes_accessed, transcendentals=0)


def move(x, step):
    pairs = []
    for i, at in enumerate(np.ndindex(*SIZES)):
        to = tuple(int(v) % s for v, s in zip(step(*at), SIZES))
        pairs.append((i, int(np.ravel_multi_index(to, SIZES))))
    return lax.ppermute(x, AXES, pairs)


def sign(c):
    return 1 - 2 * c


def whiten_kernel(x_ref, o_ref):
    row = lax.broadcasted_iota(jnp.int32, (BINS, BINS), 0)
    col = lax.broadcasted_iota(jnp.int32, (BINS, BINS), 1)
    window = (jnp.abs(row - col) <= HALF).astype(F32).astype(BF16)
    pos = lax.broadcasted_iota(jnp.int32, (1, BINS), 1)
    count = jnp.minimum(pos + HALF, BINS - 1) - jnp.maximum(pos - HALF, 0) + 1
    inverse = 1.0 / count.astype(F32)
    for s in range(2):
        re = x_ref[0, s].astype(F32).T
        im = x_ref[1, s].astype(F32).T
        energy = re * re + im * im
        high = energy.astype(BF16)
        low = (energy - high.astype(F32)).astype(BF16)
        total = jnp.dot(high, window, preferred_element_type=F32)
        total += jnp.dot(low, window, preferred_element_type=F32)
        scale = lax.rsqrt(total * inverse + 1e-06)
        o_ref[:, s * BINS : (s + 1) * BINS] = (re * scale).astype(BF16)
        o_ref[:, (2 + s) * BINS : (3 + s) * BINS] = (im * scale).astype(BF16)


def whiten(spectra, half):
    return pl.pallas_call(
        whiten_kernel,
        grid=(1,),
        in_specs=[pl.BlockSpec((2, 2, BINS, 128), lambda i: (0, 0, 0, half))],
        out_specs=pl.BlockSpec((128, DEPTH), lambda i: (0, 0)),
        out_shape=jax.ShapeDtypeStruct((128, DEPTH), BF16),
        compiler_params=params(12),
        cost_estimate=cost(2 * 4 * 128 * 512 * 512, MIB),
        name="whiten",
    )(spectra)


def phases(bin_index):
    lag_samples = (jnp.arange(LAGS, dtype=jnp.int32) + 1) * LAG_STEP
    phase_turn = lag_samples[:, None] * bin_index[None, :] % NFFT
    phase_angle = 2.0 * math.pi / NFFT * phase_turn.astype(F32)
    cosine, sine = jnp.cos(phase_angle), jnp.sin(phase_angle)
    return jnp.concatenate([cosine, cosine], 1), jnp.concatenate([sine, sine], 1)


def rotate_kernel(a_ref, b_ref, cos_ref, sin_ref, plus_ref, minus_ref):
    half = DEPTH // 2
    for n, ref in enumerate((a_ref, b_ref)):

        @pl.loop(0, 8)
        def _(i):
            at = pl.ds(pl.multiple_of(i * 16, 16), 16)
            to = pl.ds(pl.multiple_of(n * 128 + i * 16, 16), 16)
            re = ref[at, :half].astype(F32)
            im = ref[at, half:].astype(F32)
            for m in range(LAGS):
                cosine, sine = cos_ref[m : m + 1, :], sin_ref[m : m + 1, :]
                rc, rs, ic, is_ = re * cosine, re * sine, im * cosine, im * sine
                plus_ref[m, to, :half] = (rc - is_).astype(BF16)
                plus_ref[m, to, half:] = (rs + ic).astype(BF16)
                minus_ref[m, to, :half] = (rc + is_).astype(BF16)
                minus_ref[m, to, half:] = (ic - rs).astype(BF16)


def rotations(chunks, cosine, sine):
    shape = jax.ShapeDtypeStruct((LAGS, BLOCK, DEPTH), BF16)
    return pl.pallas_call(
        rotate_kernel,
        out_shape=(shape, shape),
        compiler_params=params(12),
        cost_estimate=cost(2 * 8 * 256 * 2048, 6 * MIB),
        name="rotate",
    )(*chunks, cosine, sine)


def store_product(acc_ref, m, first, value, scale):
    n = value.shape[1]
    for h in range(2):
        for x in range(4):
            at = h * 128 + x * 32
            acc_ref[m, h, x, :, first : first + n] = (value[at : at + 32] * scale).astype(BF16)


def products(at, parts, chunks, wide, scale, name, stage="near"):
    count = len(chunks)

    def kernel(at_ref, *refs):
        ins, (keep_ref, send_ref), acc_ref = refs[:count], refs[count : count + 2], refs[count + 2]
        x, c = at_ref[3], at_ref[4]
        near, far = 1 + 2 * c, 3 - 2 * c
        for m in range(LAGS):
            for first, value in parts(m, ins):
                store_product(acc_ref, m, first, value, scale)
        if stage == "yhi":
            for out, h in ((keep_ref, at_ref[2]), (send_ref, 1 - at_ref[2])):
                for k, which in enumerate((x, x ^ far, x ^ near, x ^ 2)):
                    for m in range(LAGS):
                        out[k, m] = acc_ref[m, h, which]
            return
        if stage == "far":
            near, far = far, near
        slices = ((keep_ref, 0, x), (keep_ref, 1, x ^ far), (send_ref, 0, x ^ near), (send_ref, 1, x ^ 2))
        for out, k, which in slices:
            for m in range(LAGS):
                for h in range(2):
                    out[k, h, m] = acc_ref[m, h, which]

    shape = jax.ShapeDtypeStruct((4, LAGS, 32, wide) if stage == "yhi" else (2, 2, LAGS, 32, wide), BF16)
    whole = pl.BlockSpec(memory_space=pltpu.VMEM)
    return pl.pallas_call(
        kernel,
        in_specs=[pl.BlockSpec(memory_space=pltpu.SMEM)] + [whole] * count,
        out_specs=[whole] * 2,
        out_shape=(shape,) * 2,
        scratch_shapes=[pltpu.VMEM((LAGS, 2, 4, 32, wide), BF16)],
        compiler_params=params(14),
        cost_estimate=cost(2 * 2 * 256 * wide * DEPTH, 8 * MIB),
        name=name,
    )(at, *chunks)


def both(a_ref, b_ref):
    return jnp.concatenate([a_ref[...], b_ref[...]], 0)


def call(kernel, scalars, arrays, shapes, name):
    whole = pl.BlockSpec(memory_space=pltpu.VMEM)
    lead = [] if scalars is None else [scalars]
    return pl.pallas_call(
        kernel,
        in_specs=[pl.BlockSpec(memory_space=pltpu.SMEM)] * len(lead) + [whole] * len(arrays),
        out_specs=[whole] * len(shapes),
        out_shape=tuple(jax.ShapeDtypeStruct(s, t) for s, t in shapes),
        compiler_params=params(12),
        cost_estimate=cost(1000, 10 * MIB),
        name=name,
    )(*lead, *arrays)


def sum_1(groups, picks):
    total = sum(n for _, _, n in picks)

    def kernel(*refs):
        kept_ref, send_ref = refs[-2:]
        for h in range(2):
            for m in range(LAGS):
                to = 0
                for g, first, n in picks:
                    cols, out = slice(first, first + n), slice(to, to + n)
                    keep, recv = refs[2 * g], refs[2 * g + 1]
                    kept_ref[h, m, :, out] = keep[0, h, m, :, cols].astype(F32) + recv[0, h, m, :, cols].astype(F32)
                    value = keep[1, h, m, :, cols].astype(F32) + recv[1, h, m, :, cols].astype(F32)
                    send_ref[h, m, :, out] = value.astype(BF16)
                    to += n

    shape = (2, LAGS, 32, total)
    return call(kernel, None, [r for g in groups for r in g], [(shape, F32), (shape, BF16)], "sum_1")


def sum_h(keep_c, recv_c, keep_d, recv_d):
    nc, nd = keep_c.shape[3], keep_d.shape[4]

    def kernel(c_ref, rc_ref, d_ref, rd_ref, keep_ref, send_ref):
        for k in range(2):
            for m in range(LAGS):
                keep_ref[k, m, :, :nc] = c_ref[k, m].astype(F32) + rc_ref[k, m].astype(F32)
                send_ref[k, m, :, :nc] = (c_ref[2 + k, m].astype(F32) + rc_ref[2 + k, m].astype(F32)).astype(BF16)
                keep_ref[k, m, :, nc:] = d_ref[0, k, m].astype(F32) + rd_ref[0, k, m].astype(F32)
                send_ref[k, m, :, nc:] = (d_ref[1, k, m].astype(F32) + rd_ref[1, k, m].astype(F32)).astype(BF16)

    shape = (2, LAGS, 32, nc + nd)
    return call(kernel, None, [keep_c, recv_c, keep_d, recv_d], [(shape, F32), (shape, BF16)], "sum_h")


def sum_n(place, kept, recv, nc):
    n = kept.shape[3]

    def kernel(place_ref, kept_ref, recv_ref, keep_ref, send_c_ref, send_d_ref):
        mine, other = place_ref[2], 1 - place_ref[2]
        c, d = slice(0, nc), slice(nc, n)
        for m in range(LAGS):
            keep_ref[m, :, c] = kept_ref[0, m, :, c] + recv_ref[0, m, :, c].astype(F32)
            send_c_ref[m] = (kept_ref[1, m, :, c] + recv_ref[1, m, :, c].astype(F32)).astype(BF16)
            keep_ref[m, :, d] = kept_ref[mine, m, :, d] + recv_ref[mine, m, :, d].astype(F32)
            send_d_ref[m] = (kept_ref[other, m, :, d] + recv_ref[other, m, :, d].astype(F32)).astype(BF16)

    shapes = [((LAGS, 32, n), F32), ((LAGS, 32, nc), BF16), ((LAGS, 32, n - nc), BF16)]
    return call(kernel, place, [kept, recv], shapes, "sum_n")


def sum_2(place, groups):
    widths = [g[0].shape[3] for g in groups]

    def kernel(place_ref, *refs):
        keep_ref, send_ref = refs[-2:]
        mine, other = place_ref[2], 1 - place_ref[2]
        first = 0
        for k, n in enumerate(widths):
            kept, recv, cols = refs[2 * k], refs[2 * k + 1], slice(first, first + n)
            for m in range(LAGS):
                keep_ref[m, :, cols] = kept[mine, m] + recv[mine, m].astype(F32)
                send_ref[m, :, cols] = (kept[other, m] + recv[other, m].astype(F32)).astype(BF16)
            first += n

    shape = (LAGS, 32, sum(widths))
    return call(kernel, place, [r for g in groups for r in g], [(shape, F32), (shape, BF16)], "sum_2")


def sum_y(keep, recvs, outputs, extra=None):
    arrays = [keep] + list(recvs) + ([] if extra is None else [extra])
    more = 0 if extra is None else extra.shape[2]
    split_at = recvs[0].shape[2]

    def kernel(*refs):
        keep_ref, outs = refs[0], refs[len(arrays) :]
        for m in range(LAGS):
            for k, (out, picks) in enumerate(zip(outs, outputs)):
                to = 0
                if k == 1 and more:
                    out[m, :, :more] = refs[len(arrays) - 1][m]
                    to = more
                for first, n in picks:
                    recv_ref, at = (refs[1], first) if first < split_at else (refs[2], first - split_at)
                    value = keep_ref[m, :, first : first + n] + recv_ref[m, :, at : at + n].astype(F32)
                    out[m, :, to : to + n] = value.astype(BF16)
                    to += n

    shapes = [((LAGS, 32, sum(n for _, n in p) + (more if k == 1 else 0)), BF16) for k, p in enumerate(outputs)]
    return call(kernel, None, arrays, shapes, "sum_y")


def split(place, arrays):
    total = sum(a.shape[2] for a in arrays)

    def kernel(place_ref, *refs):
        at = pl.ds(pl.multiple_of((1 - place_ref[4]) * 16, 16), 16)
        first = 0
        for ref in refs[:-1]:
            n = ref.shape[2]
            for m in range(LAGS):
                refs[-1][m, :, first : first + n] = ref[m, at, :]
            first += n

    return call(kernel, place, arrays, [((LAGS, 16, total), BF16)], "split")[0]


def finish(place, arrays, blocks, recv):
    def kernel(place_ref, *refs):
        ins, recv_ref, out = refs[:-2], refs[-2], refs[-1]
        z, y, c = place_ref[0], place_ref[1], place_ref[4]
        rows = pl.ds(pl.multiple_of(c * 16, 16), 16)

        def cols(block, way):
            dist, dy = block
            zz = lax.rem(z - way * dist + 16, 8)
            yy = y if dy == 0 else 1 - y
            return pl.ds(pl.multiple_of((zz * 2 + yy) * BLOCK, BLOCK), BLOCK)

        for m in range(LAGS):
            for ref, ids in zip(ins, blocks):
                for n, block in enumerate(ids):
                    out[m, :, cols(block, 1 - 2 * c)] = ref[m, rows, n * BLOCK : (n + 1) * BLOCK].astype(F32)
            for n, block in enumerate(sum(blocks, [])):
                out[m, :, cols(block, 2 * c - 1)] += recv_ref[m, :, n * BLOCK : (n + 1) * BLOCK].astype(F32)

    return call(kernel, place, list(arrays) + [recv], [((LAGS, 16, 4096), F32)], "finish")[0]


def chain_step(z, ylo, yhi, x, c):
    return z + sign(c), ylo, yhi, x, c


def y_step(z, ylo, yhi, x, c):
    return z, 1 - ylo, yhi, x, c


def yhi_step(z, ylo, yhi, x, c):
    return z, ylo, 1 - yhi, x, c


def core_step(z, ylo, yhi, x, c):
    return z, ylo, yhi, x, 1 - c


def x_near(z, ylo, yhi, x, c):
    return z, ylo, yhi, x ^ (1 + 2 * c), c


def x_far(z, ylo, yhi, x, c):
    return z, ylo, yhi, x ^ (3 - 2 * c), c


def back(d):
    return lambda z, ylo, yhi, x, c: (z - sign(c) * d, ylo, yhi, x, c)


def after(value, *others):
    return lax.optimization_barrier((value,) + others)[0]


def body(spectra, bin_index):
    scale = 1.0 / math.sqrt(32 * BINS)
    place = jnp.stack([lax.axis_index(a) for a in AXES]).astype(jnp.int32)

    spectra = after(spectra, place)
    own = [whiten(spectra, 0), whiten(spectra, 1)]
    near = [move(b, y_step) for b in own]
    first = [move(b, chain_step) for b in own]
    second = [move(b, chain_step) for b in (first[0], first[1])]

    cosine, sine = phases(bin_index)
    own_plus, own_minus = rotations(own, cosine, sine)
    near_plus, near_minus = rotations(near, cosine, sine)

    def all_pairs(m, ins, at=0):
        b = both(ins[at], ins[at + 1])
        op, om, np_, nm = ins[-4:]
        yield 0, dot_nt(op[m], b)
        yield BLOCK, dot_nt(np_[m], b)
        yield 2 * BLOCK, dot_nt(b, om[m])
        yield 3 * BLOCK, dot_nt(b, nm[m])

    def own_pairs(m, ins):
        op, om = ins[-2:]
        b = both(ins[0], ins[1])
        yield 0, dot_nt(op[m], both(ins[2], ins[3]))
        yield BLOCK, dot_nt(op[m], b)
        yield 2 * BLOCK, dot_nt(b, om[m])

    def near_pairs(m, ins):
        op, np_, nm = ins[-3:]
        b = both(ins[0], ins[1])
        yield 0, dot_nt(op[m], both(ins[2], ins[3]))
        yield BLOCK, dot_nt(np_[m], b)
        yield 2 * BLOCK, dot_nt(b, nm[m])

    def last_pairs(m, ins):
        b = both(ins[0], ins[1])
        yield 0, dot_nt(ins[2][m], b)
        yield BLOCK, dot_nt(ins[3][m], b)

    rotated = [own_plus, own_minus, near_plus, near_minus]
    straight = [(0, 0, 4 * BLOCK)]

    keep_o, send_o = products(place, own_pairs, first + own + rotated[:2], 3 * BLOCK, scale, "pairs_own")
    recv_o = move(send_o, x_near)
    third = [move(after(second[0], near[0], keep_o), chain_step)]
    at = after(place, recv_o)
    near_rotated = [own_plus, near_plus, near_minus]
    keep_n, send_n = products(at, near_pairs, first + near + near_rotated, 3 * BLOCK, scale, "pairs_near")
    recv_n = move(send_n, x_near)
    third.append(move(after(second[1], keep_n), chain_step))
    at = after(place, keep_n)
    keep_b, send_b = products(at, all_pairs, second + rotated, 4 * BLOCK, scale, "pairs_2")
    recv_b = move(send_b, x_near)
    fourth = [move(b, chain_step) for b in (after(third[0], keep_b), third[1])]
    at = after(place, keep_b, recv_n)
    keep_c, send_c = products(at, all_pairs, third + rotated, 4 * BLOCK, scale, "pairs_3", "yhi")
    recv_c = move(send_c, yhi_step)
    picks = [(0, 0, 2 * BLOCK), (1, 0, BLOCK), (1, BLOCK, BLOCK), (0, 2 * BLOCK, BLOCK), (1, 2 * BLOCK, BLOCK)]
    keep_o = after(keep_o, keep_c, fourth[0])
    kept_ab, send_ab = sum_1([(keep_o, recv_o), (keep_n, recv_n), (keep_b, recv_b)], picks + [(2, 0, 4 * BLOCK)])
    recv_ab = move(send_ab, x_far)
    at = after(place, kept_ab)
    keep_d, send_d = products(at, last_pairs, fourth + [own_plus, near_plus], 2 * BLOCK, scale, "pairs_4", "far")
    recv_d = move(send_d, x_far)
    keep_ab, send_ab = sum_2(place, [(after(kept_ab, keep_d), recv_ab)])
    recv_ab = move(send_ab, yhi_step)
    kept_cd, send_cd = sum_h(after(keep_c, keep_ab), recv_c, keep_d, recv_d)
    recv_cd = move(send_cd, x_near)
    keep_cd, send_c, send_d = sum_n(place, kept_cd, recv_cd, 4 * BLOCK)
    recv_cd = [move(send_c, x_far), move(send_d, yhi_step)]
    outputs = [[(0, 768), (1536, 256)], [(768, 256), (1792, 256)], [(1024, 512)], [(2048, 512)]]
    own_ab, near_ab, ret_1, ret_2 = sum_y(after(keep_ab, keep_cd), [recv_ab], outputs)
    ret_1, ret_2 = move(ret_1, back(1)), move(ret_2, back(2))
    outputs = [[(0, 256), (1024, 256)], [(256, 256), (1280, 256)], [(512, 512)]]
    own_cd, near_all, ret_3 = sum_y(after(keep_cd, own_ab), recv_cd, outputs, near_ab)
    ret_3 = move(ret_3, back(3))
    near_all = move(near_all, y_step)
    arrays = [own_ab, own_cd, near_all, ret_1, ret_2, ret_3]
    blocks = [[(0, 0), (1, 0), (0, 1), (2, 0)], [(3, 0), (4, 0)], [(1, 1), (2, 1), (3, 1), (4, 1)]]
    blocks += [[(-d, 0), (-d, 1)] for d in (1, 2, 3)]
    others = move(split(place, arrays), core_step)
    return finish(place, arrays, blocks, others)


def solution(mesh):
    torus = Mesh(mesh.devices.reshape(SIZES), AXES)
    placed = (P(None, ("yhi", "x", "c"), None, ("z", "ylo")), P())
    return jax.shard_map(
        body, mesh=torus, in_specs=placed, out_specs=P(None, AXES, None), check_vma=False
    )
```

```python
import math

import jax
import jax.numpy as jnp
import numpy as np
from jax import lax
from jax.experimental import pallas as pl
from jax.experimental.pallas import tpu as pltpu
from jax.sharding import Mesh
from jax.sharding import PartitionSpec as P

NFFT = 8192
LAGS = 2
LAG_STEP = 37
HALF = 64
BINS = 512
BLOCK = 256
DEPTH = 2048
AXES = ("z", "ylo", "yhi", "x", "c")
SIZES = (8, 2, 2, 4, 2)
F32 = jnp.float32
BF16 = jnp.bfloat16
MIB = 1 << 20


def dot_nt(a, b):
    return lax.dot_general(a, b, (((1,), (1,)), ((), ())), preferred_element_type=F32)


def params(mib, **kw):
    return pltpu.CompilerParams(vmem_limit_bytes=mib * MIB, **kw)


def cost(flops, bytes_accessed):
    return pl.CostEstimate(flops=flops, bytes_accessed=bytes_accessed, transcendentals=0)


def move(x, step):
    pairs = []
    for i, at in enumerate(np.ndindex(*SIZES)):
        to = tuple(int(v) % s for v, s in zip(step(*at), SIZES))
        pairs.append((i, int(np.ravel_multi_index(to, SIZES))))
    return lax.ppermute(x, AXES, pairs)


def sign(c):
    return 1 - 2 * c


def whiten_kernel(x_ref, o_ref):
    row = lax.broadcasted_iota(jnp.int32, (BINS, BINS), 0)
    col = lax.broadcasted_iota(jnp.int32, (BINS, BINS), 1)
    window = (jnp.abs(row - col) <= HALF).astype(F32).astype(BF16)
    pos = lax.broadcasted_iota(jnp.int32, (1, BINS), 1)
    count = jnp.minimum(pos + HALF, BINS - 1) - jnp.maximum(pos - HALF, 0) + 1
    inverse = 1.0 / count.astype(F32)
    for s in range(2):
        re = x_ref[0, s].astype(F32).T
        im = x_ref[1, s].astype(F32).T
        energy = re * re + im * im
        high = energy.astype(BF16)
        low = (energy - high.astype(F32)).astype(BF16)
        total = jnp.dot(high, window, preferred_element_type=F32)
        total += jnp.dot(low, window, preferred_element_type=F32)
        scale = lax.rsqrt(total * inverse + 1e-06)
        o_ref[:, s * BINS : (s + 1) * BINS] = (re * scale).astype(BF16)
        o_ref[:, (2 + s) * BINS : (3 + s) * BINS] = (im * scale).astype(BF16)


def whiten(spectra, half):
    return pl.pallas_call(
        whiten_kernel,
        grid=(1,),
        in_specs=[pl.BlockSpec((2, 2, BINS, 128), lambda i: (0, 0, 0, half))],
        out_specs=pl.BlockSpec((128, DEPTH), lambda i: (0, 0)),
        out_shape=jax.ShapeDtypeStruct((128, DEPTH), BF16),
        compiler_params=params(12),
        cost_estimate=cost(2 * 4 * 128 * 512 * 512, MIB),
        name="whiten",
    )(spectra)


def phases(bin_index):
    lag_samples = (jnp.arange(LAGS, dtype=jnp.int32) + 1) * LAG_STEP
    phase_turn = lag_samples[:, None] * bin_index[None, :] % NFFT
    phase_angle = 2.0 * math.pi / NFFT * phase_turn.astype(F32)
    cosine, sine = jnp.cos(phase_angle), jnp.sin(phase_angle)
    return jnp.concatenate([cosine, cosine], 1), jnp.concatenate([sine, sine], 1)


def rotate_kernel(a_ref, b_ref, cos_ref, sin_ref, plus_ref, minus_ref):
    half = DEPTH // 2
    for n, ref in enumerate((a_ref, b_ref)):

        @pl.loop(0, 8)
        def _(i):
            at = pl.ds(pl.multiple_of(i * 16, 16), 16)
            to = pl.ds(pl.multiple_of(n * 128 + i * 16, 16), 16)
            re = ref[at, :half].astype(F32)
            im = ref[at, half:].astype(F32)
            for m in range(LAGS):
                cosine, sine = cos_ref[m : m + 1, :], sin_ref[m : m + 1, :]
                rc, rs, ic, is_ = re * cosine, re * sine, im * cosine, im * sine
                plus_ref[m, to, :half] = (rc - is_).astype(BF16)
                plus_ref[m, to, half:] = (rs + ic).astype(BF16)
                minus_ref[m, to, :half] = (rc + is_).astype(BF16)
                minus_ref[m, to, half:] = (ic - rs).astype(BF16)


def rotations(chunks, cosine, sine):
    shape = jax.ShapeDtypeStruct((LAGS, BLOCK, DEPTH), BF16)
    return pl.pallas_call(
        rotate_kernel,
        out_shape=(shape, shape),
        compiler_params=params(12),
        cost_estimate=cost(2 * 8 * 256 * 2048, 6 * MIB),
        name="rotate",
    )(*chunks, cosine, sine)


def store_product(acc_ref, m, first, value, scale):
    n = value.shape[1]
    for h in range(2):
        for x in range(4):
            at = h * 128 + x * 32
            acc_ref[m, h, x, :, first : first + n] = (value[at : at + 32] * scale).astype(BF16)


def products(at, parts, chunks, wide, scale, name, stage="near"):
    count = len(chunks)

    def kernel(at_ref, *refs):
        ins, (keep_ref, send_ref), acc_ref = refs[:count], refs[count : count + 2], refs[count + 2]
        x, c = at_ref[3], at_ref[4]
        near, far = 1 + 2 * c, 3 - 2 * c
        for m in range(LAGS):
            for first, value in parts(m, ins):
                store_product(acc_ref, m, first, value, scale)
        if stage == "yhi":
            for out, h in ((keep_ref, at_ref[2]), (send_ref, 1 - at_ref[2])):
                for k, which in enumerate((x, x ^ far, x ^ near, x ^ 2)):
                    for m in range(LAGS):
                        out[k, m] = acc_ref[m, h, which]
            return
        if stage == "far":
            near, far = far, near
        slices = ((keep_ref, 0, x), (keep_ref, 1, x ^ far), (send_ref, 0, x ^ near), (send_ref, 1, x ^ 2))
        for out, k, which in slices:
            for m in range(LAGS):
                for h in range(2):
                    out[k, h, m] = acc_ref[m, h, which]

    shape = jax.ShapeDtypeStruct((4, LAGS, 32, wide) if stage == "yhi" else (2, 2, LAGS, 32, wide), BF16)
    whole = pl.BlockSpec(memory_space=pltpu.VMEM)
    return pl.pallas_call(
        kernel,
        in_specs=[pl.BlockSpec(memory_space=pltpu.SMEM)] + [whole] * count,
        out_specs=[whole] * 2,
        out_shape=(shape,) * 2,
        scratch_shapes=[pltpu.VMEM((LAGS, 2, 4, 32, wide), BF16)],
        compiler_params=params(14),
        cost_estimate=cost(2 * 2 * 256 * wide * DEPTH, 8 * MIB),
        name=name,
    )(at, *chunks)


def both(a_ref, b_ref):
    return jnp.concatenate([a_ref[...], b_ref[...]], 0)


def call(kernel, scalars, arrays, shapes, name):
    whole = pl.BlockSpec(memory_space=pltpu.VMEM)
    lead = [] if scalars is None else [scalars]
    return pl.pallas_call(
        kernel,
        in_specs=[pl.BlockSpec(memory_space=pltpu.SMEM)] * len(lead) + [whole] * len(arrays),
        out_specs=[whole] * len(shapes),
        out_shape=tuple(jax.ShapeDtypeStruct(s, t) for s, t in shapes),
        compiler_params=params(12),
        cost_estimate=cost(1000, 10 * MIB),
        name=name,
    )(*lead, *arrays)


def sum_1(groups, picks):
    total = sum(n for _, _, n in picks)

    def kernel(*refs):
        kept_ref, send_ref = refs[-2:]
        for h in range(2):
            for m in range(LAGS):
                to = 0
                for g, first, n in picks:
                    cols, out = slice(first, first + n), slice(to, to + n)
                    keep, recv = refs[2 * g], refs[2 * g + 1]
                    kept_ref[h, m, :, out] = keep[0, h, m, :, cols].astype(F32) + recv[0, h, m, :, cols].astype(F32)
                    value = keep[1, h, m, :, cols].astype(F32) + recv[1, h, m, :, cols].astype(F32)
                    send_ref[h, m, :, out] = value.astype(BF16)
                    to += n

    shape = (2, LAGS, 32, total)
    return call(kernel, None, [r for g in groups for r in g], [(shape, F32), (shape, BF16)], "sum_1")


def sum_h(keep_c, recv_c, keep_d, recv_d):
    nc, nd = keep_c.shape[3], keep_d.shape[4]

    def kernel(c_ref, rc_ref, d_ref, rd_ref, keep_ref, send_ref):
        for k in range(2):
            for m in range(LAGS):
                keep_ref[k, m, :, :nc] = c_ref[k, m].astype(F32) + rc_ref[k, m].astype(F32)
                send_ref[k, m, :, :nc] = (c_ref[2 + k, m].astype(F32) + rc_ref[2 + k, m].astype(F32)).astype(BF16)
                keep_ref[k, m, :, nc:] = d_ref[0, k, m].astype(F32) + rd_ref[0, k, m].astype(F32)
                send_ref[k, m, :, nc:] = (d_ref[1, k, m].astype(F32) + rd_ref[1, k, m].astype(F32)).astype(BF16)

    shape = (2, LAGS, 32, nc + nd)
    return call(kernel, None, [keep_c, recv_c, keep_d, recv_d], [(shape, F32), (shape, BF16)], "sum_h")


def sum_n(place, kept, recv, nc):
    n = kept.shape[3]

    def kernel(place_ref, kept_ref, recv_ref, keep_ref, send_c_ref, send_d_ref):
        mine, other = place_ref[2], 1 - place_ref[2]
        c, d = slice(0, nc), slice(nc, n)
        for m in range(LAGS):
            keep_ref[m, :, c] = kept_ref[0, m, :, c] + recv_ref[0, m, :, c].astype(F32)
            send_c_ref[m] = (kept_ref[1, m, :, c] + recv_ref[1, m, :, c].astype(F32)).astype(BF16)
            keep_ref[m, :, d] = kept_ref[mine, m, :, d] + recv_ref[mine, m, :, d].astype(F32)
            send_d_ref[m] = (kept_ref[other, m, :, d] + recv_ref[other, m, :, d].astype(F32)).astype(BF16)

    shapes = [((LAGS, 32, n), F32), ((LAGS, 32, nc), BF16), ((LAGS, 32, n - nc), BF16)]
    return call(kernel, place, [kept, recv], shapes, "sum_n")


def sum_2(place, groups):
    widths = [g[0].shape[3] for g in groups]

    def kernel(place_ref, *refs):
        keep_ref, send_ref = refs[-2:]
        mine, other = place_ref[2], 1 - place_ref[2]
        first = 0
        for k, n in enumerate(widths):
            kept, recv, cols = refs[2 * k], refs[2 * k + 1], slice(first, first + n)
            for m in range(LAGS):
                keep_ref[m, :, cols] = kept[mine, m] + recv[mine, m].astype(F32)
                send_ref[m, :, cols] = (kept[other, m] + recv[other, m].astype(F32)).astype(BF16)
            first += n

    shape = (LAGS, 32, sum(widths))
    return call(kernel, place, [r for g in groups for r in g], [(shape, F32), (shape, BF16)], "sum_2")


def sum_y(keep, recvs, outputs, extra=None):
    arrays = [keep] + list(recvs) + ([] if extra is None else [extra])
    more = 0 if extra is None else extra.shape[2]
    split_at = recvs[0].shape[2]

    def kernel(*refs):
        keep_ref, outs = refs[0], refs[len(arrays) :]
        for m in range(LAGS):
            for k, (out, picks) in enumerate(zip(outs, outputs)):
                to = 0
                if k == 1 and more:
                    out[m, :, :more] = refs[len(arrays) - 1][m]
                    to = more
                for first, n in picks:
                    recv_ref, at = (refs[1], first) if first < split_at else (refs[2], first - split_at)
                    value = keep_ref[m, :, first : first + n] + recv_ref[m, :, at : at + n].astype(F32)
                    out[m, :, to : to + n] = value.astype(BF16)
                    to += n

    shapes = [((LAGS, 32, sum(n for _, n in p) + (more if k == 1 else 0)), BF16) for k, p in enumerate(outputs)]
    return call(kernel, None, arrays, shapes, "sum_y")


def split(place, arrays):
    total = sum(a.shape[2] for a in arrays)

    def kernel(place_ref, *refs):
        at = pl.ds(pl.multiple_of((1 - place_ref[4]) * 16, 16), 16)
        first = 0
        for ref in refs[:-1]:
            n = ref.shape[2]
            for m in range(LAGS):
                refs[-1][m, :, first : first + n] = ref[m, at, :]
            first += n

    return call(kernel, place, arrays, [((LAGS, 16, total), BF16)], "split")[0]


def finish(place, arrays, blocks, recv):
    def kernel(place_ref, *refs):
        ins, recv_ref, out = refs[:-2], refs[-2], refs[-1]
        z, y, c = place_ref[0], place_ref[1], place_ref[4]
        rows = pl.ds(pl.multiple_of(c * 16, 16), 16)

        def cols(block, way):
            dist, dy = block
            zz = lax.rem(z - way * dist + 16, 8)
            yy = y if dy == 0 else 1 - y
            return pl.ds(pl.multiple_of((zz * 2 + yy) * BLOCK, BLOCK), BLOCK)

        for m in range(LAGS):
            for ref, ids in zip(ins, blocks):
                for n, block in enumerate(ids):
                    out[m, :, cols(block, 1 - 2 * c)] = ref[m, rows, n * BLOCK : (n + 1) * BLOCK].astype(F32)
            for n, block in enumerate(sum(blocks, [])):
                out[m, :, cols(block, 2 * c - 1)] += recv_ref[m, :, n * BLOCK : (n + 1) * BLOCK].astype(F32)

    return call(kernel, place, list(arrays) + [recv], [((LAGS, 16, 4096), F32)], "finish")[0]


def chain_step(z, ylo, yhi, x, c):
    return z + sign(c), ylo, yhi, x, c


def y_step(z, ylo, yhi, x, c):
    return z, 1 - ylo, yhi, x, c


def yhi_step(z, ylo, yhi, x, c):
    return z, ylo, 1 - yhi, x, c


def core_step(z, ylo, yhi, x, c):
    return z, ylo, yhi, x, 1 - c


def x_near(z, ylo, yhi, x, c):
    return z, ylo, yhi, x ^ (1 + 2 * c), c


def x_far(z, ylo, yhi, x, c):
    return z, ylo, yhi, x ^ (3 - 2 * c), c


def back(d):
    return lambda z, ylo, yhi, x, c: (z - sign(c) * d, ylo, yhi, x, c)


def after(value, *others):
    return lax.optimization_barrier((value,) + others)[0]


def body(spectra, bin_index):
    scale = 1.0 / math.sqrt(32 * BINS)
    place = jnp.stack([lax.axis_index(a) for a in AXES]).astype(jnp.int32)

    spectra = after(spectra, place)
    own = [whiten(spectra, 0), whiten(spectra, 1)]
    near = [move(b, y_step) for b in own]
    first = [move(b, chain_step) for b in own]
    second = [move(b, chain_step) for b in (first[0], first[1])]

    cosine, sine = phases(bin_index)
    own_plus, own_minus = rotations(own, cosine, sine)
    near_plus, near_minus = rotations(near, cosine, sine)

    def all_pairs(m, ins, at=0):
        b = both(ins[at], ins[at + 1])
        op, om, np_, nm = ins[-4:]
        yield 0, dot_nt(op[m], b)
        yield BLOCK, dot_nt(np_[m], b)
        yield 2 * BLOCK, dot_nt(b, om[m])
        yield 3 * BLOCK, dot_nt(b, nm[m])

    def own_pairs(m, ins):
        op, om = ins[-2:]
        b = both(ins[0], ins[1])
        yield 0, dot_nt(op[m], both(ins[2], ins[3]))
        yield BLOCK, dot_nt(op[m], b)
        yield 2 * BLOCK, dot_nt(b, om[m])

    def near_pairs(m, ins):
        op, np_, nm = ins[-3:]
        b = both(ins[0], ins[1])
        yield 0, dot_nt(op[m], both(ins[2], ins[3]))
        yield BLOCK, dot_nt(np_[m], b)
        yield 2 * BLOCK, dot_nt(b, nm[m])

    def last_pairs(m, ins):
        b = both(ins[0], ins[1])
        yield 0, dot_nt(ins[2][m], b)
        yield BLOCK, dot_nt(ins[3][m], b)

    rotated = [own_plus, own_minus, near_plus, near_minus]
    straight = [(0, 0, 4 * BLOCK)]

    keep_o, send_o = products(place, own_pairs, first + own + rotated[:2], 3 * BLOCK, scale, "pairs_own")
    recv_o = move(send_o, x_near)
    third = [move(after(second[0], near[0], keep_o), chain_step)]
    at = after(place, recv_o)
    near_rotated = [own_plus, near_plus, near_minus]
    keep_n, send_n = products(at, near_pairs, first + near + near_rotated, 3 * BLOCK, scale, "pairs_near")
    recv_n = move(send_n, x_near)
    third.append(move(second[1], chain_step))
    at = after(place, keep_n)
    keep_b, send_b = products(at, all_pairs, second + rotated, 4 * BLOCK, scale, "pairs_2")
    recv_b = move(send_b, x_near)
    fourth = [move(b, chain_step) for b in (after(third[0], keep_b), third[1])]
    at = after(place, keep_b, recv_n)
    keep_c, send_c = products(at, all_pairs, third + rotated, 4 * BLOCK, scale, "pairs_3", "yhi")
    recv_c = move(send_c, yhi_step)
    picks = [(0, 0, 2 * BLOCK), (1, 0, BLOCK), (1, BLOCK, BLOCK), (0, 2 * BLOCK, BLOCK), (1, 2 * BLOCK, BLOCK)]
    keep_o = after(keep_o, keep_c, fourth[0])
    kept_ab, send_ab = sum_1([(keep_o, recv_o), (keep_n, recv_n), (keep_b, recv_b)], picks + [(2, 0, 4 * BLOCK)])
    recv_ab = move(send_ab, x_far)
    at = after(place, kept_ab)
    keep_d, send_d = products(at, last_pairs, fourth + [own_plus, near_plus], 2 * BLOCK, scale, "pairs_4", "far")
    recv_d = move(send_d, x_far)
    kept_cd, send_cd = sum_h(keep_c, recv_c, keep_d, recv_d)
    recv_cd = move(send_cd, x_near)
    keep_ab, send_ab = sum_2(place, [(after(kept_ab, kept_cd), recv_ab)])
    recv_ab = move(send_ab, yhi_step)
    keep_cd, send_c, send_d = sum_n(place, kept_cd, recv_cd, 4 * BLOCK)
    recv_cd = [move(send_c, x_far), move(send_d, yhi_step)]
    outputs = [[(0, 768), (1536, 256)], [(768, 256), (1792, 256)], [(1024, 512)], [(2048, 512)]]
    own_ab, near_ab, ret_1, ret_2 = sum_y(after(keep_ab, keep_cd), [recv_ab], outputs)
    ret_1, ret_2 = move(ret_1, back(1)), move(ret_2, back(2))
    outputs = [[(0, 256), (1024, 256)], [(256, 256), (1280, 256)], [(512, 512)]]
    own_cd, near_all, ret_3 = sum_y(after(keep_cd, own_ab), recv_cd, outputs, near_ab)
    ret_3 = move(ret_3, back(3))
    near_all = move(near_all, y_step)
    arrays = [own_ab, own_cd, near_all, ret_1, ret_2, ret_3]
    blocks = [[(0, 0), (1, 0), (0, 1), (2, 0)], [(3, 0), (4, 0)], [(1, 1), (2, 1), (3, 1), (4, 1)]]
    blocks += [[(-d, 0), (-d, 1)] for d in (1, 2, 3)]
    others = move(split(place, arrays), core_step)
    return finish(place, arrays, blocks, others)


def solution(mesh):
    torus = Mesh(mesh.devices.reshape(SIZES), AXES)
    placed = (P(None, ("yhi", "x", "c"), None, ("z", "ylo")), P())
    return jax.shard_map(
        body, mesh=torus, in_specs=placed, out_specs=P(None, AXES, None), check_vma=False
    )
```

```python
import functools
import math

import jax
import jax.numpy as jnp
import numpy as np
from jax import lax
from jax.experimental import pallas as pl
from jax.experimental.pallas import tpu as pltpu
from jax.sharding import Mesh
from jax.sharding import PartitionSpec as P

NFFT = 8192
LAGS = 2
LAG_STEP = 37
HALF = 64
BINS = 512
BLOCK = 256
DEPTH = 2048
AXES = ("z", "ylo", "yhi", "x", "c")
SIZES = (8, 2, 2, 4, 2)
F32 = jnp.float32
BF16 = jnp.bfloat16
MIB = 1 << 20


def dot_nt(a, b):
    return lax.dot_general(a, b, (((1,), (1,)), ((), ())), preferred_element_type=F32)


def params(mib, **kw):
    return pltpu.CompilerParams(vmem_limit_bytes=mib * MIB, **kw)


def cost(flops, bytes_accessed):
    return pl.CostEstimate(flops=flops, bytes_accessed=bytes_accessed, transcendentals=0)


def move(x, step):
    pairs = []
    for i, at in enumerate(np.ndindex(*SIZES)):
        to = tuple(int(v) % s for v, s in zip(step(*at), SIZES))
        pairs.append((i, int(np.ravel_multi_index(to, SIZES))))
    return lax.ppermute(x, AXES, pairs)


def sign(c):
    return 1 - 2 * c


def whiten_kernel(half, spectra_ref, o_ref, x_ref, sem):
    copy = pltpu.make_async_copy(spectra_ref.at[:, :, :, pl.ds(half * 128, 128)], x_ref, sem)
    copy.start()
    row = lax.broadcasted_iota(jnp.int32, (BINS, BINS), 0)
    col = lax.broadcasted_iota(jnp.int32, (BINS, BINS), 1)
    window = (jnp.abs(row - col) <= HALF).astype(F32).astype(BF16)
    pos = lax.broadcasted_iota(jnp.int32, (1, BINS), 1)
    count = jnp.minimum(pos + HALF, BINS - 1) - jnp.maximum(pos - HALF, 0) + 1
    inverse = 1.0 / count.astype(F32)
    copy.wait()
    for s in range(2):
        re = x_ref[0, s].astype(F32).T
        im = x_ref[1, s].astype(F32).T
        energy = re * re + im * im
        high = energy.astype(BF16)
        low = (energy - high.astype(F32)).astype(BF16)
        total = jnp.dot(high, window, preferred_element_type=F32)
        total += jnp.dot(low, window, preferred_element_type=F32)
        scale = lax.rsqrt(total * inverse + 1e-06)
        o_ref[:, s * BINS : (s + 1) * BINS] = (re * scale).astype(BF16)
        o_ref[:, (2 + s) * BINS : (3 + s) * BINS] = (im * scale).astype(BF16)


def whiten(spectra, half):
    return pl.pallas_call(
        functools.partial(whiten_kernel, half),
        in_specs=[pl.BlockSpec(memory_space=pl.ANY)],
        out_specs=pl.BlockSpec(memory_space=pltpu.VMEM),
        out_shape=jax.ShapeDtypeStruct((128, DEPTH), BF16),
        scratch_shapes=[pltpu.VMEM((2, 2, BINS, 128), BF16), pltpu.SemaphoreType.DMA],
        compiler_params=params(60),
        cost_estimate=cost(2 * 4 * 128 * 512 * 512, MIB),
        name="whiten",
    )(spectra)


def phases(bin_index):
    lag_samples = (jnp.arange(LAGS, dtype=jnp.int32) + 1) * LAG_STEP
    phase_turn = lag_samples[:, None] * bin_index[None, :] % NFFT
    phase_angle = 2.0 * math.pi / NFFT * phase_turn.astype(F32)
    cosine, sine = jnp.cos(phase_angle), jnp.sin(phase_angle)
    return jnp.concatenate([cosine, cosine], 1), jnp.concatenate([sine, sine], 1)


def rotate_kernel(a_ref, b_ref, cos_ref, sin_ref, plus_ref, minus_ref):
    half = DEPTH // 2
    for n, ref in enumerate((a_ref, b_ref)):

        @pl.loop(0, 8)
        def _(i):
            at = pl.ds(pl.multiple_of(i * 16, 16), 16)
            to = pl.ds(pl.multiple_of(n * 128 + i * 16, 16), 16)
            re = ref[at, :half].astype(F32)
            im = ref[at, half:].astype(F32)
            for m in range(LAGS):
                cosine, sine = cos_ref[m : m + 1, :], sin_ref[m : m + 1, :]
                rc, rs, ic, is_ = re * cosine, re * sine, im * cosine, im * sine
                plus_ref[m, to, :half] = (rc - is_).astype(BF16)
                plus_ref[m, to, half:] = (rs + ic).astype(BF16)
                minus_ref[m, to, :half] = (rc + is_).astype(BF16)
                minus_ref[m, to, half:] = (ic - rs).astype(BF16)


def rotations(chunks, cosine, sine):
    shape = jax.ShapeDtypeStruct((LAGS, BLOCK, DEPTH), BF16)
    return pl.pallas_call(
        rotate_kernel,
        out_shape=(shape, shape),
        compiler_params=params(12),
        cost_estimate=cost(2 * 8 * 256 * 2048, 6 * MIB),
        name="rotate",
    )(*chunks, cosine, sine)


def store_product(acc_ref, m, first, value, scale):
    n = value.shape[1]
    for h in range(2):
        for x in range(4):
            at = h * 128 + x * 32
            acc_ref[m, h, x, :, first : first + n] = (value[at : at + 32] * scale).astype(BF16)


def products(at, parts, chunks, wide, scale, name, stage="near"):
    count = len(chunks)

    def kernel(at_ref, *refs):
        ins, (keep_ref, send_ref), acc_ref = refs[:count], refs[count : count + 2], refs[count + 2]
        x, c = at_ref[3], at_ref[4]
        near, far = 1 + 2 * c, 3 - 2 * c
        for m in range(LAGS):
            for first, value in parts(m, ins):
                store_product(acc_ref, m, first, value, scale)
        if stage == "yhi":
            for out, h in ((keep_ref, at_ref[2]), (send_ref, 1 - at_ref[2])):
                for k, which in enumerate((x, x ^ far, x ^ near, x ^ 2)):
                    for m in range(LAGS):
                        out[k, m] = acc_ref[m, h, which]
            return
        if stage == "far":
            near, far = far, near
        slices = ((keep_ref, 0, x), (keep_ref, 1, x ^ far), (send_ref, 0, x ^ near), (send_ref, 1, x ^ 2))
        for out, k, which in slices:
            for m in range(LAGS):
                for h in range(2):
                    out[k, h, m] = acc_ref[m, h, which]

    shape = jax.ShapeDtypeStruct((4, LAGS, 32, wide) if stage == "yhi" else (2, 2, LAGS, 32, wide), BF16)
    whole = pl.BlockSpec(memory_space=pltpu.VMEM)
    return pl.pallas_call(
        kernel,
        in_specs=[pl.BlockSpec(memory_space=pltpu.SMEM)] + [whole] * count,
        out_specs=[whole] * 2,
        out_shape=(shape,) * 2,
        scratch_shapes=[pltpu.VMEM((LAGS, 2, 4, 32, wide), BF16)],
        compiler_params=params(14),
        cost_estimate=cost(2 * 2 * 256 * wide * DEPTH, 8 * MIB),
        name=name,
    )(at, *chunks)


def both(a_ref, b_ref):
    return jnp.concatenate([a_ref[...], b_ref[...]], 0)


def call(kernel, scalars, arrays, shapes, name):
    whole = pl.BlockSpec(memory_space=pltpu.VMEM)
    lead = [] if scalars is None else [scalars]
    return pl.pallas_call(
        kernel,
        in_specs=[pl.BlockSpec(memory_space=pltpu.SMEM)] * len(lead) + [whole] * len(arrays),
        out_specs=[whole] * len(shapes),
        out_shape=tuple(jax.ShapeDtypeStruct(s, t) for s, t in shapes),
        compiler_params=params(12),
        cost_estimate=cost(1000, 10 * MIB),
        name=name,
    )(*lead, *arrays)


def sum_1(groups, picks):
    total = sum(n for _, _, n in picks)

    def kernel(*refs):
        kept_ref, send_ref = refs[-2:]
        for h in range(2):
            for m in range(LAGS):
                to = 0
                for g, first, n in picks:
                    cols, out = slice(first, first + n), slice(to, to + n)
                    keep, recv = refs[2 * g], refs[2 * g + 1]
                    kept_ref[h, m, :, out] = keep[0, h, m, :, cols].astype(F32) + recv[0, h, m, :, cols].astype(F32)
                    value = keep[1, h, m, :, cols].astype(F32) + recv[1, h, m, :, cols].astype(F32)
                    send_ref[h, m, :, out] = value.astype(BF16)
                    to += n

    shape = (2, LAGS, 32, total)
    return call(kernel, None, [r for g in groups for r in g], [(shape, F32), (shape, BF16)], "sum_1")


def sum_h(keep_c, recv_c, keep_d, recv_d):
    nc, nd = keep_c.shape[3], keep_d.shape[4]

    def kernel(c_ref, rc_ref, d_ref, rd_ref, keep_ref, send_ref):
        for k in range(2):
            for m in range(LAGS):
                keep_ref[k, m, :, :nc] = c_ref[k, m].astype(F32) + rc_ref[k, m].astype(F32)
                send_ref[k, m, :, :nc] = (c_ref[2 + k, m].astype(F32) + rc_ref[2 + k, m].astype(F32)).astype(BF16)
                keep_ref[k, m, :, nc:] = d_ref[0, k, m].astype(F32) + rd_ref[0, k, m].astype(F32)
                send_ref[k, m, :, nc:] = (d_ref[1, k, m].astype(F32) + rd_ref[1, k, m].astype(F32)).astype(BF16)

    shape = (2, LAGS, 32, nc + nd)
    return call(kernel, None, [keep_c, recv_c, keep_d, recv_d], [(shape, F32), (shape, BF16)], "sum_h")


def sum_n(place, kept, recv, nc):
    n = kept.shape[3]

    def kernel(place_ref, kept_ref, recv_ref, keep_ref, send_c_ref, send_d_ref):
        mine, other = place_ref[2], 1 - place_ref[2]
        c, d = slice(0, nc), slice(nc, n)
        for m in range(LAGS):
            keep_ref[m, :, c] = kept_ref[0, m, :, c] + recv_ref[0, m, :, c].astype(F32)
            send_c_ref[m] = (kept_ref[1, m, :, c] + recv_ref[1, m, :, c].astype(F32)).astype(BF16)
            keep_ref[m, :, d] = kept_ref[mine, m, :, d] + recv_ref[mine, m, :, d].astype(F32)
            send_d_ref[m] = (kept_ref[other, m, :, d] + recv_ref[other, m, :, d].astype(F32)).astype(BF16)

    shapes = [((LAGS, 32, n), F32), ((LAGS, 32, nc), BF16), ((LAGS, 32, n - nc), BF16)]
    return call(kernel, place, [kept, recv], shapes, "sum_n")


def sum_2(place, groups):
    widths = [g[0].shape[3] for g in groups]

    def kernel(place_ref, *refs):
        keep_ref, send_ref = refs[-2:]
        mine, other = place_ref[2], 1 - place_ref[2]
        first = 0
        for k, n in enumerate(widths):
            kept, recv, cols = refs[2 * k], refs[2 * k + 1], slice(first, first + n)
            for m in range(LAGS):
                keep_ref[m, :, cols] = kept[mine, m] + recv[mine, m].astype(F32)
                send_ref[m, :, cols] = (kept[other, m] + recv[other, m].astype(F32)).astype(BF16)
            first += n

    shape = (LAGS, 32, sum(widths))
    return call(kernel, place, [r for g in groups for r in g], [(shape, F32), (shape, BF16)], "sum_2")


def sum_y(keep, recvs, outputs, extra=None):
    arrays = [keep] + list(recvs) + ([] if extra is None else [extra])
    more = 0 if extra is None else extra.shape[2]
    split_at = recvs[0].shape[2]

    def kernel(*refs):
        keep_ref, outs = refs[0], refs[len(arrays) :]
        for m in range(LAGS):
            for k, (out, picks) in enumerate(zip(outs, outputs)):
                to = 0
                if k == 1 and more:
                    out[m, :, :more] = refs[len(arrays) - 1][m]
                    to = more
                for first, n in picks:
                    recv_ref, at = (refs[1], first) if first < split_at else (refs[2], first - split_at)
                    value = keep_ref[m, :, first : first + n] + recv_ref[m, :, at : at + n].astype(F32)
                    out[m, :, to : to + n] = value.astype(BF16)
                    to += n

    shapes = [((LAGS, 32, sum(n for _, n in p) + (more if k == 1 else 0)), BF16) for k, p in enumerate(outputs)]
    return call(kernel, None, arrays, shapes, "sum_y")


def split(place, arrays):
    total = sum(a.shape[2] for a in arrays)

    def kernel(place_ref, *refs):
        at = pl.ds(pl.multiple_of((1 - place_ref[4]) * 16, 16), 16)
        first = 0
        for ref in refs[:-1]:
            n = ref.shape[2]
            for m in range(LAGS):
                refs[-1][m, :, first : first + n] = ref[m, at, :]
            first += n

    return call(kernel, place, arrays, [((LAGS, 16, total), BF16)], "split")[0]


def finish(place, arrays, blocks, recv):
    def kernel(place_ref, *refs):
        ins, recv_ref, out = refs[:-2], refs[-2], refs[-1]
        z, y, c = place_ref[0], place_ref[1], place_ref[4]
        rows = pl.ds(pl.multiple_of(c * 16, 16), 16)

        def cols(block, way):
            dist, dy = block
            zz = lax.rem(z - way * dist + 16, 8)
            yy = y if dy == 0 else 1 - y
            return pl.ds(pl.multiple_of((zz * 2 + yy) * BLOCK, BLOCK), BLOCK)

        for m in range(LAGS):
            for ref, ids in zip(ins, blocks):
                for n, block in enumerate(ids):
                    out[m, :, cols(block, 1 - 2 * c)] = ref[m, rows, n * BLOCK : (n + 1) * BLOCK].astype(F32)
            for n, block in enumerate(sum(blocks, [])):
                out[m, :, cols(block, 2 * c - 1)] += recv_ref[m, :, n * BLOCK : (n + 1) * BLOCK].astype(F32)

    return call(kernel, place, list(arrays) + [recv], [((LAGS, 16, 4096), F32)], "finish")[0]


def chain_step(z, ylo, yhi, x, c):
    return z + sign(c), ylo, yhi, x, c


def y_step(z, ylo, yhi, x, c):
    return z, 1 - ylo, yhi, x, c


def yhi_step(z, ylo, yhi, x, c):
    return z, ylo, 1 - yhi, x, c


def core_step(z, ylo, yhi, x, c):
    return z, ylo, yhi, x, 1 - c


def x_near(z, ylo, yhi, x, c):
    return z, ylo, yhi, x ^ (1 + 2 * c), c


def x_far(z, ylo, yhi, x, c):
    return z, ylo, yhi, x ^ (3 - 2 * c), c


def back(d):
    return lambda z, ylo, yhi, x, c: (z - sign(c) * d, ylo, yhi, x, c)


def after(value, *others):
    return lax.optimization_barrier((value,) + others)[0]


def body(spectra, bin_index):
    scale = 1.0 / math.sqrt(32 * BINS)
    place = jnp.stack([lax.axis_index(a) for a in AXES]).astype(jnp.int32)

    spectra = after(spectra, place)
    own = [whiten(spectra, 0), whiten(spectra, 1)]
    near = [move(b, y_step) for b in own]
    first = [move(b, chain_step) for b in own]
    second = [move(b, chain_step) for b in (first[0], first[1])]

    cosine, sine = phases(bin_index)
    own_plus, own_minus = rotations(own, cosine, sine)
    near_plus, near_minus = rotations(near, cosine, sine)

    def all_pairs(m, ins, at=0):
        b = both(ins[at], ins[at + 1])
        op, om, np_, nm = ins[-4:]
        yield 0, dot_nt(op[m], b)
        yield BLOCK, dot_nt(np_[m], b)
        yield 2 * BLOCK, dot_nt(b, om[m])
        yield 3 * BLOCK, dot_nt(b, nm[m])

    def own_pairs(m, ins):
        op, om = ins[-2:]
        b = both(ins[0], ins[1])
        yield 0, dot_nt(op[m], both(ins[2], ins[3]))
        yield BLOCK, dot_nt(op[m], b)
        yield 2 * BLOCK, dot_nt(b, om[m])

    def near_pairs(m, ins):
        op, np_, nm = ins[-3:]
        b = both(ins[0], ins[1])
        yield 0, dot_nt(op[m], both(ins[2], ins[3]))
        yield BLOCK, dot_nt(np_[m], b)
        yield 2 * BLOCK, dot_nt(b, nm[m])

    def last_pairs(m, ins):
        b = both(ins[0], ins[1])
        yield 0, dot_nt(ins[2][m], b)
        yield BLOCK, dot_nt(ins[3][m], b)

    rotated = [own_plus, own_minus, near_plus, near_minus]
    straight = [(0, 0, 4 * BLOCK)]

    keep_o, send_o = products(place, own_pairs, first + own + rotated[:2], 3 * BLOCK, scale, "pairs_own")
    recv_o = move(send_o, x_near)
    third = [move(after(second[0], near[0], keep_o), chain_step)]
    at = after(place, recv_o)
    near_rotated = [own_plus, near_plus, near_minus]
    keep_n, send_n = products(at, near_pairs, first + near + near_rotated, 3 * BLOCK, scale, "pairs_near")
    recv_n = move(send_n, x_near)
    third.append(move(second[1], chain_step))
    at = after(place, keep_n)
    keep_b, send_b = products(at, all_pairs, second + rotated, 4 * BLOCK, scale, "pairs_2")
    recv_b = move(send_b, x_near)
    fourth = [move(b, chain_step) for b in (after(third[0], keep_b), third[1])]
    at = after(place, keep_b, recv_n)
    keep_c, send_c = products(at, all_pairs, third + rotated, 4 * BLOCK, scale, "pairs_3", "yhi")
    recv_c = move(send_c, yhi_step)
    picks = [(0, 0, 2 * BLOCK), (1, 0, BLOCK), (1, BLOCK, BLOCK), (0, 2 * BLOCK, BLOCK), (1, 2 * BLOCK, BLOCK)]
    keep_o = after(keep_o, keep_c, fourth[0])
    kept_ab, send_ab = sum_1([(keep_o, recv_o), (keep_n, recv_n), (keep_b, recv_b)], picks + [(2, 0, 4 * BLOCK)])
    recv_ab = move(send_ab, x_far)
    at = after(place, kept_ab)
    keep_d, send_d = products(at, last_pairs, fourth + [own_plus, near_plus], 2 * BLOCK, scale, "pairs_4", "far")
    recv_d = move(send_d, x_far)
    kept_cd, send_cd = sum_h(keep_c, recv_c, keep_d, recv_d)
    recv_cd = move(send_cd, x_near)
    keep_ab, send_ab = sum_2(place, [(after(kept_ab, kept_cd), recv_ab)])
    recv_ab = move(send_ab, yhi_step)
    keep_cd, send_c, send_d = sum_n(place, kept_cd, recv_cd, 4 * BLOCK)
    recv_cd = [move(send_c, x_far), move(send_d, yhi_step)]
    outputs = [[(0, 768), (1536, 256)], [(768, 256), (1792, 256)], [(1024, 512)], [(2048, 512)]]
    own_ab, near_ab, ret_1, ret_2 = sum_y(after(keep_ab, keep_cd), [recv_ab], outputs)
    ret_1, ret_2 = move(ret_1, back(1)), move(ret_2, back(2))
    outputs = [[(0, 256), (1024, 256)], [(256, 256), (1280, 256)], [(512, 512)]]
    own_cd, near_all, ret_3 = sum_y(after(keep_cd, own_ab), recv_cd, outputs, near_ab)
    ret_3 = move(ret_3, back(3))
    near_all = move(near_all, y_step)
    arrays = [own_ab, own_cd, near_all, ret_1, ret_2, ret_3]
    blocks = [[(0, 0), (1, 0), (0, 1), (2, 0)], [(3, 0), (4, 0)], [(1, 1), (2, 1), (3, 1), (4, 1)]]
    blocks += [[(-d, 0), (-d, 1)] for d in (1, 2, 3)]
    others = move(split(place, arrays), core_step)
    return finish(place, arrays, blocks, others)


def solution(mesh):
    torus = Mesh(mesh.devices.reshape(SIZES), AXES)
    placed = (P(None, ("yhi", "x", "c"), None, ("z", "ylo")), P())
    return jax.shard_map(
        body, mesh=torus, in_specs=placed, out_specs=P(None, AXES, None), check_vma=False
    )
```

```python
import math

import jax
import jax.numpy as jnp
import numpy as np
from jax import lax
from jax.experimental import pallas as pl
from jax.experimental.pallas import tpu as pltpu
from jax.sharding import Mesh
from jax.sharding import PartitionSpec as P

NFFT = 8192
LAGS = 2
LAG_STEP = 37
HALF = 64
BINS = 512
BLOCK = 256
DEPTH = 2048
AXES = ("z", "ylo", "yhi", "x", "c")
SIZES = (8, 2, 2, 4, 2)
F32 = jnp.float32
BF16 = jnp.bfloat16
MIB = 1 << 20


def dot_nt(a, b):
    return lax.dot_general(a, b, (((1,), (1,)), ((), ())), preferred_element_type=F32)


def params(mib, **kw):
    return pltpu.CompilerParams(vmem_limit_bytes=mib * MIB, **kw)


def cost(flops, bytes_accessed):
    return pl.CostEstimate(flops=flops, bytes_accessed=bytes_accessed, transcendentals=0)


def move(x, step):
    pairs = []
    for i, at in enumerate(np.ndindex(*SIZES)):
        to = tuple(int(v) % s for v, s in zip(step(*at), SIZES))
        pairs.append((i, int(np.ravel_multi_index(to, SIZES))))
    return lax.ppermute(x, AXES, pairs)


def sign(c):
    return 1 - 2 * c


def whiten_kernel(x_ref, o_ref):
    row = lax.broadcasted_iota(jnp.int32, (BINS, BINS), 0)
    col = lax.broadcasted_iota(jnp.int32, (BINS, BINS), 1)
    window = (jnp.abs(row - col) <= HALF).astype(F32).astype(BF16)
    pos = lax.broadcasted_iota(jnp.int32, (1, BINS), 1)
    count = jnp.minimum(pos + HALF, BINS - 1) - jnp.maximum(pos - HALF, 0) + 1
    inverse = 1.0 / count.astype(F32)
    for s in range(2):
        re = x_ref[0, s].astype(F32).T
        im = x_ref[1, s].astype(F32).T
        energy = re * re + im * im
        high = energy.astype(BF16)
        low = (energy - high.astype(F32)).astype(BF16)
        total = jnp.dot(high, window, preferred_element_type=F32)
        total += jnp.dot(low, window, preferred_element_type=F32)
        scale = lax.rsqrt(total * inverse + 1e-06)
        o_ref[:, s * BINS : (s + 1) * BINS] = (re * scale).astype(BF16)
        o_ref[:, (2 + s) * BINS : (3 + s) * BINS] = (im * scale).astype(BF16)


def whiten(spectra, half):
    return pl.pallas_call(
        whiten_kernel,
        grid=(1,),
        in_specs=[pl.BlockSpec((2, 2, BINS, 128), lambda i: (0, 0, 0, half))],
        out_specs=pl.BlockSpec((128, DEPTH), lambda i: (0, 0)),
        out_shape=jax.ShapeDtypeStruct((128, DEPTH), BF16),
        compiler_params=params(12),
        cost_estimate=cost(2 * 4 * 128 * 512 * 512, MIB),
        name="whiten",
    )(spectra)


def phases(bin_index):
    lag_samples = (jnp.arange(LAGS, dtype=jnp.int32) + 1) * LAG_STEP
    phase_turn = lag_samples[:, None] * bin_index[None, :] % NFFT
    phase_angle = 2.0 * math.pi / NFFT * phase_turn.astype(F32)
    cosine, sine = jnp.cos(phase_angle), jnp.sin(phase_angle)
    return jnp.concatenate([cosine, cosine], 1), jnp.concatenate([sine, sine], 1)


def rotate_kernel(a_ref, b_ref, cos_ref, sin_ref, plus_ref, minus_ref):
    half = DEPTH // 2
    for n, ref in enumerate((a_ref, b_ref)):

        @pl.loop(0, 8)
        def _(i):
            at = pl.ds(pl.multiple_of(i * 16, 16), 16)
            to = pl.ds(pl.multiple_of(n * 128 + i * 16, 16), 16)
            re = ref[at, :half].astype(F32)
            im = ref[at, half:].astype(F32)
            for m in range(LAGS):
                cosine, sine = cos_ref[m : m + 1, :], sin_ref[m : m + 1, :]
                rc, rs, ic, is_ = re * cosine, re * sine, im * cosine, im * sine
                plus_ref[m, to, :half] = (rc - is_).astype(BF16)
                plus_ref[m, to, half:] = (rs + ic).astype(BF16)
                minus_ref[m, to, :half] = (rc + is_).astype(BF16)
                minus_ref[m, to, half:] = (ic - rs).astype(BF16)


def rotations(chunks, cosine, sine):
    shape = jax.ShapeDtypeStruct((LAGS, BLOCK, DEPTH), BF16)
    return pl.pallas_call(
        rotate_kernel,
        out_shape=(shape, shape),
        compiler_params=params(12),
        cost_estimate=cost(2 * 8 * 256 * 2048, 6 * MIB),
        name="rotate",
    )(*chunks, cosine, sine)


def store_product(acc_ref, m, first, value, scale):
    n = value.shape[1]
    for h in range(2):
        for x in range(4):
            at = h * 128 + x * 32
            acc_ref[m, h, x, :, first : first + n] = (value[at : at + 32] * scale).astype(BF16)


def products(at, parts, chunks, wide, scale, name, stage="near"):
    count = len(chunks)

    def kernel(at_ref, *refs):
        ins, (keep_ref, send_ref), acc_ref = refs[:count], refs[count : count + 2], refs[count + 2]
        x, c = at_ref[3], at_ref[4]
        near, far = 1 + 2 * c, 3 - 2 * c
        for m in range(LAGS):
            for first, value in parts(m, ins):
                store_product(acc_ref, m, first, value, scale)
        if stage == "yhi":
            for out, h in ((keep_ref, at_ref[2]), (send_ref, 1 - at_ref[2])):
                for k, which in enumerate((x, x ^ far, x ^ near, x ^ 2)):
                    for m in range(LAGS):
                        out[k, m] = acc_ref[m, h, which]
            return
        if stage == "far":
            near, far = far, near
        slices = ((keep_ref, 0, x), (keep_ref, 1, x ^ far), (send_ref, 0, x ^ near), (send_ref, 1, x ^ 2))
        for out, k, which in slices:
            for m in range(LAGS):
                for h in range(2):
                    out[k, h, m] = acc_ref[m, h, which]

    shape = jax.ShapeDtypeStruct((4, LAGS, 32, wide) if stage == "yhi" else (2, 2, LAGS, 32, wide), BF16)
    whole = pl.BlockSpec(memory_space=pltpu.VMEM)
    return pl.pallas_call(
        kernel,
        in_specs=[pl.BlockSpec(memory_space=pltpu.SMEM)] + [whole] * count,
        out_specs=[whole] * 2,
        out_shape=(shape,) * 2,
        scratch_shapes=[pltpu.VMEM((LAGS, 2, 4, 32, wide), BF16)],
        compiler_params=params(14),
        cost_estimate=cost(2 * 2 * 256 * wide * DEPTH, 8 * MIB),
        name=name,
    )(at, *chunks)


def both(a_ref, b_ref):
    return jnp.concatenate([a_ref[...], b_ref[...]], 0)


def call(kernel, scalars, arrays, shapes, name):
    whole = pl.BlockSpec(memory_space=pltpu.VMEM)
    lead = [] if scalars is None else [scalars]
    return pl.pallas_call(
        kernel,
        in_specs=[pl.BlockSpec(memory_space=pltpu.SMEM)] * len(lead) + [whole] * len(arrays),
        out_specs=[whole] * len(shapes),
        out_shape=tuple(jax.ShapeDtypeStruct(s, t) for s, t in shapes),
        compiler_params=params(12),
        cost_estimate=cost(1000, 10 * MIB),
        name=name,
    )(*lead, *arrays)


def sum_1(groups, picks):
    total = sum(n for _, _, n in picks)

    def kernel(*refs):
        kept_ref, send_ref = refs[-2:]
        for h in range(2):
            for m in range(LAGS):
                to = 0
                for g, first, n in picks:
                    cols, out = slice(first, first + n), slice(to, to + n)
                    keep, recv = refs[2 * g], refs[2 * g + 1]
                    kept_ref[h, m, :, out] = keep[0, h, m, :, cols].astype(F32) + recv[0, h, m, :, cols].astype(F32)
                    value = keep[1, h, m, :, cols].astype(F32) + recv[1, h, m, :, cols].astype(F32)
                    send_ref[h, m, :, out] = value.astype(BF16)
                    to += n

    shape = (2, LAGS, 32, total)
    return call(kernel, None, [r for g in groups for r in g], [(shape, F32), (shape, BF16)], "sum_1")


def sum_h(keep_c, recv_c, keep_d, recv_d):
    nc, nd = keep_c.shape[3], keep_d.shape[4]

    def kernel(c_ref, rc_ref, d_ref, rd_ref, keep_ref, send_ref):
        for k in range(2):
            for m in range(LAGS):
                keep_ref[k, m, :, :nc] = c_ref[k, m].astype(F32) + rc_ref[k, m].astype(F32)
                send_ref[k, m, :, :nc] = (c_ref[2 + k, m].astype(F32) + rc_ref[2 + k, m].astype(F32)).astype(BF16)
                keep_ref[k, m, :, nc:] = d_ref[0, k, m].astype(F32) + rd_ref[0, k, m].astype(F32)
                send_ref[k, m, :, nc:] = (d_ref[1, k, m].astype(F32) + rd_ref[1, k, m].astype(F32)).astype(BF16)

    shape = (2, LAGS, 32, nc + nd)
    return call(kernel, None, [keep_c, recv_c, keep_d, recv_d], [(shape, F32), (shape, BF16)], "sum_h")


def sum_n(place, kept, recv, nc):
    n = kept.shape[3]

    def kernel(place_ref, kept_ref, recv_ref, keep_ref, send_c_ref, send_d_ref):
        mine, other = place_ref[2], 1 - place_ref[2]
        c, d = slice(0, nc), slice(nc, n)
        for m in range(LAGS):
            keep_ref[m, :, c] = kept_ref[0, m, :, c] + recv_ref[0, m, :, c].astype(F32)
            send_c_ref[m] = (kept_ref[1, m, :, c] + recv_ref[1, m, :, c].astype(F32)).astype(BF16)
            keep_ref[m, :, d] = kept_ref[mine, m, :, d] + recv_ref[mine, m, :, d].astype(F32)
            send_d_ref[m] = (kept_ref[other, m, :, d] + recv_ref[other, m, :, d].astype(F32)).astype(BF16)

    shapes = [((LAGS, 32, n), F32), ((LAGS, 32, nc), BF16), ((LAGS, 32, n - nc), BF16)]
    return call(kernel, place, [kept, recv], shapes, "sum_n")


def sum_2(place, groups):
    widths = [g[0].shape[3] for g in groups]

    def kernel(place_ref, *refs):
        keep_ref, send_ref = refs[-2:]
        mine, other = place_ref[2], 1 - place_ref[2]
        first = 0
        for k, n in enumerate(widths):
            kept, recv, cols = refs[2 * k], refs[2 * k + 1], slice(first, first + n)
            for m in range(LAGS):
                keep_ref[m, :, cols] = kept[mine, m] + recv[mine, m].astype(F32)
                send_ref[m, :, cols] = (kept[other, m] + recv[other, m].astype(F32)).astype(BF16)
            first += n

    shape = (LAGS, 32, sum(widths))
    return call(kernel, place, [r for g in groups for r in g], [(shape, F32), (shape, BF16)], "sum_2")


def sum_y(keep, recvs, outputs, extra=None):
    arrays = [keep] + list(recvs) + ([] if extra is None else [extra])
    more = 0 if extra is None else extra.shape[2]
    split_at = recvs[0].shape[2]

    def kernel(*refs):
        keep_ref, outs = refs[0], refs[len(arrays) :]
        for m in range(LAGS):
            for k, (out, picks) in enumerate(zip(outs, outputs)):
                to = 0
                if k == 1 and more:
                    out[m, :, :more] = refs[len(arrays) - 1][m]
                    to = more
                for first, n in picks:
                    recv_ref, at = (refs[1], first) if first < split_at else (refs[2], first - split_at)
                    value = keep_ref[m, :, first : first + n] + recv_ref[m, :, at : at + n].astype(F32)
                    out[m, :, to : to + n] = value.astype(BF16)
                    to += n

    shapes = [((LAGS, 32, sum(n for _, n in p) + (more if k == 1 else 0)), BF16) for k, p in enumerate(outputs)]
    return call(kernel, None, arrays, shapes, "sum_y")


def split(place, arrays):
    total = sum(a.shape[2] for a in arrays)

    def kernel(place_ref, *refs):
        at = pl.ds(pl.multiple_of((1 - place_ref[4]) * 16, 16), 16)
        first = 0
        for ref in refs[:-1]:
            n = ref.shape[2]
            for m in range(LAGS):
                refs[-1][m, :, first : first + n] = ref[m, at, :]
            first += n

    return call(kernel, place, arrays, [((LAGS, 16, total), BF16)], "split")[0]


def finish(place, arrays, blocks, recv):
    def kernel(place_ref, *refs):
        ins, recv_ref, out = refs[:-2], refs[-2], refs[-1]
        z, y, c = place_ref[0], place_ref[1], place_ref[4]
        rows = pl.ds(pl.multiple_of(c * 16, 16), 16)

        def cols(block, way):
            dist, dy = block
            zz = lax.rem(z - way * dist + 16, 8)
            yy = y if dy == 0 else 1 - y
            return pl.ds(pl.multiple_of((zz * 2 + yy) * BLOCK, BLOCK), BLOCK)

        for m in range(LAGS):
            for ref, ids in zip(ins, blocks):
                for n, block in enumerate(ids):
                    out[m, :, cols(block, 1 - 2 * c)] = ref[m, rows, n * BLOCK : (n + 1) * BLOCK].astype(F32)
            for n, block in enumerate(sum(blocks, [])):
                out[m, :, cols(block, 2 * c - 1)] += recv_ref[m, :, n * BLOCK : (n + 1) * BLOCK].astype(F32)

    return call(kernel, place, list(arrays) + [recv], [((LAGS, 16, 4096), F32)], "finish")[0]


def chain_step(z, ylo, yhi, x, c):
    return z + sign(c), ylo, yhi, x, c


def y_step(z, ylo, yhi, x, c):
    return z, 1 - ylo, yhi, x, c


def yhi_step(z, ylo, yhi, x, c):
    return z, ylo, 1 - yhi, x, c


def core_step(z, ylo, yhi, x, c):
    return z, ylo, yhi, x, 1 - c


def x_near(z, ylo, yhi, x, c):
    return z, ylo, yhi, x ^ (1 + 2 * c), c


def x_far(z, ylo, yhi, x, c):
    return z, ylo, yhi, x ^ (3 - 2 * c), c


def back(d):
    return lambda z, ylo, yhi, x, c: (z - sign(c) * d, ylo, yhi, x, c)


def after(value, *others):
    return lax.optimization_barrier((value,) + others)[0]


def body(spectra, bin_index):
    scale = 1.0 / math.sqrt(32 * BINS)
    place = jnp.stack([lax.axis_index(a) for a in AXES]).astype(jnp.int32)

    spectra = after(spectra, place)
    own = [whiten(spectra, 0), whiten(spectra, 1)]
    near = [move(b, y_step) for b in own]
    first = [move(b, chain_step) for b in own]
    second = [move(b, chain_step) for b in (first[0], first[1])]

    cosine, sine = phases(bin_index)
    own_plus, own_minus = rotations(own, cosine, sine)
    near_plus, near_minus = rotations(near, cosine, sine)

    def all_pairs(m, ins, at=0):
        b = both(ins[at], ins[at + 1])
        op, om, np_, nm = ins[-4:]
        yield 0, dot_nt(op[m], b)
        yield BLOCK, dot_nt(np_[m], b)
        yield 2 * BLOCK, dot_nt(b, om[m])
        yield 3 * BLOCK, dot_nt(b, nm[m])

    def own_pairs(m, ins):
        op, om = ins[-2:]
        b = both(ins[0], ins[1])
        yield 0, dot_nt(op[m], both(ins[2], ins[3]))
        yield BLOCK, dot_nt(op[m], b)
        yield 2 * BLOCK, dot_nt(b, om[m])

    def near_pairs(m, ins):
        op, np_, nm = ins[-3:]
        b = both(ins[0], ins[1])
        yield 0, dot_nt(op[m], both(ins[2], ins[3]))
        yield BLOCK, dot_nt(np_[m], b)
        yield 2 * BLOCK, dot_nt(b, nm[m])

    def last_pairs(m, ins):
        b = both(ins[0], ins[1])
        yield 0, dot_nt(ins[2][m], b)
        yield BLOCK, dot_nt(ins[3][m], b)

    rotated = [own_plus, own_minus, near_plus, near_minus]
    straight = [(0, 0, 4 * BLOCK)]

    keep_o, send_o = products(place, own_pairs, first + own + rotated[:2], 3 * BLOCK, scale, "pairs_own")
    recv_o = move(send_o, x_near)
    third = [move(after(second[0], near[0], keep_o), chain_step)]
    at = after(place, recv_o)
    near_rotated = [own_plus, near_plus, near_minus]
    keep_n, send_n = products(at, near_pairs, first + near + near_rotated, 3 * BLOCK, scale, "pairs_near")
    recv_n = move(send_n, x_near)
    third.append(move(second[1], chain_step))
    at = after(place, keep_n)
    keep_b, send_b = products(at, all_pairs, second + rotated, 4 * BLOCK, scale, "pairs_2")
    recv_b = move(send_b, x_near)
    fourth = [move(b, chain_step) for b in (after(third[0], keep_b), third[1])]
    at = after(place, keep_b, recv_n)
    keep_c, send_c = products(at, all_pairs, third + rotated, 4 * BLOCK, scale, "pairs_3", "yhi")
    recv_c = move(send_c, yhi_step)
    picks = [(0, 0, 2 * BLOCK), (1, 0, BLOCK), (1, BLOCK, BLOCK), (0, 2 * BLOCK, BLOCK), (1, 2 * BLOCK, BLOCK)]
    keep_o = after(keep_o, keep_c, fourth[0])
    kept_ab, send_ab = sum_1([(keep_o, recv_o), (keep_n, recv_n), (keep_b, recv_b)], picks + [(2, 0, 4 * BLOCK)])
    recv_ab = move(send_ab, x_far)
    at = after(place, kept_ab)
    keep_d, send_d = products(at, last_pairs, fourth + [own_plus, near_plus], 2 * BLOCK, scale, "pairs_4", "far")
    recv_d = move(send_d, x_far)
    keep_ab, send_ab = sum_2(place, [(after(kept_ab, keep_d), recv_ab)])
    recv_ab = move(send_ab, yhi_step)
    kept_cd, send_cd = sum_h(after(keep_c, keep_ab), recv_c, keep_d, recv_d)
    recv_cd = move(send_cd, x_near)
    keep_cd, send_c, send_d = sum_n(place, kept_cd, recv_cd, 4 * BLOCK)
    recv_cd = [move(send_c, x_far), move(send_d, yhi_step)]
    outputs = [[(0, 768), (1536, 256)], [(768, 256), (1792, 256)], [(1024, 512)], [(2048, 512)]]
    own_ab, near_ab, ret_1, ret_2 = sum_y(after(keep_ab, keep_cd), [recv_ab], outputs)
    ret_1, ret_2 = move(ret_1, back(1)), move(ret_2, back(2))
    outputs = [[(0, 256), (1024, 256)], [(256, 256), (1280, 256)], [(512, 512)]]
    own_cd, near_all, ret_3 = sum_y(after(keep_cd, own_ab), recv_cd, outputs, near_ab)
    ret_3 = move(ret_3, back(3))
    near_all = move(near_all, y_step)
    arrays = [own_ab, own_cd, near_all, ret_1, ret_2, ret_3]
    blocks = [[(0, 0), (1, 0), (0, 1), (2, 0)], [(3, 0), (4, 0)], [(1, 1), (2, 1), (3, 1), (4, 1)]]
    blocks += [[(-d, 0), (-d, 1)] for d in (1, 2, 3)]
    others = move(split(place, arrays), core_step)
    return finish(place, arrays, blocks, others)


def solution(mesh):
    torus = Mesh(mesh.devices.reshape(SIZES), AXES)
    placed = (P(None, ("yhi", "x", "c"), None, ("z", "ylo")), P())
    return jax.shard_map(
        body, mesh=torus, in_specs=placed, out_specs=P(None, AXES, None), check_vma=False
    )
```
